128 devices in a mesh: section: 4 (over z_hi, core), rep: 32 (over x, z_lo, y).
Axes of the slice: x: 4, y: 4, z: 4 (z_hi: 2, z_lo: 2; z = z_hi * 2 + z_lo), core: 2. Of those that a mesh axis runs over, the one named last changes fastest.
Arguments:
- micro_inputs: bfloat16 [2, 4096, 6144], P(None, 'rep'), may hold values from -6 to 6
- output_grads: bfloat16 [2, 4096, 6144], P(None, 'rep'), may hold values from -0.09375 to 0.09375
- stash: bfloat16 [4, 2, 2, 4096, 6144], P('section', None, None, 'rep'), may hold values from -6 to 6, as said below
- sample_ids: int32 [2, 32], P(None, 'rep'), may hold values from 0 to 1
- fwd_exps: int32 [4, 2, 4096, 48], P(None, None, 'rep'), may hold values from -1 to 2
- bwd_exps: int32 [4, 2, 4096, 48], P(None, None, 'rep'), may hold values from -13 to -10
- adapter_in: bfloat16 [4, 1, 6144, 128], P('section'), may hold values from -0.078125 to 0.078125
- adapter_out: bfloat16 [4, 1, 128, 6144], P('section'), may hold values from -0.5 to 0.5
Outputs:
- grad_in: bfloat16 [4, 1, 6144, 128], P('section')
- grad_out: bfloat16 [4, 1, 128, 6144], P('section')
The draws below stay inside these ranges and needn't reach their ends.
Inputs may be any that keep to these rules, and one draw needn't show every extreme that they name: stash[s, 1] equals stash[s + 1, 0]: the stored output of a section is the stored input of the next.
All inputs are finite; a program needn't handle non-finite values.
Results may differ from the reference program's by a relative error of at most 0.014.
Values may be sent and summed in bfloat16 or wider, within the bound.
No kernel may reach another device: no remote copies, remote signals or barrier semaphores. Data moves between devices by JAX's collectives and lax.ppermute only.
A program may use at most 128 MiB of HBM per device.

```python
import jax
import jax.numpy as jnp
from jax import lax

D = 6144
R = 128
LAYERS = 1
MB = 2
SAMPLES = 2
TOK_DEV = 128
SECTIONS = 4
REPLICAS = 32
TOKENS = 4096
BLOCKS = 48


def draw_stash(key, part):
    key = jax.random.fold_in(key, 11)
    full_shape = (SECTIONS + 1, SAMPLES, TOKENS, D)
    stored = jnp.clip(jax.random.normal(key, full_shape, jnp.float32), -6.0, 6.0)
    return jnp.stack([stored[:-1], stored[1:]], axis=1).astype(jnp.bfloat16)


def place_ends(drawn, stream_key, least, largest):
    extent = drawn.shape
    spot = [jax.random.randint(jax.random.fold_in(stream_key, axis), (), 0, extent[axis]) for axis in range(len(extent))]
    drawn = drawn.at[tuple(spot)].set(least)
    longest = extent.index(max(extent))
    spot[longest] = (spot[longest] + 1) % extent[longest]
    return drawn.at[tuple(spot)].set(largest)


def levels(key, extent, cuts, least, high):
    def one(dim, shards_of):
        heights = jax.random.uniform(jax.random.fold_in(jax.random.fold_in(key, 6), dim), (shards_of,), jnp.float32, least / len(cuts), high / len(cuts))
        return jnp.repeat(jnp.exp(heights), extent[dim] // shards_of).reshape((-1,) + (1,) * (len(extent) - dim - 1))

    factor_of = one(*cuts[0])
    for cut in cuts[1:]:
        factor_of = factor_of * one(*cut)
    return factor_of


def scatter_about(own_key, shape, deviation, most, pieces=(), dtype=jnp.bfloat16):
    array = deviation * jax.random.normal(own_key, shape, jnp.float32)
    if pieces:
        array = array * levels(own_key, shape, pieces, -0.22, 0.18)
    return jnp.clip(array, -most, most).astype(dtype)


def setup_inputs(seed: int = 0) -> dict:
    seeds = jax.random.split(jax.random.key(seed), 9)
    micro_inputs = scatter_about(seeds[0], (MB, TOKENS, D), 1.0, 6.0, ((1, 32),))
    output_grads = scatter_about(seeds[1], (MB, TOKENS, D), TOKENS ** -0.5, 0.09375, ((1, 32),))
    stash = draw_stash(jax.random.fold_in(seeds[8], 71), 0)
    sample_ids = place_ends(jax.random.randint(seeds[3], (MB, REPLICAS), 0, SAMPLES), jax.random.fold_in(seeds[3], 1), 0, SAMPLES - 1).astype(jnp.int32)
    fwd_exps = place_ends(jax.random.randint(seeds[4], (SECTIONS, MB, TOKENS, BLOCKS), -1, 3), jax.random.fold_in(seeds[4], 1), -1, 2).astype(jnp.int32)
    bwd_exps = place_ends(jax.random.randint(seeds[5], (SECTIONS, MB, TOKENS, BLOCKS), -13, -9), jax.random.fold_in(seeds[5], 1), -13, (-9) - 1).astype(jnp.int32)
    adapter_in = scatter_about(seeds[6], (SECTIONS, LAYERS, D, R), D ** -0.5, 0.078125, ((0, 4),))
    adapter_out = scatter_about(seeds[7], (SECTIONS, LAYERS, R, D), R ** -0.5, 0.5, ((0, 4),))
    return dict(micro_inputs=micro_inputs, output_grads=output_grads, stash=stash, sample_ids=sample_ids, fwd_exps=fwd_exps, bwd_exps=bwd_exps, adapter_in=adapter_in, adapter_out=adapter_out)


EPS = 1e-05

def scaled(values, exponents):
    factor = jnp.exp2(exponents.astype(jnp.float32))
    token_count = values.shape[0]
    blocks = factor.shape[1]
    shaped = values.reshape(token_count, blocks, values.shape[1] // blocks)
    return (shaped * factor[:, :, None]).reshape(values.shape)

def normalize(hidden):
    average = lax.optimization_barrier(jnp.mean(hidden, axis=-1, keepdims=True))
    centred = hidden - average
    variance = lax.optimization_barrier(jnp.mean(centred * centred, axis=-1, keepdims=True))
    inverse_std = lax.rsqrt(variance + EPS)
    return (centred * inverse_std, inverse_std)

def layer_forward(hidden, weight_in, weight_out):
    unit_rows, inverse_std = normalize(hidden)
    normed = unit_rows.astype(jnp.bfloat16)
    latent = jnp.dot(normed, weight_in, preferred_element_type=jnp.float32).astype(jnp.bfloat16)
    result = hidden + jnp.dot(latent, weight_out, preferred_element_type=jnp.float32)
    return (result, (unit_rows, inverse_std, normed, latent))

def layer_backward(gradient, stored_cache, weight_in, weight_out):
    unit_rows, inverse_std, normed, latent = stored_cache
    grad_low = gradient.astype(jnp.bfloat16)
    grad_wout = lax.dot_general(latent, grad_low, (((0,), (0,)), ((), ())), preferred_element_type=jnp.float32)
    grad_latent = lax.dot_general(grad_low, weight_out, (((1,), (1,)), ((), ())), preferred_element_type=jnp.float32).astype(jnp.bfloat16)
    grad_win = lax.dot_general(normed, grad_latent, (((0,), (0,)), ((), ())), preferred_element_type=jnp.float32)
    grad_norm = lax.dot_general(grad_latent, weight_in, (((1,), (1,)), ((), ())), preferred_element_type=jnp.float32)
    centred = grad_norm - lax.optimization_barrier(jnp.mean(grad_norm, axis=-1, keepdims=True)) - unit_rows * lax.optimization_barrier(jnp.mean(grad_norm * unit_rows, axis=-1, keepdims=True))
    return (gradient + inverse_std * centred, grad_win, grad_wout)

def pick_sample(stored, sample_ids, micro):
    blocks = stored.reshape(SAMPLES, REPLICAS, TOK_DEV, D)
    chosen = blocks[sample_ids[micro], jnp.arange(REPLICAS)]
    return chosen.reshape(TOKENS, D).astype(jnp.float32)

def reference(micro_inputs, output_grads, stash, sample_ids, fwd_exps, bwd_exps, adapter_in, adapter_out):
    sums_in = [[jnp.zeros((D, R), jnp.float32) for layer_index in range(LAYERS)] for section_index in range(SECTIONS)]
    sums_out = [[jnp.zeros((R, D), jnp.float32) for layer_index in range(LAYERS)] for section_index in range(SECTIONS)]
    for micro in range(MB):
        hidden = micro_inputs[micro].astype(jnp.float32)
        inputs = []
        for section_index in range(SECTIONS):
            inputs.append(hidden)
            for layer_index in range(LAYERS):
                hidden = layer_forward(hidden, adapter_in[section_index, layer_index], adapter_out[section_index, layer_index])[0]
            if section_index < SECTIONS - 1:
                exponent = fwd_exps[section_index, micro]
                difference = hidden - pick_sample(stash[section_index, 1], sample_ids, micro)
                delta = jnp.clip(scaled(difference, -exponent), -8.0, 7.0).astype(jnp.bfloat16)
                hidden = pick_sample(stash[section_index + 1, 0], sample_ids, micro) + scaled(delta.astype(jnp.float32), exponent)
        gradient = output_grads[micro].astype(jnp.float32)
        for section_index in reversed(range(SECTIONS)):
            hidden = inputs[section_index]
            caches = []
            for layer_index in range(LAYERS):
                hidden, stored_cache = layer_forward(hidden, adapter_in[section_index, layer_index], adapter_out[section_index, layer_index])
                caches.append(stored_cache)
            for layer_index in reversed(range(LAYERS)):
                gradient, grad_win, grad_wout = layer_backward(gradient, caches[layer_index], adapter_in[section_index, layer_index], adapter_out[section_index, layer_index])
                sums_in[section_index][layer_index] = sums_in[section_index][layer_index] + grad_win
                sums_out[section_index][layer_index] = sums_out[section_index][layer_index] + grad_wout
            if section_index > 0:
                exponent = bwd_exps[section_index, micro]
                grad_codes = jnp.clip(scaled(gradient, -exponent), -128.0, 127.0).astype(jnp.bfloat16)
                gradient = scaled(grad_codes.astype(jnp.float32), exponent)
    grad_in = jnp.stack([jnp.stack(row) for row in sums_in]).astype(jnp.bfloat16)
    grad_out = jnp.stack([jnp.stack(row) for row in sums_out]).astype(jnp.bfloat16)
    return (grad_in, grad_out)
```

```python
import functools

import jax
import jax.numpy as jnp
from jax import lax
from jax.experimental import pallas as pl
from jax.experimental.pallas import tpu as pltpu
from jax.sharding import PartitionSpec as P

EPS = 1e-05
BF = jnp.bfloat16
F32 = jnp.float32
ROWS = 16
LANES = 128
VMEM_LIMIT = 40 * 1024 * 1024
ANY = pl.BlockSpec(memory_space=pl.ANY)
VMEM = pl.BlockSpec(memory_space=pltpu.VMEM)
SMEM = pl.BlockSpec(memory_space=pltpu.SMEM)


def dot_nn(a, b):
    return lax.dot_general(a, b, (((1,), (0,)), ((), ())), preferred_element_type=F32)


def dot_nt(a, b):
    return lax.dot_general(a, b, (((1,), (1,)), ((), ())), preferred_element_type=F32)


def dot_tn(a, b):
    return lax.dot_general(a, b, (((0,), (0,)), ((), ())), preferred_element_type=F32)


def call(body, outs, scratch, ins, flops=10**8, nbytes=4 * 10**6):
    return pl.pallas_call(
        body,
        out_shape=[jax.ShapeDtypeStruct(s, d) for s, d, _ in outs],
        in_specs=[spec for _, spec in ins],
        out_specs=[spec for _, _, spec in outs],
        scratch_shapes=scratch,
        compiler_params=pltpu.CompilerParams(vmem_limit_bytes=VMEM_LIMIT),
        cost_estimate=pl.CostEstimate(flops=flops, bytes_accessed=nbytes, transcendentals=0),
    )(*[a for a, _ in ins])


def lane_iota(rows):
    return lax.broadcasted_iota(jnp.int32, (rows, LANES), 1)


def row_iota(rows):
    return lax.broadcasted_iota(jnp.int32, (rows, LANES), 0)


def three(x):
    hi = x.astype(BF).astype(F32)
    rest = x - hi
    mid = rest.astype(BF).astype(F32)
    return hi, mid, (rest - mid).astype(BF).astype(F32)


def pack_rows(first_half, second_half, extra):
    at = row_iota(16)
    out = jnp.zeros((16, LANES), F32)
    for base, (a, b) in ((0, first_half), (8, second_half)):
        for j, row in enumerate(three(a) + three(b)):
            out = jnp.where(at == base + j, row, out)
    if extra is not None:
        hi, mid, _ = three(extra)
        out = jnp.where(at == 6, hi, out)
        out = jnp.where(at == 7, mid, out)
    return out.astype(BF)


def unpack_rows(block):
    block = block.astype(F32)

    def joined(base):
        return block[base : base + 1] + block[base + 1 : base + 2] + block[base + 2 : base + 3]

    return (joined(0), joined(8)), (joined(3), joined(11)), block[6:7] + block[7:8]


def columns(rows):
    at = row_iota(LANES)
    out = jnp.zeros((LANES, LANES), F32)
    for j, row in enumerate(rows):
        out = jnp.where(at == j, row, out)
    return out.T


def join_latent(msgs, tokens, width):
    parsed = [unpack_rows(m[tokens : tokens + 16]) for m in msgs]
    total = msgs[0][:tokens].astype(F32)
    for m in msgs[1:]:
        total = total + m[:tokens].astype(F32)
    halves = []
    for half in range(2):
        means = [p[0][half] for p in parsed]
        mean = (means[0] + means[1] + means[2] + means[3]) * 0.25
        offs = [m - mean for m in means]
        var = (parsed[0][1][half] + parsed[1][1][half] + parsed[2][1][half] + parsed[3][1][half]) * 0.25
        var = var + (offs[0] * offs[0] + offs[1] * offs[1] + offs[2] * offs[2] + offs[3] * offs[3]) * 0.25
        halves.append(columns([mean, lax.rsqrt(var + EPS)] + offs))
    cols = jnp.concatenate(halves, axis=0)
    colsum = parsed[0][2]
    for d in range(4):
        total = total + cols[:, 2 + d : 3 + d] * parsed[d][2]
        if d:
            colsum = colsum + parsed[d][2]
    return total * cols[:, 1:2], cols[:, 0:1], cols[:, 1:2], colsum


def start_first(pairs, sem):
    for cond, src, dst in pairs:
        @pl.when(cond)
        def _(src=src, dst=dst):
            pltpu.make_async_copy(src, dst, sem).start()


def start_weight(section, q, own, near, same, cross, dst, sem):
    zh, c = q // 2, q % 2
    here = zh == section // 2
    mine = c == section % 2
    start_first(
        [
            (here & mine, own, dst),
            (here & jnp.logical_not(mine), near, dst),
            (jnp.logical_not(here) & mine, same, dst),
            (jnp.logical_not(here) & jnp.logical_not(mine), cross, dst),
        ],
        sem,
    )


def wait_for(dst, sem):
    pltpu.make_async_copy(dst, dst, sem).wait()


def send_body(sc, stash, w_in, w_out, far, mid, in_a, in_b, in_c, out_a, out_b, out_c, sems):
    q = sc[0]
    c = q % 2
    tok, quarter = far.shape[0] // 2, far.shape[1]
    mid_slot = jnp.where(q == 1, 1, 0)
    copies = []

    def go(src, dst):
        copy = pltpu.make_async_copy(src, dst, sems.at[len(copies)])
        copy.start()
        copies.append(copy)

    def cols(k):
        return pl.ds(pl.multiple_of((q ^ k) * quarter, quarter), quarter)

    for k, dst in ((2, out_a), (3, out_b), (1, out_c)):
        go(w_out.at[0, 0, :, cols(k)], dst)
    for k, dst in ((2, in_a), (3, in_b), (1, in_c)):
        go(w_in.at[0, 0, cols(k), :], dst)
    for m in range(2):
        go(stash.at[0, 1 - c, sc[1 + m], :, cols(2)], far.at[pl.ds(m * tok, tok)])
    for m in range(2):
        go(stash.at[0, mid_slot, sc[1 + m], :, cols(1)], mid.at[pl.ds(m * tok, tok)])
    for copy in copies:
        copy.wait()


def first_body(sc, micro, grads, w_in, w_out, msg, x_v, w_v, wo_v, n_v, st, sems):
    q = sc[0]
    tokens, width = x_v.shape
    tok = tokens // 2
    msg[...] = jnp.zeros(msg.shape, BF)

    def load(src, wsrc, wdst):
        copies = [pltpu.make_async_copy(src.at[m], x_v.at[pl.ds(m * tok, tok)], sems.at[m]) for m in range(2)]
        copies.append(pltpu.make_async_copy(wsrc.at[0, 0], wdst, sems.at[2]))
        for copy in copies:
            copy.start()
        for copy in copies:
            copy.wait()

    @pl.when(q == 0)
    def _():
        load(micro, w_in, w_v)

        @pl.loop(0, tokens // ROWS)
        def _(i):
            rows = pl.ds(pl.multiple_of(i * ROWS, ROWS), ROWS)

            def block(b):
                return x_v[rows, b * LANES : (b + 1) * LANES].astype(F32)

            acc = block(0)
            for b in range(1, width // LANES):
                acc = acc + block(b)
            mean = jnp.sum(acc, axis=1, keepdims=True) * (1.0 / width)
            acc = jnp.zeros((ROWS, LANES), F32)
            for b in range(width // LANES):
                d = block(b) - mean
                acc = acc + d * d
            inv = lax.rsqrt(jnp.sum(acc, axis=1, keepdims=True) * (1.0 / width) + EPS)
            for b in range(width // LANES):
                n_v[rows, b * LANES : (b + 1) * LANES] = ((block(b) - mean) * inv).astype(BF)
            st[rows, :] = jnp.where(lane_iota(ROWS) == 0, mean, inv)

        latent = dot_nn(n_v[...], w_v[...])
        msg[:tokens] = latent.astype(BF)
        t0, t1 = st[:LANES].T, st[LANES:].T
        msg[tokens:] = pack_rows((t0[0:1], t0[1:2]), (t1[0:1], t1[1:2]), None)

    @pl.when(q == 3)
    def _():
        load(grads, w_out, wo_v)
        msg[:tokens] = dot_nt(x_v[...], wo_v[...]).astype(BF)


def forward_body(section, sc, *refs):
    first = section == 1
    refs = list(refs)
    take = refs.pop
    msgs = [take(0) for _ in range(4)]
    h_in = take(0)
    factor = take(0)
    stash, held = take(0), take(0)
    wo_own, wo_near, wo_same, wo_cross = [take(0) for _ in range(4)]
    wi_own, wi_near, wi_same, wi_cross = [take(0) for _ in range(4)]
    h_out, normed, msg, latf, invb, colsum_out = [take(0) for _ in range(6)]
    x_v, pick, up, cen, wo_v, wi_v, st, mc = [take(0) for _ in range(8)]
    lat_v, sems = take(0), take(0)
    q = sc[0]
    c = q % 2
    tokens, quarter = pick.shape
    tok = tokens // 2
    cols = pl.ds(pl.multiple_of(q * quarter, quarter), quarter)
    start_weight(section - 1, q, wo_own.at[0, 0, :, cols], wo_near, wo_same, wo_cross, wo_v, sems.at[0])
    if first:
        for m in range(2):
            pltpu.make_async_copy(h_in.at[m, :, cols], x_v.at[pl.ds(m * tok, tok)], sems.at[2]).start()
    if section == 2:
        local, slot = (q == 1) | (q == 2), jnp.where(q == 1, 1, 0)
    else:
        local, slot = (q // 2 == 0) if section == 1 else (q // 2 == 1), 1 - c
    for m in range(2):
        rows = pl.ds(m * tok, tok)
        start_first(
            [
                (local, stash.at[0, slot, sc[1 + m], :, cols], pick.at[rows]),
                (jnp.logical_not(local), held.at[rows], pick.at[rows]),
            ],
            sems.at[3],
        )
    start_weight(section, q, wi_own.at[0, 0, cols, :], wi_near, wi_same, wi_cross, wi_v, sems.at[1])

    if first:
        for k in range(4):
            @pl.when(q == k)
            def _(k=k):
                lat_v[...] = msgs[k][...]

        (m0, m1), (v0, v1), _ = unpack_rows(lat_v[tokens:])
        both = jnp.concatenate([columns([m0, v0]), columns([m1, v1])], axis=0)
        latent = lat_v[:tokens].astype(F32)
        mean, inv = both[:, 0:1], both[:, 1:2]
        colsum_out[...] = jnp.zeros(colsum_out.shape, F32)
    else:
        latent, mean, inv, colsum = join_latent([m[...] for m in msgs], tokens, quarter)
        colsum_out[...] = jnp.broadcast_to(colsum, colsum_out.shape)
    latf[...] = latent
    invb[...] = jnp.broadcast_to(inv, invb.shape)
    mc[...] = jnp.broadcast_to(mean, mc.shape)
    wait_for(wo_v, sems.at[0])
    up[...] = dot_nn(latent.astype(BF), wo_v[...])
    if first:
        wait_for(x_v, sems.at[2])
        src = x_v
    else:
        src = h_in
    wait_for(pick, sems.at[3])

    @pl.loop(0, tokens // ROWS)
    def _(i):
        rows = pl.ds(pl.multiple_of(i * ROWS, ROWS), ROWS)
        mean_t, inv_t = mc[rows, :], invb[rows, :]
        fac = factor[rows, :]
        acc = jnp.zeros((ROWS, LANES), F32)
        kept = []
        for b in range(quarter // LANES):
            lanes = slice(b * LANES, (b + 1) * LANES)
            h = src[rows, lanes].astype(F32)
            normed[rows, lanes] = ((h - mean_t) * inv_t).astype(BF)
            stored = pick[rows, lanes].astype(F32)
            f = fac[:, b : b + 1]
            d = jnp.clip(h + up[rows, lanes] - stored, f * -8.0, f * 7.0).astype(BF)
            h = stored + d.astype(F32)
            h_out[rows, lanes] = h
            acc = acc + h
            kept.append(h)
        mean_d = jnp.sum(acc, axis=1, keepdims=True) * (1.0 / quarter)
        acc = jnp.zeros((ROWS, LANES), F32)
        for b in range(quarter // LANES):
            d = kept[b] - mean_d
            cen[rows, b * LANES : (b + 1) * LANES] = d.astype(BF)
            acc = acc + d * d
        var_d = jnp.sum(acc, axis=1, keepdims=True) * (1.0 / quarter)
        st[rows, :] = jnp.where(lane_iota(ROWS) == 0, mean_d, var_d)

    wait_for(wi_v, sems.at[1])
    w = wi_v[...]
    msg[:tokens] = dot_nn(cen[...], w).astype(BF)
    colsum = dot_nn(jnp.ones((16, quarter), BF), w)[0:1]
    t0, t1 = st[:LANES].T, st[LANES:].T
    msg[tokens:] = pack_rows((t0[0:1], t0[1:2]), (t1[0:1], t1[1:2]), colsum)


def backward_body(section, sc, *refs):
    top = section == 3
    refs = list(refs)
    take = refs.pop
    msgs = [take(0) for _ in range(4)]
    if top:
        lat_msgs = [take(0) for _ in range(4)]
        h_in = take(0)
    else:
        normed_in, latf, invb, colsum_in = [take(0) for _ in range(4)]
    g_in = take(0)
    factor = take(0)
    wo_own, wo_near, wo_same, wo_cross = [take(0) for _ in range(4)]
    wi_own, wi_near, wi_same, wi_cross = [take(0) for _ in range(4)]
    g_out, msg, glat_out = [take(0) for _ in range(3)]
    if top:
        normed, latf, g_v = [take(0) for _ in range(3)]
    gn, wo_v, wi_v, mc, inv_v, a_v, b_v, sems = [take(0) for _ in range(8)]
    q = sc[0]
    tokens, quarter = gn.shape
    tok = tokens // 2
    width = 4 * quarter
    cols = pl.ds(pl.multiple_of(q * quarter, quarter), quarter)
    start_weight(section, q, wi_own.at[0, 0, cols, :], wi_near, wi_same, wi_cross, wi_v, sems.at[0])
    start_weight(section - 1, q, wo_own.at[0, 0, :, cols], wo_near, wo_same, wo_cross, wo_v, sems.at[1])
    if top:
        for m in range(2):
            pltpu.make_async_copy(g_in.at[m, :, cols], g_v.at[pl.ds(m * tok, tok)], sems.at[2]).start()
        latent, mean, inv, colsum = join_latent([m[...] for m in lat_msgs], tokens, quarter)
        latf[...] = latent
        mc[...] = jnp.broadcast_to(mean, mc.shape)
        inv_v[...] = jnp.broadcast_to(inv, inv_v.shape)
        for k in range(4):
            @pl.when(q ^ 3 == k)
            def _(k=k):
                glat_out[...] = msgs[k][:tokens]

        glat = glat_out[...]
        src, norm, inv_ref = g_v, normed, inv_v
    else:
        latent, colsum = latf[...], colsum_in[0:1]
        glat = msgs[0][:tokens].astype(F32)
        for m in msgs[1:]:
            glat = glat + m[:tokens].astype(F32)
        glat = glat.astype(BF)
        glat_out[...] = glat
        src, norm, inv_ref = g_in, normed_in, invb
    wide = glat.astype(F32)
    a_v[...] = jnp.broadcast_to(jnp.sum(wide * colsum, axis=1, keepdims=True) * (1.0 / width), a_v.shape)
    b_v[...] = jnp.broadcast_to(jnp.sum(wide * latent, axis=1, keepdims=True) * (1.0 / width), b_v.shape)
    wait_for(wi_v, sems.at[0])
    gn[...] = dot_nt(glat, wi_v[...])
    if top:
        wait_for(g_v, sems.at[2])

    @pl.loop(0, tokens // ROWS)
    def _(i):
        rows = pl.ds(pl.multiple_of(i * ROWS, ROWS), ROWS)
        fac = factor[rows, :]
        inv_t, a_t, b_t = inv_ref[rows, :], a_v[rows, :], b_v[rows, :]
        for b in range(quarter // LANES):
            lanes = slice(b * LANES, (b + 1) * LANES)
            if top:
                n = (h_in[rows, lanes] - mc[rows, :]) * inv_t
                normed[rows, lanes] = n.astype(BF)
            else:
                n = norm[rows, lanes].astype(F32)
            f = fac[:, b : b + 1]
            g = src[rows, lanes].astype(F32) + inv_t * (gn[rows, lanes] - a_t - n * b_t)
            g_out[rows, lanes] = jnp.clip(g, f * -128.0, f * 127.0).astype(BF)

    wait_for(wo_v, sems.at[1])
    msg[...] = dot_nt(g_out[...], wo_v[...]).astype(BF)


def grads_body(normed, latf, g_ref, glat, gin, gout):
    gin[...] = dot_tn(normed[...], glat[...]).astype(BF)
    gout[...] = dot_tn(latf[...].astype(BF), g_ref[...]).astype(BF)


def grads_top_body(sc, normed, latf, g_ref, glat, gin, gout, g_v, sems):
    quarter = g_v.shape[1]
    tok = g_v.shape[0] // 2
    cols = pl.ds(pl.multiple_of(sc[0] * quarter, quarter), quarter)
    for m in range(2):
        pltpu.make_async_copy(g_ref.at[m, :, cols], g_v.at[pl.ds(m * tok, tok)], sems.at[0]).start()
    gin[...] = dot_tn(normed[...], glat[...]).astype(BF)
    wait_for(g_v, sems.at[0])
    gout[...] = dot_tn(latf[...].astype(BF), g_v[...]).astype(BF)


def grads_first_body(m0, m1, m2, m3, normed, latf, g_ref, gin, gout):
    glat = m0[...].astype(F32) + m1[...].astype(F32) + m2[...].astype(F32) + m3[...].astype(F32)
    gin[...] = dot_tn(normed[...], glat.astype(BF)).astype(BF)
    gout[...] = dot_tn(latf[...].astype(BF), g_ref[...]).astype(BF)


def rep_of(x, z, y):
    return x * 8 + z * 4 + y


EVERY = [(x, z, y) for x in range(4) for z in range(2) for y in range(4)]


def along_x(value, k):
    return lax.ppermute(value, "rep", [(rep_of(x, z, y), rep_of((x + k) % 4, z, y)) for x, z, y in EVERY])


def along_y(value, k):
    return lax.ppermute(value, "rep", [(rep_of(x, z, y), rep_of(x, z, (y + k) % 4)) for x, z, y in EVERY])


def along_z(value, k):
    return lax.ppermute(value, "rep", [(rep_of(x, z, y), rep_of(x, (z + k) % 2, y)) for x, z, y in EVERY])


def scatter_sum(value, count, move, me, dim):
    size = value.shape[dim] // count
    parts = [lax.dynamic_slice_in_dim(value, me * size, size, dim)]
    for k in range(1, count):
        parts.append(move(lax.dynamic_slice_in_dim(value, ((me + k) % count) * size, size, dim), k))
    total = parts[0].astype(F32)
    for part in parts[1:]:
        total = total + part.astype(F32)
    return total.astype(BF)


def reduce_section(gin, gout, place):
    x, z, y = place
    a = scatter_sum(gin, 4, along_x, x, 0)
    b = scatter_sum(gout, 4, along_y, y, 0)
    a = scatter_sum(a, 4, along_y, y, 0)
    b = scatter_sum(b, 4, along_x, x, 1)
    half = a.shape[0] // 2
    low = b.shape[0] // 2
    strips = [b[:, j * LANES : (j + 1) * LANES] for j in range(b.shape[1] // LANES)]
    both = jnp.concatenate(
        [jnp.concatenate([a[i * half : (i + 1) * half]] + [s[i * low : (i + 1) * low] for s in strips], 0) for i in range(2)], 0
    )
    return scatter_sum(both, 2, along_z, z, 0)


def gather(value, count, move):
    return [value] + [move(value, k) for k in range(1, count)]


def place_body(sc, a0, a1, a2, a3, b0, b1, b2, b3, gin, gout):
    q, x, z, y = sc[0], sc[3], sc[4], sc[5]
    quarter = gin.shape[2] // 4
    for i in range(4):
        a_ref, b_ref = (a0, a1, a2, a3)[i], (b0, b1, b2, b3)[i]
        for j in range(4):
            for k in range(2):
                for d in range(4):
                    xs, ys, zs, qs = (x - i + 4) % 4, (y - j + 4) % 4, (z + k) % 2, q ^ d
                    row = qs * quarter + xs * (quarter // 4) + ys * (quarter // 16) + zs * (quarter // 32)
                    gin[0, 0, pl.ds(pl.multiple_of(row, 16), quarter // 32), :] = a_ref[j, k, d]
                    xs, ys = (x - j + 4) % 4, (y - i + 4) % 4
                    row = pl.multiple_of(ys * 32 + zs * 16, 16)
                    for s in range(3):
                        col = pl.multiple_of(qs * quarter + xs * 384 + s * LANES, LANES)
                        gout[0, 0, pl.ds(row, 16), pl.ds(col, LANES)] = b_ref[j, k, d, s * 16 : (s + 1) * 16, :]


def on_device(micro, grads, stash, sample_ids, fwd_exps, bwd_exps, w_in, w_out):
    q = lax.axis_index("section")
    rep = lax.axis_index("rep")
    x, z, y = rep // 8, (rep // 4) % 2, rep % 4
    tok, width = micro.shape[1], micro.shape[2]
    tokens, quarter, rank = 2 * tok, width // 4, w_in.shape[3]
    blocks = quarter // LANES
    sc = jnp.stack([q, sample_ids[0, 0], sample_ids[1, 0], x, z, y]).astype(jnp.int32)

    def factors(exps):
        own = lax.dynamic_slice_in_dim(exps, q * blocks, blocks, 3).reshape(exps.shape[0], tokens, blocks)
        return lax.shift_left(jnp.ones(own.shape, jnp.int32), own + 14).astype(F32) * (2.0**-14)

    fwd_f, bwd_f = factors(fwd_exps), factors(bwd_exps)

    def swap(value, k, sources=range(4)):
        return lax.ppermute(value, "section", [(s, s ^ k) for s in sources])

    def exchange(value):
        return [value] + [swap(value, k) for k in (1, 2, 3)]

    def beside(value, cross, sections):
        pairs = []
        for s in sections:
            for xx, zz, yy in EVERY:
                pairs.append((s * 32 + rep_of(xx, zz, yy), (s ^ 2 ^ cross) * 32 + rep_of(xx, 1 - zz, yy)))
        return lax.ppermute(value, ("section", "rep"), pairs)

    dma = pltpu.SemaphoreType.DMA
    big = (tokens, quarter)
    qi, qo = (quarter, rank), (rank, quarter)
    (msg0,) = call(
        first_body,
        [((tokens + 16, rank), BF, VMEM)],
        [
            pltpu.VMEM((tokens, width), BF),
            pltpu.VMEM((width, rank), BF),
            pltpu.VMEM((rank, width), BF),
            pltpu.VMEM((tokens, width), BF),
            pltpu.VMEM((tokens, LANES), F32),
            dma((3,)),
        ],
        [(sc, SMEM), (micro, ANY), (grads, ANY), (w_in, ANY), (w_out, ANY)],
    )
    far, mid, in_a, in_b, in_c, out_a, out_b, out_c = call(
        send_body,
        [(big, BF, ANY)] * 2 + [(qi, BF, ANY)] * 3 + [(qo, BF, ANY)] * 3,
        [dma((10,))],
        [(sc, SMEM), (stash, ANY), (w_in, ANY), (w_out, ANY)],
    )
    msgs0 = [msg0] + [swap(msg0, k, (0, 3)) for k in (1, 2, 3)]
    wo = [w_out, swap(out_c, 1), beside(out_a, 0, (0, 1, 2)), beside(out_b, 1, (0, 1, 2))]
    wi = [w_in, swap(in_c, 1), beside(in_a, 0, (1, 2, 3)), beside(in_b, 1, (1, 2, 3))]
    far = swap(far, 2)
    mid = swap(mid, 1, (1, 2))

    msgs = msgs0
    h = micro
    kept = []
    for section in (1, 2, 3):
        h, normed, msg, latf, invb, colsum = call(
            functools.partial(forward_body, section),
            [
                (big, F32, VMEM),
                (big, BF, VMEM),
                ((tokens + 16, rank), BF, VMEM),
                ((tokens, rank), F32, VMEM),
                ((tokens, LANES), F32, VMEM),
                ((8, LANES), F32, VMEM),
            ],
            [
                pltpu.VMEM(big, BF),
                pltpu.VMEM(big, BF),
                pltpu.VMEM(big, F32),
                pltpu.VMEM(big, BF),
                pltpu.VMEM(qo, BF),
                pltpu.VMEM(qi, BF),
                pltpu.VMEM((tokens, LANES), F32),
                pltpu.VMEM((tokens, LANES), F32),
                pltpu.VMEM((tokens + 16, rank), BF),
                dma((4,)),
            ],
            [(sc, SMEM)]
            + [(m, VMEM) for m in msgs]
            + [(h, ANY if section == 1 else VMEM), (fwd_f[section - 1], VMEM), (stash, ANY)]
            + [(mid if section == 2 else far, ANY)]
            + [(w, ANY) for w in wo + wi],
        )
        kept.append((normed, latf, invb, colsum))
        msgs = exchange(msg)

    place = (x, z, y)
    sums = [None] * 4
    g = grads
    for section in (3, 2, 1):
        top = section == 3
        outs = [(big, BF, VMEM), ((tokens, rank), BF, VMEM), ((tokens, rank), BF, VMEM)]
        scratch = [
            pltpu.VMEM(big, F32),
            pltpu.VMEM(qo, BF),
            pltpu.VMEM(qi, BF),
            pltpu.VMEM((tokens, LANES), F32),
            pltpu.VMEM((tokens, LANES), F32),
            pltpu.VMEM((tokens, LANES), F32),
            pltpu.VMEM((tokens, LANES), F32),
            dma((3,)),
        ]
        if top:
            outs += [(big, BF, VMEM), ((tokens, rank), F32, VMEM)]
            scratch = [pltpu.VMEM(big, BF)] + scratch
            ins = [(m, VMEM) for m in msgs0] + [(m, VMEM) for m in msgs] + [(h, VMEM), (g, ANY)]
        else:
            ins = [(m, VMEM) for m in msgs] + [(v, VMEM) for v in kept[section]] + [(g, VMEM)]
        result = call(
            functools.partial(backward_body, section),
            outs,
            scratch,
            [(sc, SMEM)] + ins + [(bwd_f[section], VMEM)] + [(w, ANY) for w in wo + wi],
        )
        next_g, msg, glat = result[:3]
        if top:
            normed, latf = result[3:]
            gin, gout = call(
                grads_top_body,
                [(qi, BF, VMEM), (qo, BF, VMEM)],
                [pltpu.VMEM(big, BF), dma((1,))],
                [(sc, SMEM), (normed, VMEM), (latf, VMEM), (g, ANY), (glat, VMEM)],
            )
        else:
            normed, latf = kept[section][:2]
            gin, gout = call(
                grads_body,
                [(qi, BF, VMEM), (qo, BF, VMEM)],
                [],
                [(normed, VMEM), (latf, VMEM), (g, VMEM), (glat, VMEM)],
            )
        msgs = exchange(msg)
        sums[section] = reduce_section(gin, gout, place)
        g = next_g
    gin, gout = call(
        grads_first_body,
        [(qi, BF, VMEM), (qo, BF, VMEM)],
        [],
        [(m, VMEM) for m in msgs] + [(kept[0][0], VMEM), (kept[0][1], VMEM), (g, VMEM)],
    )
    sums[0] = reduce_section(gin, gout, place)

    shares = jnp.stack(sums)
    own = [lax.dynamic_index_in_dim(shares, q ^ k, 0, keepdims=False) for k in range(4)]
    mine = jnp.stack([own[0]] + [swap(own[k], k) for k in (1, 2, 3)])
    pair = jnp.stack(gather(mine, 2, along_z))
    a, b = pair[:, :, : quarter // 32], pair[:, :, quarter // 32 :]
    a = gather(jnp.stack(gather(a, 4, along_y)), 4, along_x)
    b = gather(jnp.stack(gather(b, 4, along_x)), 4, along_y)
    total_in, total_out = call(
        place_body,
        [((1, 1, width, rank), BF, VMEM), ((1, 1, rank, width), BF, VMEM)],
        [],
        [(sc, SMEM)] + [(v, VMEM) for v in a + b],
    )
    return total_in, total_out


def solution(mesh):
    placed = (
        P(None, "rep", None),
        P(None, "rep", None),
        P("section", None, None, "rep", None),
        P(None, "rep"),
        P(None, None, "rep", None),
        P(None, None, "rep", None),
        P("section", None, None, None),
        P("section", None, None, None),
    )
    return jax.shard_map(
        on_device,
        mesh=mesh,
        in_specs=placed,
        out_specs=(P("section", None, None, None), P("section", None, None, None)),
        check_vma=False,
    )
```

```python
import functools

import jax
import jax.numpy as jnp
from jax import lax
from jax.experimental import pallas as pl
from jax.experimental.pallas import tpu as pltpu
from jax.sharding import PartitionSpec as P

EPS = 1e-05
BF = jnp.bfloat16
F32 = jnp.float32
ROWS = 16
LANES = 128
MIB = 1024 * 1024
ANY = pl.BlockSpec(memory_space=pl.ANY)
HBM = pl.BlockSpec(memory_space=pltpu.HBM)
VMEM = pl.BlockSpec(memory_space=pltpu.VMEM)
SMEM = pl.BlockSpec(memory_space=pltpu.SMEM)


def dot_nn(a, b):
    return lax.dot_general(a, b, (((1,), (0,)), ((), ())), preferred_element_type=F32)


def dot_nt(a, b):
    return lax.dot_general(a, b, (((1,), (1,)), ((), ())), preferred_element_type=F32)


def dot_tn(a, b):
    return lax.dot_general(a, b, (((0,), (0,)), ((), ())), preferred_element_type=F32)


def call(body, outs, scratch, ins, flops=10**8, nbytes=4 * 10**6, vmem=12):
    return pl.pallas_call(
        body,
        out_shape=[jax.ShapeDtypeStruct(s, d) for s, d, _ in outs],
        in_specs=[spec for _, spec in ins],
        out_specs=[spec for _, _, spec in outs],
        scratch_shapes=scratch,
        compiler_params=pltpu.CompilerParams(vmem_limit_bytes=vmem * MIB),
        cost_estimate=pl.CostEstimate(flops=flops, bytes_accessed=nbytes, transcendentals=0),
    )(*[pltpu.with_memory_space_constraint(a, pltpu.HBM) if spec is HBM else a for a, spec in ins])


def lane_iota(rows):
    return lax.broadcasted_iota(jnp.int32, (rows, LANES), 1)


def row_iota(rows):
    return lax.broadcasted_iota(jnp.int32, (rows, LANES), 0)


def three(x):
    hi = x.astype(BF).astype(F32)
    rest = x - hi
    mid = rest.astype(BF).astype(F32)
    return hi, mid, (rest - mid).astype(BF).astype(F32)


def pack_rows(first_half, second_half, extra):
    at = row_iota(16)
    out = jnp.zeros((16, LANES), F32)
    for base, (a, b) in ((0, first_half), (8, second_half)):
        for j, row in enumerate(three(a) + three(b)):
            out = jnp.where(at == base + j, row, out)
    if extra is not None:
        hi, mid, _ = three(extra)
        out = jnp.where(at == 6, hi, out)
        out = jnp.where(at == 7, mid, out)
    return out.astype(BF)


def unpack_rows(block):
    block = block.astype(F32)

    def joined(base):
        return block[base : base + 1] + block[base + 1 : base + 2] + block[base + 2 : base + 3]

    return (joined(0), joined(8)), (joined(3), joined(11)), block[6:7] + block[7:8]


def columns(rows):
    at = row_iota(LANES)
    out = jnp.zeros((LANES, LANES), F32)
    for j, row in enumerate(rows):
        out = jnp.where(at == j, row, out)
    return out.T


def join_latent(msgs, tokens, width):
    parsed = [unpack_rows(m[tokens : tokens + 16]) for m in msgs]
    total = msgs[0][:tokens].astype(F32)
    for m in msgs[1:]:
        total = total + m[:tokens].astype(F32)
    halves = []
    for half in range(2):
        means = [p[0][half] for p in parsed]
        mean = (means[0] + means[1] + means[2] + means[3]) * 0.25
        offs = [m - mean for m in means]
        var = (parsed[0][1][half] + parsed[1][1][half] + parsed[2][1][half] + parsed[3][1][half]) * 0.25
        var = var + (offs[0] * offs[0] + offs[1] * offs[1] + offs[2] * offs[2] + offs[3] * offs[3]) * 0.25
        halves.append(columns([mean, lax.rsqrt(var + EPS)] + offs))
    cols = jnp.concatenate(halves, axis=0)
    colsum = parsed[0][2]
    for d in range(4):
        total = total + cols[:, 2 + d : 3 + d] * parsed[d][2]
        if d:
            colsum = colsum + parsed[d][2]
    return total * cols[:, 1:2], cols[:, 0:1], cols[:, 1:2], colsum


def start_first(pairs, sem):
    for cond, src, dst in pairs:
        @pl.when(cond)
        def _(src=src, dst=dst):
            pltpu.make_async_copy(src, dst, sem).start()


def start_weight(section, sc, own, near, same, cross, inner, dst, sem):
    q, x, y = sc[0], sc[3], sc[5]
    zh, c = q // 2, q % 2
    here = zh == section // 2
    mine = c == section % 2
    piece = 384

    def start(src, to):
        pltpu.make_async_copy(src, to, sem).start()

    @pl.when(here & mine)
    def _():
        start(own, dst)

    @pl.when(here & jnp.logical_not(mine))
    def _():
        start(near, dst)

    def pieces(refs, me):
        for k in range(4):
            at = ((me - k + 4) % 4) * piece
            if inner:
                start(refs[k].at[pl.ds(0, piece)], dst.at[pl.ds(pl.multiple_of(at, piece), piece)])
            else:
                for t in range(piece // LANES):
                    cols = pl.ds(pl.multiple_of(at + t * LANES, LANES), LANES)
                    start(refs[k].at[pl.ds(piece + t * LANES, LANES)], dst.at[:, cols])

    @pl.when(jnp.logical_not(here) & mine)
    def _():
        pieces(same, x)

    @pl.when(jnp.logical_not(here) & jnp.logical_not(mine))
    def _():
        pieces(cross, y)


def factors(exps, q, out):
    every = exps.shape[0] // 2
    blocks = every // 4
    for k in range(4):
        @pl.when(q == k)
        def _(k=k):
            for m in range(2):
                e = exps[m * every + k * blocks : m * every + (k + 1) * blocks, :]
                f = lax.shift_left(jnp.ones(e.shape, jnp.int32), e + 14).astype(F32) * (2.0**-14)
                full = jnp.concatenate([f, jnp.zeros((LANES - blocks, LANES), F32)], axis=0)
                out[m * LANES : (m + 1) * LANES, :] = full.T


def wait_for(dst, sem):
    pltpu.make_async_copy(dst, dst, sem).wait()


def send_body(sc, stash, w_in, w_out, far, mid, sib_in, sib_out, same, cross, sems):
    q, x, y = sc[0], sc[3], sc[5]
    c = q % 2
    tok, quarter = far.shape[0] // 2, far.shape[1]
    piece = quarter // 4
    mid_slot = jnp.where(q == 1, 1, 0)
    copies = []

    def go(src, dst):
        copy = pltpu.make_async_copy(src, dst, sems.at[len(copies)])
        copy.start()
        copies.append(copy)

    def cols(k):
        return pl.ds(pl.multiple_of((q ^ k) * quarter, quarter), quarter)

    for k, at, dst in ((2, x, same), (3, y, cross)):
        base = (q ^ k) * quarter + at * piece
        go(w_in.at[0, 0, pl.ds(pl.multiple_of(base, piece), piece), :], dst.at[pl.ds(0, piece)])
        for t in range(piece // LANES):
            from_cols = pl.ds(pl.multiple_of(base + t * LANES, LANES), LANES)
            go(w_out.at[0, 0, :, from_cols], dst.at[pl.ds(piece + t * LANES, LANES)])
    for m in range(2):
        go(stash.at[0, 1 - c, sc[1 + m], :, cols(2)], far.at[pl.ds(m * tok, tok)])
    go(w_out.at[0, 0, :, cols(1)], sib_out)
    go(w_in.at[0, 0, cols(1), :], sib_in)
    for m in range(2):
        go(stash.at[0, mid_slot, sc[1 + m], :, cols(1)], mid.at[pl.ds(m * tok, tok)])
    for copy in copies:
        copy.wait()


def first_body(sc, micro, grads, w_in, w_out, msg, x_v, w_v, wo_v, n_v, st, sems):
    q = sc[0]
    tokens, width = x_v.shape
    tok = tokens // 2
    msg[...] = jnp.zeros(msg.shape, BF)

    def load(src, wsrc, wdst):
        copies = [pltpu.make_async_copy(src.at[m], x_v.at[pl.ds(m * tok, tok)], sems.at[m]) for m in range(2)]
        copies.append(pltpu.make_async_copy(wsrc.at[0, 0], wdst, sems.at[2]))
        for copy in copies:
            copy.start()
        for copy in copies:
            copy.wait()

    @pl.when(q == 0)
    def _():
        load(micro, w_in, w_v)

        @pl.loop(0, tokens // ROWS)
        def _(i):
            rows = pl.ds(pl.multiple_of(i * ROWS, ROWS), ROWS)

            def block(b):
                return x_v[rows, b * LANES : (b + 1) * LANES].astype(F32)

            acc = block(0)
            for b in range(1, width // LANES):
                acc = acc + block(b)
            mean = jnp.sum(acc, axis=1, keepdims=True) * (1.0 / width)
            acc = jnp.zeros((ROWS, LANES), F32)
            for b in range(width // LANES):
                d = block(b) - mean
                acc = acc + d * d
            inv = lax.rsqrt(jnp.sum(acc, axis=1, keepdims=True) * (1.0 / width) + EPS)
            for b in range(width // LANES):
                n_v[rows, b * LANES : (b + 1) * LANES] = ((block(b) - mean) * inv).astype(BF)
            st[rows, :] = jnp.where(lane_iota(ROWS) == 0, mean, inv)

        latent = dot_nn(n_v[...], w_v[...])
        msg[:tokens] = latent.astype(BF)
        t0, t1 = st[:LANES].T, st[LANES:].T
        msg[tokens:] = pack_rows((t0[0:1], t0[1:2]), (t1[0:1], t1[1:2]), None)

    @pl.when(q == 3)
    def _():
        load(grads, w_out, wo_v)
        msg[:tokens] = dot_nt(x_v[...], wo_v[...]).astype(BF)


def forward_body(section, sc, *refs):
    first = section == 1
    refs = list(refs)
    take = refs.pop
    msgs = [take(0) for _ in range(4)]
    h_in = take(0)
    exps = take(0)
    stash, held = take(0), take(0)
    wi_own, wo_own, wi_near, wo_near = [take(0) for _ in range(4)]
    same, cross = [take(0) for _ in range(4)], [take(0) for _ in range(4)]
    h_out, normed, msg, latf, invb, colsum_out = [take(0) for _ in range(6)]
    x_v, pick, up, cen, wo_v, wi_v, st, mc = [take(0) for _ in range(8)]
    lat_v, e_v, factor, sems = [take(0) for _ in range(4)]
    q = sc[0]
    c = q % 2
    tokens, quarter = pick.shape
    tok = tokens // 2
    cols = pl.ds(pl.multiple_of(q * quarter, quarter), quarter)
    start_weight(section - 1, sc, wo_own.at[0, 0, :, cols], wo_near, same, cross, False, wo_v, sems.at[0])
    for m in range(2):
        pltpu.make_async_copy(exps.at[section - 1, m], e_v.at[pl.ds(m * exps.shape[2], exps.shape[2])], sems.at[4]).start()
    if first:
        for m in range(2):
            pltpu.make_async_copy(h_in.at[m, :, cols], x_v.at[pl.ds(m * tok, tok)], sems.at[2]).start()
    if section == 2:
        local, slot = (q == 1) | (q == 2), jnp.where(q == 1, 1, 0)
    else:
        local, slot = (q // 2 == 0) if section == 1 else (q // 2 == 1), 1 - c
    for m in range(2):
        rows = pl.ds(m * tok, tok)
        start_first(
            [
                (local, stash.at[0, slot, sc[1 + m], :, cols], pick.at[rows]),
                (jnp.logical_not(local), held.at[rows], pick.at[rows]),
            ],
            sems.at[3],
        )
    start_weight(section, sc, wi_own.at[0, 0, cols, :], wi_near, same, cross, True, wi_v, sems.at[1])

    if first:
        for k in range(4):
            @pl.when(q == k)
            def _(k=k):
                lat_v[...] = msgs[k][...]

        (m0, m1), (v0, v1), _ = unpack_rows(lat_v[tokens:])
        both = jnp.concatenate([columns([m0, v0]), columns([m1, v1])], axis=0)
        latent = lat_v[:tokens].astype(F32)
        mean, inv = both[:, 0:1], both[:, 1:2]
        colsum_out[...] = jnp.zeros(colsum_out.shape, F32)
    else:
        latent, mean, inv, colsum = join_latent([m[...] for m in msgs], tokens, quarter)
        colsum_out[...] = jnp.broadcast_to(colsum, colsum_out.shape)
    latf[...] = latent
    invb[...] = jnp.broadcast_to(inv, invb.shape)
    mc[...] = jnp.broadcast_to(mean, mc.shape)
    wait_for(wo_v, sems.at[0])
    up[...] = dot_nn(latent.astype(BF), wo_v[...])
    wait_for(e_v, sems.at[4])
    factors(e_v, q, factor)
    if first:
        wait_for(x_v, sems.at[2])
        src = x_v
    else:
        src = h_in
    wait_for(pick, sems.at[3])

    @pl.loop(0, tokens // ROWS)
    def _(i):
        rows = pl.ds(pl.multiple_of(i * ROWS, ROWS), ROWS)
        mean_t, inv_t = mc[rows, :], invb[rows, :]
        fac = factor[rows, :]
        acc = jnp.zeros((ROWS, LANES), F32)
        kept = []
        for b in range(quarter // LANES):
            lanes = slice(b * LANES, (b + 1) * LANES)
            h = src[rows, lanes].astype(F32)
            normed[rows, lanes] = ((h - mean_t) * inv_t).astype(BF)
            stored = pick[rows, lanes].astype(F32)
            f = fac[:, b : b + 1]
            d = jnp.clip(h + up[rows, lanes] - stored, f * -8.0, f * 7.0).astype(BF)
            h = stored + d.astype(F32)
            h_out[rows, lanes] = h
            acc = acc + h
            kept.append(h)
        mean_d = jnp.sum(acc, axis=1, keepdims=True) * (1.0 / quarter)
        acc = jnp.zeros((ROWS, LANES), F32)
        for b in range(quarter // LANES):
            d = kept[b] - mean_d
            cen[rows, b * LANES : (b + 1) * LANES] = d.astype(BF)
            acc = acc + d * d
        var_d = jnp.sum(acc, axis=1, keepdims=True) * (1.0 / quarter)
        st[rows, :] = jnp.where(lane_iota(ROWS) == 0, mean_d, var_d)

    wait_for(wi_v, sems.at[1])
    w = wi_v[...]
    msg[:tokens] = dot_nn(cen[...], w).astype(BF)
    colsum = dot_nn(jnp.ones((16, quarter), BF), w)[0:1]
    t0, t1 = st[:LANES].T, st[LANES:].T
    msg[tokens:] = pack_rows((t0[0:1], t0[1:2]), (t1[0:1], t1[1:2]), colsum)


def backward_body(section, sc, *refs):
    top = section == 3
    refs = list(refs)
    take = refs.pop
    msgs = [take(0) for _ in range(4)]
    if top:
        lat_msgs = [take(0) for _ in range(4)]
        h_in = take(0)
    else:
        normed_in, latf, invb, colsum_in = [take(0) for _ in range(4)]
    g_in = take(0)
    exps = take(0)
    wi_own, wo_own, wi_near, wo_near = [take(0) for _ in range(4)]
    same, cross = [take(0) for _ in range(4)], [take(0) for _ in range(4)]
    g_out, msg, glat_out = [take(0) for _ in range(3)]
    if top:
        normed, latf, g_v = [take(0) for _ in range(3)]
    gn, wo_v, wi_v, mc, inv_v, a_v, b_v, e_v, factor, sems = [take(0) for _ in range(10)]
    q = sc[0]
    tokens, quarter = gn.shape
    tok = tokens // 2
    width = 4 * quarter
    cols = pl.ds(pl.multiple_of(q * quarter, quarter), quarter)
    start_weight(section, sc, wi_own.at[0, 0, cols, :], wi_near, same, cross, True, wi_v, sems.at[0])
    for m in range(2):
        pltpu.make_async_copy(exps.at[section, m], e_v.at[pl.ds(m * exps.shape[2], exps.shape[2])], sems.at[3]).start()
    start_weight(section - 1, sc, wo_own.at[0, 0, :, cols], wo_near, same, cross, False, wo_v, sems.at[1])
    if top:
        for m in range(2):
            pltpu.make_async_copy(g_in.at[m, :, cols], g_v.at[pl.ds(m * tok, tok)], sems.at[2]).start()
        latent, mean, inv, colsum = join_latent([m[...] for m in lat_msgs], tokens, quarter)
        latf[...] = latent
        mc[...] = jnp.broadcast_to(mean, mc.shape)
        inv_v[...] = jnp.broadcast_to(inv, inv_v.shape)
        for k in range(4):
            @pl.when(q ^ 3 == k)
            def _(k=k):
                glat_out[...] = msgs[k][:tokens]

        glat = glat_out[...]
        src, norm, inv_ref = g_v, normed, inv_v
    else:
        latent, colsum = latf[...], colsum_in[0:1]
        glat = msgs[0][:tokens].astype(F32)
        for m in msgs[1:]:
            glat = glat + m[:tokens].astype(F32)
        glat = glat.astype(BF)
        glat_out[...] = glat
        src, norm, inv_ref = g_in, normed_in, invb
    wide = glat.astype(F32)
    a_v[...] = jnp.broadcast_to(jnp.sum(wide * colsum, axis=1, keepdims=True) * (1.0 / width), a_v.shape)
    b_v[...] = jnp.broadcast_to(jnp.sum(wide * latent, axis=1, keepdims=True) * (1.0 / width), b_v.shape)
    wait_for(wi_v, sems.at[0])
    gn[...] = dot_nt(glat, wi_v[...])
    wait_for(e_v, sems.at[3])
    factors(e_v, q, factor)
    if top:
        wait_for(g_v, sems.at[2])

    @pl.loop(0, tokens // ROWS)
    def _(i):
        rows = pl.ds(pl.multiple_of(i * ROWS, ROWS), ROWS)
        fac = factor[rows, :]
        inv_t, a_t, b_t = inv_ref[rows, :], a_v[rows, :], b_v[rows, :]
        for b in range(quarter // LANES):
            lanes = slice(b * LANES, (b + 1) * LANES)
            if top:
                n = (h_in[rows, lanes] - mc[rows, :]) * inv_t
                normed[rows, lanes] = n.astype(BF)
            else:
                n = norm[rows, lanes].astype(F32)
            f = fac[:, b : b + 1]
            g = src[rows, lanes].astype(F32) + inv_t * (gn[rows, lanes] - a_t - n * b_t)
            g_out[rows, lanes] = jnp.clip(g, f * -128.0, f * 127.0).astype(BF)

    wait_for(wo_v, sems.at[1])
    msg[...] = dot_nt(g_out[...], wo_v[...]).astype(BF)


def grads_body(normed, latf, g_ref, glat, gin, gout):
    gin[...] = dot_tn(normed[...], glat[...]).astype(BF)
    gout[...] = dot_tn(latf[...].astype(BF), g_ref[...]).astype(BF)


def grads_top_body(sc, normed, latf, g_ref, glat, gin, gout, g_v, sems):
    quarter = g_v.shape[1]
    tok = g_v.shape[0] // 2
    cols = pl.ds(pl.multiple_of(sc[0] * quarter, quarter), quarter)
    for m in range(2):
        pltpu.make_async_copy(g_ref.at[m, :, cols], g_v.at[pl.ds(m * tok, tok)], sems.at[0]).start()
    gin[...] = dot_tn(normed[...], glat[...]).astype(BF)
    wait_for(g_v, sems.at[0])
    gout[...] = dot_tn(latf[...].astype(BF), g_v[...]).astype(BF)


def grads_first_body(sc, *refs):
    refs = list(refs)
    take = refs.pop
    msgs = [take(0) for _ in range(4)]
    normed, latf, g_ref = [take(0) for _ in range(3)]
    gins = [None] + [take(0) for _ in range(3)]
    gouts = [None] + [take(0) for _ in range(3)]
    a, b = [take(0) for _ in range(4)], [take(0) for _ in range(4)]
    gin0, gout0 = take(0), take(0)
    gins[0], gouts[0] = gin0, gout0
    x, y = sc[3], sc[5]
    glat = msgs[0][...].astype(F32)
    for m in msgs[1:]:
        glat = glat + m[...].astype(F32)
    gin0[...] = dot_tn(normed[...], glat.astype(BF)).astype(BF)
    gout0[...] = dot_tn(latf[...].astype(BF), g_ref[...]).astype(BF)
    rows, low = a[0].shape[1], b[0].shape[1]
    for k in range(4):
        at = pl.ds(pl.multiple_of(((x + k) % 4) * rows, rows), rows)
        to = pl.ds(pl.multiple_of(((y + k) % 4) * low, low), low)
        for s in range(4):
            a[k][s] = gins[s][at, :]
            b[k][s] = gouts[s][to, :]


def total_of(parts):
    total = parts[0].astype(F32)
    for part in parts[1:]:
        total = total + part.astype(F32)
    return total.astype(BF)


def second_body(sc, a0, a1, a2, a3, b0, b1, b2, b3, c0, c1, c2, c3, d0, d1, d2, d3, a_v, b_v):
    x, y = sc[3], sc[5]
    for s in range(4):
        a_v[s] = total_of([r[s] for r in (a0, a1, a2, a3)])
        b_v[s] = total_of([r[s] for r in (b0, b1, b2, b3)])
    rows, cols = c0.shape[1], d0.shape[2]
    for k, (c, d) in enumerate(((c0, d0), (c1, d1), (c2, d2), (c3, d3))):
        at = pl.ds(pl.multiple_of(((y + k) % 4) * rows, rows), rows)
        to = pl.ds(pl.multiple_of(((x + k) % 4) * cols, cols), cols)
        for s in range(4):
            c[s] = a_v[s, at, :]
            d[s] = b_v[s, :, to]


def third_body(a0, a1, a2, a3, b0, b1, b2, b3, out):
    rows, low = a0.shape[1], b0.shape[1]
    for s in range(4):
        out[s, :rows] = total_of([r[s] for r in (a0, a1, a2, a3)])
        total = total_of([r[s] for r in (b0, b1, b2, b3)])
        for t in range(total.shape[1] // LANES):
            out[s, rows + t * low : rows + (t + 1) * low] = total[:, t * LANES : (t + 1) * LANES]


def rep_of(x, z, y):
    return x * 8 + z * 4 + y


EVERY = [(x, z, y) for x in range(4) for z in range(2) for y in range(4)]


def along_x(value, k):
    return lax.ppermute(value, "rep", [(rep_of(x, z, y), rep_of((x + k) % 4, z, y)) for x, z, y in EVERY])


def along_y(value, k):
    return lax.ppermute(value, "rep", [(rep_of(x, z, y), rep_of(x, z, (y + k) % 4)) for x, z, y in EVERY])


def along_z(value, k):
    return lax.ppermute(value, "rep", [(rep_of(x, z, y), rep_of(x, (z + k) % 2, y)) for x, z, y in EVERY])


def gather(value, count, move):
    return [value] + [move(value, k) for k in range(1, count)]


def place_body(sc, a0, a1, a2, a3, b0, b1, b2, b3, gin, gout):
    q, x, y = sc[0], sc[3], sc[5]
    quarter = gin.shape[2] // 4
    rows, low = quarter // 16, gout.shape[2] // 4
    for i in range(4):
        a_ref, b_ref = (a0, a1, a2, a3)[i], (b0, b1, b2, b3)[i]
        for j in range(4):
            for d in range(4):
                base = (q ^ d) * quarter
                row = base + ((x - i + 4) % 4) * (quarter // 4) + ((y - j + 4) % 4) * rows
                gin[0, 0, pl.ds(pl.multiple_of(row, rows), rows), :] = a_ref[j, d]
                at = pl.ds(pl.multiple_of(((y - i + 4) % 4) * low, low), low)
                for t in range(quarter // 4 // LANES):
                    col = base + ((x - j + 4) % 4) * (quarter // 4) + t * LANES
                    gout[0, 0, at, pl.ds(pl.multiple_of(col, LANES), LANES)] = b_ref[j, d, t * low : (t + 1) * low, :]


def on_device(micro, grads, stash, sample_ids, fwd_exps, bwd_exps, w_in, w_out):
    q = lax.axis_index("section")
    rep = lax.axis_index("rep")
    x, z, y = rep // 8, (rep // 4) % 2, rep % 4
    tok, width = micro.shape[1], micro.shape[2]
    tokens, quarter, rank = 2 * tok, width // 4, w_in.shape[3]
    fwd_exps, bwd_exps = jnp.swapaxes(fwd_exps, 2, 3), jnp.swapaxes(bwd_exps, 2, 3)
    sc = jnp.stack([q, sample_ids[0, 0], sample_ids[1, 0], x, z, y]).astype(jnp.int32)

    def swap(value, k, sources=range(4)):
        return lax.ppermute(value, "section", [(s, s ^ k) for s in sources])

    def exchange(value):
        return [value] + [swap(value, k) for k in (1, 2, 3)]

    def beside(value, cross):
        pairs = []
        for s in range(4):
            for xx, zz, yy in EVERY:
                pairs.append((s * 32 + rep_of(xx, zz, yy), (s ^ 2 ^ cross) * 32 + rep_of(xx, 1 - zz, yy)))
        return lax.ppermute(value, ("section", "rep"), pairs)

    dma = pltpu.SemaphoreType.DMA
    big = (tokens, quarter)
    qi, qo = (quarter, rank), (rank, quarter)
    far, mid, sib_in, sib_out, same, cross = call(
        send_body,
        [(big, BF, HBM)] * 2 + [(qi, BF, HBM), (qo, BF, HBM)] + [((quarter // 2, rank), BF, ANY)] * 2,
        [dma((14,))],
        [(sc, SMEM), (stash, HBM), (w_in, HBM), (w_out, HBM)],
    )
    same, cross = beside(same, 0), beside(cross, 1)
    (msg0,) = call(
        first_body,
        [((tokens + 16, rank), BF, VMEM)],
        [
            pltpu.VMEM((tokens, width), BF),
            pltpu.VMEM((width, rank), BF),
            pltpu.VMEM((rank, width), BF),
            pltpu.VMEM((tokens, width), BF),
            pltpu.VMEM((tokens, LANES), F32),
            dma((3,)),
        ],
        [(sc, SMEM), (micro, HBM), (grads, HBM), (w_in, HBM), (w_out, HBM)],
        vmem=16,
    )
    far = swap(far, 2)
    msgs0 = [msg0] + [swap(msg0, k, (0, 3)) for k in (1, 2, 3)]
    mid = swap(mid, 1, (1, 2))
    near = [swap(sib_in, 1), swap(sib_out, 1)]
    weights = [w_in, w_out] + near + gather(same, 4, along_x) + gather(cross, 4, along_y)
    weights = list(zip(weights, [HBM, HBM] + [ANY] * 10))

    msgs = msgs0
    h = micro
    kept = []
    for section in (1, 2, 3):
        h, normed, msg, latf, invb, colsum = call(
            functools.partial(forward_body, section),
            [
                (big, F32, VMEM),
                (big, BF, VMEM),
                ((tokens + 16, rank), BF, VMEM),
                ((tokens, rank), F32, VMEM),
                ((tokens, LANES), F32, VMEM),
                ((8, LANES), F32, VMEM),
            ],
            [
                pltpu.VMEM(big, BF),
                pltpu.VMEM(big, BF),
                pltpu.VMEM(big, F32),
                pltpu.VMEM(big, BF),
                pltpu.VMEM(qo, BF),
                pltpu.VMEM(qi, BF),
                pltpu.VMEM((tokens, LANES), F32),
                pltpu.VMEM((tokens, LANES), F32),
                pltpu.VMEM((tokens + 16, rank), BF),
                pltpu.VMEM((2 * fwd_exps.shape[2], tok), jnp.int32),
                pltpu.VMEM((tokens, LANES), F32),
                dma((5,)),
            ],
            [(sc, SMEM)]
            + [(m, VMEM) for m in msgs]
            + [(h, HBM if section == 1 else VMEM), (fwd_exps, HBM), (stash, HBM)]
            + [(mid if section == 2 else far, ANY)]
            + weights,
        )
        kept.append((normed, latf, invb, colsum))
        msgs = exchange(msg)

    gins, gouts = [None] * 4, [None] * 4
    g = grads
    for section in (3, 2, 1):
        top = section == 3
        outs = [(big, BF, VMEM), ((tokens, rank), BF, VMEM), ((tokens, rank), BF, VMEM)]
        scratch = [
            pltpu.VMEM(big, F32),
            pltpu.VMEM(qo, BF),
            pltpu.VMEM(qi, BF),
            pltpu.VMEM((tokens, LANES), F32),
            pltpu.VMEM((tokens, LANES), F32),
            pltpu.VMEM((tokens, LANES), F32),
            pltpu.VMEM((tokens, LANES), F32),
            pltpu.VMEM((2 * bwd_exps.shape[2], tok), jnp.int32),
            pltpu.VMEM((tokens, LANES), F32),
            dma((4,)),
        ]
        if top:
            outs += [(big, BF, VMEM), ((tokens, rank), F32, VMEM)]
            scratch = [pltpu.VMEM(big, BF)] + scratch
            ins = [(m, VMEM) for m in msgs0] + [(m, VMEM) for m in msgs] + [(h, VMEM), (g, HBM)]
        else:
            ins = [(m, VMEM) for m in msgs] + [(v, VMEM) for v in kept[section]] + [(g, VMEM)]
        result = call(
            functools.partial(backward_body, section),
            outs,
            scratch,
            [(sc, SMEM)] + ins + [(bwd_exps, HBM)] + weights,
        )
        next_g, msg, glat = result[:3]
        if top:
            normed, latf = result[3:]
            gin, gout = call(
                grads_top_body,
                [(qi, BF, VMEM), (qo, BF, VMEM)],
                [pltpu.VMEM(big, BF), dma((1,))],
                [(sc, SMEM), (normed, VMEM), (latf, VMEM), (g, HBM), (glat, VMEM)],
            )
        else:
            normed, latf = kept[section][:2]
            gin, gout = call(
                grads_body,
                [(qi, BF, VMEM), (qo, BF, VMEM)],
                [],
                [(normed, VMEM), (latf, VMEM), (g, VMEM), (glat, VMEM)],
            )
        msgs = exchange(msg)
        gins[section], gouts[section] = gin, gout
        g = next_g
    rows, low = quarter // 4, rank // 4
    cut = call(
        grads_first_body,
        [((4, rows, rank), BF, VMEM)] * 4 + [((4, low, quarter), BF, VMEM)] * 4,
        [pltpu.VMEM(qi, BF), pltpu.VMEM(qo, BF)],
        [(sc, SMEM)]
        + [(m, VMEM) for m in msgs]
        + [(kept[0][0], VMEM), (kept[0][1], VMEM), (g, VMEM)]
        + [(v, VMEM) for v in gins[1:] + gouts[1:]],
    )
    a = [cut[0]] + [along_x(cut[k], k) for k in (1, 2, 3)]
    b = [cut[4]] + [along_y(cut[4 + k], k) for k in (1, 2, 3)]
    cut = call(
        second_body,
        [((4, rows // 4, rank), BF, VMEM)] * 4 + [((4, low, rows), BF, VMEM)] * 4,
        [pltpu.VMEM((4, rows, rank), BF), pltpu.VMEM((4, low, quarter), BF)],
        [(sc, SMEM)] + [(v, VMEM) for v in a + b],
    )
    a = [cut[0]] + [along_y(cut[k], k) for k in (1, 2, 3)]
    b = [cut[4]] + [along_x(cut[4 + k], k) for k in (1, 2, 3)]
    (both,) = call(
        third_body,
        [((4, rows // 2, rank), BF, VMEM)],
        [],
        [(v, VMEM) for v in a + b],
    )
    shares = (both.astype(F32) + along_z(both, 1).astype(F32)).astype(BF)
    own = [lax.dynamic_index_in_dim(shares, q ^ k, 0, keepdims=False) for k in range(4)]
    mine = jnp.stack([own[0]] + [swap(own[k], k) for k in (1, 2, 3)])
    a, b = mine[:, : rows // 4], mine[:, rows // 4 :]
    a, b = gather(a, 4, along_y), gather(b, 4, along_x)
    a, b = lax.optimization_barrier((jnp.stack(a), jnp.stack(b)))
    a, b = gather(a, 4, along_x), gather(b, 4, along_y)
    total_in, total_out = call(
        place_body,
        [((1, 1, width, rank), BF, VMEM), ((1, 1, rank, width), BF, VMEM)],
        [],
        [(sc, SMEM)] + [(v, VMEM) for v in a + b],
    )
    return total_in, total_out


def solution(mesh):
    placed = (
        P(None, "rep", None),
        P(None, "rep", None),
        P("section", None, None, "rep", None),
        P(None, "rep"),
        P(None, None, "rep", None),
        P(None, None, "rep", None),
        P("section", None, None, None),
        P("section", None, None, None),
    )
    return jax.shard_map(
        on_device,
        mesh=mesh,
        in_specs=placed,
        out_specs=(P("section", None, None, None), P("section", None, None, None)),
        check_vma=False,
    )
```

```python
import functools

import jax
import jax.numpy as jnp
from jax import lax
from jax.experimental import pallas as pl
from jax.experimental.pallas import tpu as pltpu
from jax.sharding import PartitionSpec as P

EPS = 1e-05
BF = jnp.bfloat16
F32 = jnp.float32
ROWS = 16
LANES = 128
MIB = 1024 * 1024
ANY = pl.BlockSpec(memory_space=pl.ANY)
HBM = pl.BlockSpec(memory_space=pltpu.HBM)
VMEM = pl.BlockSpec(memory_space=pltpu.VMEM)
SMEM = pl.BlockSpec(memory_space=pltpu.SMEM)


def dot_nn(a, b):
    return lax.dot_general(a, b, (((1,), (0,)), ((), ())), preferred_element_type=F32)


def dot_nt(a, b):
    return lax.dot_general(a, b, (((1,), (1,)), ((), ())), preferred_element_type=F32)


def dot_tn(a, b):
    return lax.dot_general(a, b, (((0,), (0,)), ((), ())), preferred_element_type=F32)


class Place:
    def __init__(self, ids):
        rep = lax.axis_index("rep")
        self.ids = ids
        self.at = {0: lax.axis_index("section"), 3: rep // 8, 4: rep // 4 % 2, 5: rep % 4}

    def __getitem__(self, k):
        return self.ids[k - 1, 0] if k in (1, 2) else self.at[k]


def placed(body, ids, *refs):
    body(Place(ids), *refs)


def call(body, outs, scratch, ins, flops=10**8, nbytes=4 * 10**6, vmem=12):
    return pl.pallas_call(
        functools.partial(placed, body) if ins[0][1] is SMEM else body,
        out_shape=[jax.ShapeDtypeStruct(s, d) for s, d, _ in outs],
        in_specs=[spec for _, spec in ins],
        out_specs=[spec for _, _, spec in outs],
        scratch_shapes=scratch,
        compiler_params=pltpu.CompilerParams(vmem_limit_bytes=vmem * MIB),
        cost_estimate=pl.CostEstimate(flops=flops, bytes_accessed=nbytes, transcendentals=0),
    )(*[pltpu.with_memory_space_constraint(a, pltpu.HBM) if spec is HBM else a for a, spec in ins])


def lane_iota(rows):
    return lax.broadcasted_iota(jnp.int32, (rows, LANES), 1)


def row_iota(rows):
    return lax.broadcasted_iota(jnp.int32, (rows, LANES), 0)


def three(x):
    hi = x.astype(BF).astype(F32)
    rest = x - hi
    mid = rest.astype(BF).astype(F32)
    return hi, mid, (rest - mid).astype(BF).astype(F32)


def pack_rows(first_half, second_half, extra):
    at = row_iota(16)
    out = jnp.zeros((16, LANES), F32)
    for base, (a, b) in ((0, first_half), (8, second_half)):
        for j, row in enumerate(three(a) + three(b)):
            out = jnp.where(at == base + j, row, out)
    if extra is not None:
        hi, mid, _ = three(extra)
        out = jnp.where(at == 6, hi, out)
        out = jnp.where(at == 7, mid, out)
    return out.astype(BF)


def unpack_rows(block):
    block = block.astype(F32)

    def joined(base):
        return block[base : base + 1] + block[base + 1 : base + 2] + block[base + 2 : base + 3]

    return (joined(0), joined(8)), (joined(3), joined(11)), block[6:7] + block[7:8]


def columns(rows):
    at = row_iota(LANES)
    out = jnp.zeros((LANES, LANES), F32)
    for j, row in enumerate(rows):
        out = jnp.where(at == j, row, out)
    return out.T


def join_latent(msgs, tokens, width):
    parsed = [unpack_rows(m[tokens : tokens + 16]) for m in msgs]
    total = msgs[0][:tokens].astype(F32)
    for m in msgs[1:]:
        total = total + m[:tokens].astype(F32)
    halves = []
    for half in range(2):
        means = [p[0][half] for p in parsed]
        mean = (means[0] + means[1] + means[2] + means[3]) * 0.25
        offs = [m - mean for m in means]
        var = (parsed[0][1][half] + parsed[1][1][half] + parsed[2][1][half] + parsed[3][1][half]) * 0.25
        var = var + (offs[0] * offs[0] + offs[1] * offs[1] + offs[2] * offs[2] + offs[3] * offs[3]) * 0.25
        halves.append(columns([mean, lax.rsqrt(var + EPS)] + offs))
    cols = jnp.concatenate(halves, axis=0)
    colsum = parsed[0][2]
    for d in range(4):
        total = total + cols[:, 2 + d : 3 + d] * parsed[d][2]
        if d:
            colsum = colsum + parsed[d][2]
    return total * cols[:, 1:2], cols[:, 0:1], cols[:, 1:2], colsum


def start_first(pairs, sem):
    for cond, src, dst in pairs:
        @pl.when(cond)
        def _(src=src, dst=dst):
            pltpu.make_async_copy(src, dst, sem).start()


def start_weight(section, sc, own, near, same, cross, inner, dst, sem):
    q, x, y = sc[0], sc[3], sc[5]
    zh, c = q // 2, q % 2
    here = zh == section // 2
    mine = c == section % 2
    piece = 384

    def start(src, to):
        pltpu.make_async_copy(src, to, sem).start()

    @pl.when(here & mine)
    def _():
        start(own, dst)

    @pl.when(here & jnp.logical_not(mine))
    def _():
        start(near, dst)

    def pieces(refs, me):
        for k in range(4):
            at = ((me - k + 4) % 4) * piece
            if inner:
                start(refs[k].at[pl.ds(0, piece)], dst.at[pl.ds(pl.multiple_of(at, piece), piece)])
            else:
                for t in range(piece // LANES):
                    cols = pl.ds(pl.multiple_of(at + t * LANES, LANES), LANES)
                    start(refs[k].at[pl.ds(piece + t * LANES, LANES)], dst.at[:, cols])

    @pl.when(jnp.logical_not(here) & mine)
    def _():
        pieces(same, x)

    @pl.when(jnp.logical_not(here) & jnp.logical_not(mine))
    def _():
        pieces(cross, y)


def factors(exps, q, out):
    every = exps.shape[0] // 2
    blocks = every // 4
    for k in range(4):
        @pl.when(q == k)
        def _(k=k):
            for m in range(2):
                e = exps[m * every + k * blocks : m * every + (k + 1) * blocks, :]
                f = lax.shift_left(jnp.ones(e.shape, jnp.int32), e + 14).astype(F32) * (2.0**-14)
                full = jnp.concatenate([f, jnp.zeros((LANES - blocks, LANES), F32)], axis=0)
                out[m * LANES : (m + 1) * LANES, :] = full.T


def wait_for(dst, sem):
    pltpu.make_async_copy(dst, dst, sem).wait()


def start_sends(sc, stash, w_in, w_out, far, mid, sib_in, sib_out, same, cross, sems):
    q, x, y = sc[0], sc[3], sc[5]
    c = q % 2
    tok, quarter = far.shape[0] // 2, far.shape[1]
    piece = quarter // 4
    mid_slot = jnp.where(q == 1, 1, 0)
    copies = []

    def go(src, dst):
        copy = pltpu.make_async_copy(src, dst, sems.at[len(copies)])
        copy.start()
        copies.append(copy)

    def cols(k):
        return pl.ds(pl.multiple_of((q ^ k) * quarter, quarter), quarter)

    for k, at, dst in ((2, x, same), (3, y, cross)):
        base = (q ^ k) * quarter + at * piece
        go(w_in.at[0, 0, pl.ds(pl.multiple_of(base, piece), piece), :], dst.at[pl.ds(0, piece)])
        for t in range(piece // LANES):
            from_cols = pl.ds(pl.multiple_of(base + t * LANES, LANES), LANES)
            go(w_out.at[0, 0, :, from_cols], dst.at[pl.ds(piece + t * LANES, LANES)])
    for m in range(2):
        go(stash.at[0, 1 - c, sc[1 + m], :, cols(2)], far.at[pl.ds(m * tok, tok)])
    go(w_out.at[0, 0, :, cols(1)], sib_out)
    go(w_in.at[0, 0, cols(1), :], sib_in)
    for m in range(2):
        go(stash.at[0, mid_slot, sc[1 + m], :, cols(1)], mid.at[pl.ds(m * tok, tok)])
    return copies


def sum_blocks(block, count):
    parts = []
    for b in range(count):
        v = block(b)
        if b < 4:
            parts.append(v)
        else:
            parts[b % 4] = parts[b % 4] + v
    return (parts[0] + parts[1]) + (parts[2] + parts[3])


def first_body(sc, micro, grads, w_in, w_out, stash, msg, far, mid, sib_in, sib_out, same, cross, x_v, w_v, wo_v, n_v, st, sems, send_sems):
    q = sc[0]
    tokens, width = x_v.shape
    tok = tokens // 2
    blocks = width // LANES

    def load(src, wsrc, wdst):
        copies = [pltpu.make_async_copy(src.at[m], x_v.at[pl.ds(m * tok, tok)], sems.at[m]) for m in range(2)]
        copies.append(pltpu.make_async_copy(wsrc.at[0, 0], wdst, sems.at[2]))
        for copy in copies:
            copy.start()
        return copies

    @pl.when(q == 0)
    def _():
        load(micro, w_in, w_v)

    @pl.when(q == 3)
    def _():
        load(grads, w_out, wo_v)

    sends = start_sends(sc, stash, w_in, w_out, far, mid, sib_in, sib_out, same, cross, send_sems)

    @pl.when((q == 1) | (q == 2))
    def _():
        msg[...] = jnp.zeros(msg.shape, BF)

    @pl.when(q == 0)
    def _():
        for m in range(2):
            wait_for(x_v.at[pl.ds(m * tok, tok)], sems.at[m])

            @pl.loop(m * (tok // ROWS), (m + 1) * (tok // ROWS), unroll=2)
            def _(i):
                rows = pl.ds(pl.multiple_of(i * ROWS, ROWS), ROWS)

                def block(b):
                    return x_v[rows, b * LANES : (b + 1) * LANES].astype(F32)

                def square(b):
                    d = block(b) - mean
                    return d * d

                mean = jnp.sum(sum_blocks(block, blocks), axis=1, keepdims=True) * (1.0 / width)
                mean = jnp.broadcast_to(mean, (ROWS, LANES))
                inv = lax.rsqrt(jnp.sum(sum_blocks(square, blocks), axis=1, keepdims=True) * (1.0 / width) + EPS)
                inv = jnp.broadcast_to(inv, (ROWS, LANES))
                for b in range(blocks):
                    n_v[rows, b * LANES : (b + 1) * LANES] = ((block(b) - mean) * inv).astype(BF)
                st[rows, :] = jnp.where(lane_iota(ROWS) == 0, mean, inv)

        wait_for(w_v, sems.at[2])
        latent = dot_nn(n_v[...], w_v[...])
        msg[:tokens] = latent.astype(BF)
        t0, t1 = st[:LANES].T, st[LANES:].T
        msg[tokens:] = pack_rows((t0[0:1], t0[1:2]), (t1[0:1], t1[1:2]), None)

    @pl.when(q == 3)
    def _():
        for m in range(2):
            wait_for(x_v.at[pl.ds(m * tok, tok)], sems.at[m])
        wait_for(wo_v, sems.at[2])
        msg[:tokens] = dot_nt(x_v[...], wo_v[...]).astype(BF)
        msg[tokens:] = jnp.zeros((msg.shape[0] - tokens, msg.shape[1]), BF)

    for copy in sends:
        copy.wait()


def forward_body(section, sc, *refs):
    first = section == 1
    refs = list(refs)
    take = refs.pop
    msgs = [take(0) for _ in range(4)]
    h_in = take(0)
    exps = take(0)
    stash, held = take(0), take(0)
    wi_own, wo_own, wi_near, wo_near = [take(0) for _ in range(4)]
    same, cross = [take(0) for _ in range(4)], [take(0) for _ in range(4)]
    h_out, normed, msg, latf, invb, colsum_out = [take(0) for _ in range(6)]
    x_v, pick, up, cen, wo_v, wi_v, st, mc = [take(0) for _ in range(8)]
    lat_v, e_v, factor, sems = [take(0) for _ in range(4)]
    q = sc[0]
    c = q % 2
    tokens, quarter = pick.shape
    tok = tokens // 2
    cols = pl.ds(pl.multiple_of(q * quarter, quarter), quarter)
    start_weight(section - 1, sc, wo_own.at[0, 0, :, cols], wo_near, same, cross, False, wo_v, sems.at[0])
    for m in range(2):
        pltpu.make_async_copy(exps.at[section - 1, m], e_v.at[pl.ds(m * exps.shape[2], exps.shape[2])], sems.at[4]).start()
    if first:
        for m in range(2):
            pltpu.make_async_copy(h_in.at[m, :, cols], x_v.at[pl.ds(m * tok, tok)], sems.at[2]).start()
    if section == 2:
        local, slot = (q == 1) | (q == 2), jnp.where(q == 1, 1, 0)
    else:
        local, slot = (q // 2 == 0) if section == 1 else (q // 2 == 1), 1 - c
    for m in range(2):
        rows = pl.ds(m * tok, tok)
        start_first(
            [
                (local, stash.at[0, slot, sc[1 + m], :, cols], pick.at[rows]),
                (jnp.logical_not(local), held.at[rows], pick.at[rows]),
            ],
            sems.at[3],
        )
    start_weight(section, sc, wi_own.at[0, 0, cols, :], wi_near, same, cross, True, wi_v, sems.at[1])

    if first:
        for k in range(4):
            @pl.when(q == k)
            def _(k=k):
                lat_v[...] = msgs[k][...]

        (m0, m1), (v0, v1), _ = unpack_rows(lat_v[tokens:])
        both = jnp.concatenate([columns([m0, v0]), columns([m1, v1])], axis=0)
        latent = lat_v[:tokens].astype(F32)
        mean, inv = both[:, 0:1], both[:, 1:2]
        colsum_out[...] = jnp.zeros(colsum_out.shape, F32)
    else:
        latent, mean, inv, colsum = join_latent([m[...] for m in msgs], tokens, quarter)
        colsum_out[...] = jnp.broadcast_to(colsum, colsum_out.shape)
    latf[...] = latent
    invb[...] = jnp.broadcast_to(inv, invb.shape)
    mc[...] = jnp.broadcast_to(mean, mc.shape)
    wait_for(wo_v, sems.at[0])
    up[...] = dot_nn(latent.astype(BF), wo_v[...])
    wait_for(e_v, sems.at[4])
    factors(e_v, q, factor)
    if first:
        wait_for(x_v, sems.at[2])
        src = x_v
    else:
        src = h_in
    wait_for(pick, sems.at[3])

    @pl.loop(0, tokens // ROWS, unroll=2)
    def _(i):
        rows = pl.ds(pl.multiple_of(i * ROWS, ROWS), ROWS)
        mean_t, inv_t = mc[rows, :], invb[rows, :]
        fac = factor[rows, :]
        kept = []
        for b in range(quarter // LANES):
            lanes = slice(b * LANES, (b + 1) * LANES)
            h = src[rows, lanes].astype(F32)
            normed[rows, lanes] = ((h - mean_t) * inv_t).astype(BF)
            stored = pick[rows, lanes].astype(F32)
            f = fac[:, b : b + 1]
            d = jnp.clip(h + up[rows, lanes] - stored, f * -8.0, f * 7.0).astype(BF)
            h = stored + d.astype(F32)
            h_out[rows, lanes] = h
            kept.append(h)
        total = sum_blocks(lambda b: kept[b], quarter // LANES)
        mean_d = jnp.broadcast_to(jnp.sum(total, axis=1, keepdims=True) * (1.0 / quarter), (ROWS, LANES))
        kept = [h - mean_d for h in kept]
        for b in range(quarter // LANES):
            cen[rows, b * LANES : (b + 1) * LANES] = kept[b].astype(BF)
        var_d = jnp.sum(sum_blocks(lambda b: kept[b] * kept[b], quarter // LANES), axis=1, keepdims=True) * (1.0 / quarter)
        st[rows, :] = jnp.where(lane_iota(ROWS) == 0, mean_d, var_d)

    wait_for(wi_v, sems.at[1])
    w = wi_v[...]
    msg[:tokens] = dot_nn(cen[...], w).astype(BF)
    colsum = dot_nn(jnp.ones((16, quarter), BF), w)[0:1]
    t0, t1 = st[:LANES].T, st[LANES:].T
    msg[tokens:] = pack_rows((t0[0:1], t0[1:2]), (t1[0:1], t1[1:2]), colsum)


def backward_body(section, sc, *refs):
    top = section == 3
    refs = list(refs)
    take = refs.pop
    msgs = [take(0) for _ in range(4)]
    if top:
        lat_msgs = [take(0) for _ in range(4)]
        h_in = take(0)
    else:
        normed_in, latf, invb, colsum_in = [take(0) for _ in range(4)]
    g_in = take(0)
    exps = take(0)
    wi_own, wo_own, wi_near, wo_near = [take(0) for _ in range(4)]
    same, cross = [take(0) for _ in range(4)], [take(0) for _ in range(4)]
    g_out, msg, glat_out = [take(0) for _ in range(3)]
    if top:
        normed, latf, g_v = [take(0) for _ in range(3)]
    gn, wo_v, wi_v, mc, inv_v, a_v, b_v, e_v, factor, sems = [take(0) for _ in range(10)]
    q = sc[0]
    tokens, quarter = gn.shape
    tok = tokens // 2
    width = 4 * quarter
    cols = pl.ds(pl.multiple_of(q * quarter, quarter), quarter)
    start_weight(section, sc, wi_own.at[0, 0, cols, :], wi_near, same, cross, True, wi_v, sems.at[0])
    for m in range(2):
        pltpu.make_async_copy(exps.at[section, m], e_v.at[pl.ds(m * exps.shape[2], exps.shape[2])], sems.at[3]).start()
    start_weight(section - 1, sc, wo_own.at[0, 0, :, cols], wo_near, same, cross, False, wo_v, sems.at[1])
    if top:
        for m in range(2):
            pltpu.make_async_copy(g_in.at[m, :, cols], g_v.at[pl.ds(m * tok, tok)], sems.at[2]).start()
        latent, mean, inv, colsum = join_latent([m[...] for m in lat_msgs], tokens, quarter)
        latf[...] = latent
        mc[...] = jnp.broadcast_to(mean, mc.shape)
        inv_v[...] = jnp.broadcast_to(inv, inv_v.shape)
        for k in range(4):
            @pl.when(q ^ 3 == k)
            def _(k=k):
                glat_out[...] = msgs[k][:tokens]

        glat = glat_out[...]
        src, norm, inv_ref = g_v, normed, inv_v
    else:
        latent, colsum = latf[...], colsum_in[0:1]
        glat = msgs[0][:tokens].astype(F32)
        for m in msgs[1:]:
            glat = glat + m[:tokens].astype(F32)
        glat = glat.astype(BF)
        glat_out[...] = glat
        src, norm, inv_ref = g_in, normed_in, invb
    wide = glat.astype(F32)
    a_v[...] = jnp.broadcast_to(jnp.sum(wide * colsum, axis=1, keepdims=True) * (1.0 / width), a_v.shape)
    b_v[...] = jnp.broadcast_to(jnp.sum(wide * latent, axis=1, keepdims=True) * (1.0 / width), b_v.shape)
    wait_for(wi_v, sems.at[0])
    gn[...] = dot_nt(glat, wi_v[...])
    wait_for(e_v, sems.at[3])
    factors(e_v, q, factor)
    if top:
        wait_for(g_v, sems.at[2])

    @pl.loop(0, tokens // ROWS, unroll=2)
    def _(i):
        rows = pl.ds(pl.multiple_of(i * ROWS, ROWS), ROWS)
        fac = factor[rows, :]
        inv_t, a_t, b_t = inv_ref[rows, :], a_v[rows, :], b_v[rows, :]
        for b in range(quarter // LANES):
            lanes = slice(b * LANES, (b + 1) * LANES)
            if top:
                n = (h_in[rows, lanes] - mc[rows, :]) * inv_t
                normed[rows, lanes] = n.astype(BF)
            else:
                n = norm[rows, lanes].astype(F32)
            f = fac[:, b : b + 1]
            g = src[rows, lanes].astype(F32) + inv_t * (gn[rows, lanes] - a_t - n * b_t)
            g_out[rows, lanes] = jnp.clip(g, f * -128.0, f * 127.0).astype(BF)

    wait_for(wo_v, sems.at[1])
    msg[...] = dot_nt(g_out[...], wo_v[...]).astype(BF)


def grads_body(normed, latf, g_ref, glat, gin, gout):
    gin[...] = dot_tn(normed[...], glat[...]).astype(BF)
    gout[...] = dot_tn(latf[...].astype(BF), g_ref[...]).astype(BF)


def grads_top_body(sc, normed, latf, g_ref, glat, gin, gout, g_v, sems):
    quarter = g_v.shape[1]
    tok = g_v.shape[0] // 2
    cols = pl.ds(pl.multiple_of(sc[0] * quarter, quarter), quarter)
    for m in range(2):
        pltpu.make_async_copy(g_ref.at[m, :, cols], g_v.at[pl.ds(m * tok, tok)], sems.at[0]).start()
    gin[...] = dot_tn(normed[...], glat[...]).astype(BF)
    wait_for(g_v, sems.at[0])
    gout[...] = dot_tn(latf[...].astype(BF), g_v[...]).astype(BF)


def grads_first_body(sc, *refs):
    refs = list(refs)
    take = refs.pop
    msgs = [take(0) for _ in range(4)]
    normed, latf, g_ref = [take(0) for _ in range(3)]
    gins = [None] + [take(0) for _ in range(3)]
    gouts = [None] + [take(0) for _ in range(3)]
    a, b = [take(0) for _ in range(5)], [take(0) for _ in range(5)]
    gin0, gout0 = take(0), take(0)
    gins[0], gouts[0] = gin0, gout0
    x, y = sc[3], sc[5]
    glat = msgs[0][...].astype(F32)
    for m in msgs[1:]:
        glat = glat + m[...].astype(F32)
    gin0[...] = dot_tn(normed[...], glat.astype(BF)).astype(BF)
    gout0[...] = dot_tn(latf[...].astype(BF), g_ref[...]).astype(BF)
    rows, low = a[0].shape[1], b[0].shape[1]
    for k in range(4):
        at = pl.ds(pl.multiple_of(((x + k) % 4) * rows, rows), rows)
        to = pl.ds(pl.multiple_of(((y + k) % 4) * low, low), low)
        for s in range(4):
            d, i = (2 + s // 2, s % 2) if k == 2 else ((0, 1, 2, 4)[k], s)
            a[d][i] = gins[s][at, :]
            b[d][i] = gouts[s][to, :]


def relay_body(a1, a3, a_lo, a_hi, b1, b3, b_lo, b_hi, a1_out, a3_out, b1_out, b3_out):
    for src, extra, at, dst in (
        (a1, a_lo, 0, a1_out),
        (a3, a_hi, 2, a3_out),
        (b1, b_lo, 0, b1_out),
        (b3, b_hi, 2, b3_out),
    ):
        for s in range(4):
            if at <= s < at + 2:
                dst[s] = total_of([src[s], extra[s - at]])
            else:
                dst[s] = src[s]


def total_of(parts):
    total = parts[0].astype(F32)
    for part in parts[1:]:
        total = total + part.astype(F32)
    return total.astype(BF)


def second_body(sc, a0, a1, a2, b0, b1, b2, c0, c1, c2, c3, d0, d1, d2, d3, a_v, b_v):
    x, y = sc[3], sc[5]
    for s in range(4):
        a_v[s] = total_of([r[s] for r in (a0, a1, a2)])
        b_v[s] = total_of([r[s] for r in (b0, b1, b2)])
    rows, cols = c0.shape[1], d0.shape[2]
    for k, (c, d) in enumerate(((c0, d0), (c1, d1), (c2, d2), (c3, d3))):
        at = pl.ds(pl.multiple_of(((y + k) % 4) * rows, rows), rows)
        to = pl.ds(pl.multiple_of(((x + k) % 4) * cols, cols), cols)
        for s in range(4):
            c[s] = a_v[s, at, :]
            d[s] = b_v[s, :, to]


def third_body(a0, a1, a2, a3, b0, b1, b2, b3, out):
    rows, low = a0.shape[1], b0.shape[1]
    for s in range(4):
        out[s, :rows] = total_of([r[s] for r in (a0, a1, a2, a3)])
        total = total_of([r[s] for r in (b0, b1, b2, b3)])
        for t in range(total.shape[1] // LANES):
            out[s, rows + t * low : rows + (t + 1) * low] = total[:, t * LANES : (t + 1) * LANES]


def rep_of(x, z, y):
    return x * 8 + z * 4 + y


EVERY = [(x, z, y) for x in range(4) for z in range(2) for y in range(4)]


def along_x(value, k):
    return lax.ppermute(value, "rep", [(rep_of(x, z, y), rep_of((x + k) % 4, z, y)) for x, z, y in EVERY])


def along_y(value, k):
    return lax.ppermute(value, "rep", [(rep_of(x, z, y), rep_of(x, z, (y + k) % 4)) for x, z, y in EVERY])


def along_z(value, k):
    return lax.ppermute(value, "rep", [(rep_of(x, z, y), rep_of(x, (z + k) % 2, y)) for x, z, y in EVERY])


def gather(value, count, move):
    return [value] + [move(value, k) for k in range(1, count)]


def gather_relayed(value, move):
    before, after = move(value, 1), move(value, 3)
    half = value.shape[0] // 2
    return [value, before, move(before[:half], 1), move(after[half:], 3), after]


def place_body(sc, a0, a1, a2, a3, a4, b0, b1, b2, b3, b4, gin, gout):
    q, x, y = sc[0], sc[3], sc[5]
    quarter = gin.shape[2] // 4
    rows, low = quarter // 16, gout.shape[2] // 4
    for back, first, a_ref, b_ref in ((0, 0, a0, b0), (1, 0, a1, b1), (2, 0, a2, b2), (2, 2, a3, b3), (3, 0, a4, b4)):
        for i in range(a_ref.shape[0]):
            j = first + i
            for d in range(4):
                base = (q ^ d) * quarter
                row = base + ((x - back + 4) % 4) * (quarter // 4) + ((y - j + 4) % 4) * rows
                gin[0, 0, pl.ds(pl.multiple_of(row, rows), rows), :] = a_ref[i, d]
                at = pl.ds(pl.multiple_of(((y - back + 4) % 4) * low, low), low)
                for t in range(quarter // 4 // LANES):
                    col = base + ((x - j + 4) % 4) * (quarter // 4) + t * LANES
                    gout[0, 0, at, pl.ds(pl.multiple_of(col, LANES), LANES)] = b_ref[i, d, t * low : (t + 1) * low, :]


def on_device(micro, grads, stash, sample_ids, fwd_exps, bwd_exps, w_in, w_out):
    q = lax.axis_index("section")
    tok, width = micro.shape[1], micro.shape[2]
    tokens, quarter, rank = 2 * tok, width // 4, w_in.shape[3]
    fwd_exps, bwd_exps = jnp.swapaxes(fwd_exps, 2, 3), jnp.swapaxes(bwd_exps, 2, 3)
    sc = sample_ids

    def swap(value, k, sources=range(4)):
        return lax.ppermute(value, "section", [(s, s ^ k) for s in sources])

    def exchange(value):
        return [value] + [swap(value, k) for k in (1, 2, 3)]

    def beside(value, cross):
        pairs = []
        for s in range(4):
            for xx, zz, yy in EVERY:
                pairs.append((s * 32 + rep_of(xx, zz, yy), (s ^ 2 ^ cross) * 32 + rep_of(xx, 1 - zz, yy)))
        return lax.ppermute(value, ("section", "rep"), pairs)

    dma = pltpu.SemaphoreType.DMA
    big = (tokens, quarter)
    qi, qo = (quarter, rank), (rank, quarter)
    msg0, far, mid, sib_in, sib_out, same, cross = call(
        first_body,
        [((tokens + 16, rank), BF, VMEM)]
        + [(big, BF, VMEM)] * 2
        + [(qi, BF, VMEM), (qo, BF, VMEM)]
        + [((quarter // 2, rank), BF, VMEM)] * 2,
        [
            pltpu.VMEM((tokens, width), BF),
            pltpu.VMEM((width, rank), BF),
            pltpu.VMEM((rank, width), BF),
            pltpu.VMEM((tokens, width), BF),
            pltpu.VMEM((tokens, LANES), F32),
            dma((3,)),
            dma((14,)),
        ],
        [(sc, SMEM), (micro, HBM), (grads, HBM), (w_in, HBM), (w_out, HBM), (stash, HBM)],
        vmem=20,
    )
    same, cross = beside(same, 0), beside(cross, 1)
    msgs0 = [swap(msg0, k, (0, 3)) for k in (1, 2, 3)]
    same, cross, msgs0, far, sib_in, sib_out, mid = lax.optimization_barrier((same, cross, msgs0, far, sib_in, sib_out, mid))
    msgs0 = [msg0] + msgs0
    far = swap(far, 2)
    pieces = gather(same, 4, along_x) + gather(cross, 4, along_y)
    near = [swap(sib_in, 1), swap(sib_out, 1)]
    pieces, far, near, mid = lax.optimization_barrier((pieces, far, near, mid))
    mid = swap(mid, 1, (1, 2))
    weights = [w_in, w_out] + near + pieces
    weights = list(zip(weights, [HBM, HBM] + [ANY] * 10))

    msgs = msgs0
    h = micro
    kept = []
    for section in (1, 2, 3):
        h, normed, msg, latf, invb, colsum = call(
            functools.partial(forward_body, section),
            [
                (big, F32, VMEM),
                (big, BF, VMEM),
                ((tokens + 16, rank), BF, VMEM),
                ((tokens, rank), F32, VMEM),
                ((tokens, LANES), F32, VMEM),
                ((8, LANES), F32, VMEM),
            ],
            [
                pltpu.VMEM(big, BF),
                pltpu.VMEM(big, BF),
                pltpu.VMEM(big, F32),
                pltpu.VMEM(big, BF),
                pltpu.VMEM(qo, BF),
                pltpu.VMEM(qi, BF),
                pltpu.VMEM((tokens, LANES), F32),
                pltpu.VMEM((tokens, LANES), F32),
                pltpu.VMEM((tokens + 16, rank), BF),
                pltpu.VMEM((2 * fwd_exps.shape[2], tok), jnp.int32),
                pltpu.VMEM((tokens, LANES), F32),
                dma((5,)),
            ],
            [(sc, SMEM)]
            + [(m, VMEM) for m in msgs]
            + [(h, HBM if section == 1 else VMEM), (fwd_exps, HBM), (stash, HBM)]
            + [(mid if section == 2 else far, ANY)]
            + weights,
        )
        kept.append((normed, latf, invb, colsum))
        msgs = exchange(msg)

    gins, gouts = [None] * 4, [None] * 4
    g = grads
    for section in (3, 2, 1):
        top = section == 3
        outs = [(big, BF, VMEM), ((tokens, rank), BF, VMEM), ((tokens, rank), BF, VMEM)]
        scratch = [
            pltpu.VMEM(big, F32),
            pltpu.VMEM(qo, BF),
            pltpu.VMEM(qi, BF),
            pltpu.VMEM((tokens, LANES), F32),
            pltpu.VMEM((tokens, LANES), F32),
            pltpu.VMEM((tokens, LANES), F32),
            pltpu.VMEM((tokens, LANES), F32),
            pltpu.VMEM((2 * bwd_exps.shape[2], tok), jnp.int32),
            pltpu.VMEM((tokens, LANES), F32),
            dma((4,)),
        ]
        if top:
            outs += [(big, BF, VMEM), ((tokens, rank), F32, VMEM)]
            scratch = [pltpu.VMEM(big, BF)] + scratch
            ins = [(m, VMEM) for m in msgs0] + [(m, VMEM) for m in msgs] + [(h, VMEM), (g, HBM)]
        else:
            ins = [(m, VMEM) for m in msgs] + [(v, VMEM) for v in kept[section]] + [(g, VMEM)]
        result = call(
            functools.partial(backward_body, section),
            outs,
            scratch,
            [(sc, SMEM)] + ins + [(bwd_exps, HBM)] + weights,
        )
        next_g, msg, glat = result[:3]
        if top:
            normed, latf = result[3:]
            gin, gout = call(
                grads_top_body,
                [(qi, BF, VMEM), (qo, BF, VMEM)],
                [pltpu.VMEM(big, BF), dma((1,))],
                [(sc, SMEM), (normed, VMEM), (latf, VMEM), (g, HBM), (glat, VMEM)],
            )
        else:
            normed, latf = kept[section][:2]
            gin, gout = call(
                grads_body,
                [(qi, BF, VMEM), (qo, BF, VMEM)],
                [],
                [(normed, VMEM), (latf, VMEM), (g, VMEM), (glat, VMEM)],
            )
        msgs = exchange(msg)
        gins[section], gouts[section] = gin, gout
        g = next_g
    rows, low = quarter // 4, rank // 4
    cut = call(
        grads_first_body,
        [((n, rows, rank), BF, VMEM) for n in (4, 4, 2, 2, 4)] + [((n, low, quarter), BF, VMEM) for n in (4, 4, 2, 2, 4)],
        [pltpu.VMEM(qi, BF), pltpu.VMEM(qo, BF)],
        [(sc, SMEM)]
        + [(m, VMEM) for m in msgs]
        + [(kept[0][0], VMEM), (kept[0][1], VMEM), (g, VMEM)]
        + [(v, VMEM) for v in gins[1:] + gouts[1:]],
    )
    a, b = cut[:5], cut[5:]
    far_a, far_b = (along_x(a[2], 1), along_x(a[3], 3)), (along_y(b[2], 1), along_y(b[3], 3))
    to_a, back_a, to_b, back_b = call(
        relay_body,
        [((4, rows, rank), BF, VMEM)] * 2 + [((4, low, quarter), BF, VMEM)] * 2,
        [],
        [(v, VMEM) for v in (a[1], a[4], *far_a, b[1], b[4], *far_b)],
    )
    a = [a[0], along_x(to_a, 1), along_x(back_a, 3)]
    b = [b[0], along_y(to_b, 1), along_y(back_b, 3)]
    cut = call(
        second_body,
        [((4, rows // 4, rank), BF, VMEM)] * 4 + [((4, low, rows), BF, VMEM)] * 4,
        [pltpu.VMEM((4, rows, rank), BF), pltpu.VMEM((4, low, quarter), BF)],
        [(sc, SMEM)] + [(v, VMEM) for v in a + b],
    )
    a = [cut[0]] + [along_y(cut[k], k) for k in (1, 2, 3)]
    b = [cut[4]] + [along_x(cut[4 + k], k) for k in (1, 2, 3)]
    (both,) = call(
        third_body,
        [((4, rows // 2, rank), BF, VMEM)],
        [],
        [(v, VMEM) for v in a + b],
    )
    shares = (both.astype(F32) + along_z(both, 1).astype(F32)).astype(BF)
    own = [lax.dynamic_index_in_dim(shares, q ^ k, 0, keepdims=False) for k in range(4)]
    mine = jnp.stack([own[0]] + [swap(own[k], k) for k in (1, 2, 3)])
    a, b = mine[:, : rows // 4], mine[:, rows // 4 :]
    a, b = gather(a, 4, along_y), gather(b, 4, along_x)
    a, b = lax.optimization_barrier((jnp.stack(a), jnp.stack(b)))
    a, b = gather_relayed(a, along_x), gather_relayed(b, along_y)
    total_in, total_out = call(
        place_body,
        [((1, 1, width, rank), BF, VMEM), ((1, 1, rank, width), BF, VMEM)],
        [],
        [(sc, SMEM)] + [(v, VMEM) for v in a + b],
    )
    return total_in, total_out


def solution(mesh):
    placed = (
        P(None, "rep", None),
        P(None, "rep", None),
        P("section", None, None, "rep", None),
        P(None, "rep"),
        P(None, None, "rep", None),
        P(None, None, "rep", None),
        P("section", None, None, None),
        P("section", None, None, None),
    )
    return jax.shard_map(
        on_device,
        mesh=mesh,
        in_specs=placed,
        out_specs=(P("section", None, None, None), P("section", None, None, None)),
        check_vma=False,
    )
```

```python
import functools

import jax
import jax.numpy as jnp
from jax import lax
from jax.experimental import pallas as pl
from jax.experimental.pallas import tpu as pltpu
from jax.sharding import PartitionSpec as P

EPS = 1e-05
BF = jnp.bfloat16
F32 = jnp.float32
ROWS = 16
LANES = 128
MIB = 1024 * 1024
ANY = pl.BlockSpec(memory_space=pl.ANY)
HBM = pl.BlockSpec(memory_space=pltpu.HBM)
VMEM = pl.BlockSpec(memory_space=pltpu.VMEM)
SMEM = pl.BlockSpec(memory_space=pltpu.SMEM)


def dot_nn(a, b):
    return lax.dot_general(a, b, (((1,), (0,)), ((), ())), preferred_element_type=F32)


def dot_nt(a, b):
    return lax.dot_general(a, b, (((1,), (1,)), ((), ())), preferred_element_type=F32)


def dot_tn(a, b):
    return lax.dot_general(a, b, (((0,), (0,)), ((), ())), preferred_element_type=F32)


class Place:
    def __init__(self, ids):
        rep = lax.axis_index("rep")
        self.ids = ids
        self.at = {0: lax.axis_index("section"), 3: rep // 8, 4: rep // 4 % 2, 5: rep % 4}

    def __getitem__(self, k):
        return self.ids[k - 1, 0] if k in (1, 2) else self.at[k]


def placed(body, ids, *refs):
    body(Place(ids), *refs)


def call(body, outs, scratch, ins, flops=10**8, nbytes=4 * 10**6, vmem=12):
    return pl.pallas_call(
        functools.partial(placed, body) if ins[0][1] is SMEM else body,
        out_shape=[jax.ShapeDtypeStruct(s, d) for s, d, _ in outs],
        in_specs=[spec for _, spec in ins],
        out_specs=[spec for _, _, spec in outs],
        scratch_shapes=scratch,
        compiler_params=pltpu.CompilerParams(vmem_limit_bytes=vmem * MIB),
        cost_estimate=pl.CostEstimate(flops=flops, bytes_accessed=nbytes, transcendentals=0),
    )(*[pltpu.with_memory_space_constraint(a, pltpu.HBM) if spec is HBM else a for a, spec in ins])


def lane_iota(rows):
    return lax.broadcasted_iota(jnp.int32, (rows, LANES), 1)


def row_iota(rows):
    return lax.broadcasted_iota(jnp.int32, (rows, LANES), 0)


def three(x):
    hi = x.astype(BF).astype(F32)
    rest = x - hi
    mid = rest.astype(BF).astype(F32)
    return hi, mid, (rest - mid).astype(BF).astype(F32)


def pack_rows(first_half, second_half, extra):
    at = row_iota(16)
    out = jnp.zeros((16, LANES), F32)
    for base, (a, b) in ((0, first_half), (8, second_half)):
        for j, row in enumerate(three(a) + three(b)):
            out = jnp.where(at == base + j, row, out)
    if extra is not None:
        hi, mid, _ = three(extra)
        out = jnp.where(at == 6, hi, out)
        out = jnp.where(at == 7, mid, out)
    return out.astype(BF)


def unpack_rows(block):
    block = block.astype(F32)

    def joined(base):
        return block[base : base + 1] + block[base + 1 : base + 2] + block[base + 2 : base + 3]

    return (joined(0), joined(8)), (joined(3), joined(11)), block[6:7] + block[7:8]


def columns(rows):
    at = row_iota(LANES)
    out = jnp.zeros((LANES, LANES), F32)
    for j, row in enumerate(rows):
        out = jnp.where(at == j, row, out)
    return out.T


def join_latent(msgs, tokens, width):
    parsed = [unpack_rows(m[tokens : tokens + 16]) for m in msgs]
    total = msgs[0][:tokens].astype(F32)
    for m in msgs[1:]:
        total = total + m[:tokens].astype(F32)
    halves = []
    for half in range(2):
        means = [p[0][half] for p in parsed]
        mean = (means[0] + means[1] + means[2] + means[3]) * 0.25
        offs = [m - mean for m in means]
        var = (parsed[0][1][half] + parsed[1][1][half] + parsed[2][1][half] + parsed[3][1][half]) * 0.25
        var = var + (offs[0] * offs[0] + offs[1] * offs[1] + offs[2] * offs[2] + offs[3] * offs[3]) * 0.25
        halves.append(columns([mean, lax.rsqrt(var + EPS)] + offs))
    cols = jnp.concatenate(halves, axis=0)
    colsum = parsed[0][2]
    for d in range(4):
        total = total + cols[:, 2 + d : 3 + d] * parsed[d][2]
        if d:
            colsum = colsum + parsed[d][2]
    return total * cols[:, 1:2], cols[:, 0:1], cols[:, 1:2], colsum


def start_first(pairs, sem):
    for cond, src, dst in pairs:
        @pl.when(cond)
        def _(src=src, dst=dst):
            pltpu.make_async_copy(src, dst, sem).start()


def start_weight(section, sc, own, near, same, cross, inner, dst, sem):
    q, x, y = sc[0], sc[3], sc[5]
    zh, c = q // 2, q % 2
    here = zh == section // 2
    mine = c == section % 2
    piece = 384

    def start(src, to):
        pltpu.make_async_copy(src, to, sem).start()

    @pl.when(here & mine)
    def _():
        start(own, dst)

    @pl.when(here & jnp.logical_not(mine))
    def _():
        start(near, dst)

    def pieces(refs, first):
        for j in range(2):
            for i in range(2):
                px, py = (i, j) if first == 0 else (j, i)
                at = piece_of(x ^ px, y ^ py) * piece
                base = i * 2 * piece
                if inner:
                    start(refs[j].at[pl.ds(base, piece)], dst.at[pl.ds(pl.multiple_of(at, piece), piece)])
                else:
                    for t in range(piece // LANES):
                        cols = pl.ds(pl.multiple_of(at + t * LANES, LANES), LANES)
                        start(refs[j].at[pl.ds(base + piece + t * LANES, LANES)], dst.at[:, cols])

    @pl.when(jnp.logical_not(here) & mine)
    def _():
        pieces(same, 0)

    @pl.when(jnp.logical_not(here) & jnp.logical_not(mine))
    def _():
        pieces(cross, 1)


def piece_of(x, y):
    return (x & 1) * 2 + (y & 1)


def factors(exps, q, out):
    every = exps.shape[0] // 2
    blocks = every // 4
    for k in range(4):
        @pl.when(q == k)
        def _(k=k):
            for m in range(2):
                e = exps[m * every + k * blocks : m * every + (k + 1) * blocks, :]
                f = lax.shift_left(jnp.ones(e.shape, jnp.int32), e + 14).astype(F32) * (2.0**-14)
                full = jnp.concatenate([f, jnp.zeros((LANES - blocks, LANES), F32)], axis=0)
                out[m * LANES : (m + 1) * LANES, :] = full.T


def wait_for(dst, sem):
    pltpu.make_async_copy(dst, dst, sem).wait()


def send_body(sc, stash, w_in, w_out, far, mid, sib_in, sib_out, over, sems):
    q, x, y = sc[0], sc[3], sc[5]
    c = q % 2
    tok, quarter = far.shape[0] // 2, far.shape[1]
    piece = quarter // 4
    mid_slot = jnp.where(q == 1, 1, 0)
    copies = []

    def go(src, dst):
        copy = pltpu.make_async_copy(src, dst, sems.at[len(copies)])
        copy.start()
        copies.append(copy)

    def cols(k):
        return pl.ds(pl.multiple_of((q ^ k) * quarter, quarter), quarter)

    for k in (2, 3):
        base = (q ^ k) * quarter + piece_of(x, y) * piece
        first = (k - 2) * 2 * piece
        go(w_in.at[0, 0, pl.ds(pl.multiple_of(base, piece), piece), :], over.at[pl.ds(first, piece)])
        for t in range(piece // LANES):
            from_cols = pl.ds(pl.multiple_of(base + t * LANES, LANES), LANES)
            go(w_out.at[0, 0, :, from_cols], over.at[pl.ds(first + piece + t * LANES, LANES)])
    for m in range(2):
        go(stash.at[0, 1 - c, sc[1 + m], :, cols(2)], far.at[pl.ds(m * tok, tok)])
    go(w_out.at[0, 0, :, cols(1)], sib_out)
    go(w_in.at[0, 0, cols(1), :], sib_in)
    for m in range(2):
        go(stash.at[0, mid_slot, sc[1 + m], :, cols(1)], mid.at[pl.ds(m * tok, tok)])
    for copy in copies:
        copy.wait()


def sum_blocks(block, count):
    parts = []
    for b in range(count):
        v = block(b)
        if b < 4:
            parts.append(v)
        else:
            parts[b % 4] = parts[b % 4] + v
    return (parts[0] + parts[1]) + (parts[2] + parts[3])


def first_body(sc, micro, grads, w_in, w_out, msg, x_v, w_v, wo_v, n_v, st, sems):
    q = sc[0]
    tokens, width = x_v.shape
    tok = tokens // 2
    blocks = width // LANES

    def load(src, wsrc, wdst):
        copies = [pltpu.make_async_copy(src.at[m], x_v.at[pl.ds(m * tok, tok)], sems.at[m]) for m in range(2)]
        copies.append(pltpu.make_async_copy(wsrc.at[0, 0], wdst, sems.at[2]))
        for copy in copies:
            copy.start()
        return copies

    @pl.when(q == 0)
    def _():
        load(micro, w_in, w_v)

    @pl.when(q == 3)
    def _():
        load(grads, w_out, wo_v)

    @pl.when((q == 1) | (q == 2))
    def _():
        msg[...] = jnp.zeros(msg.shape, BF)

    @pl.when(q == 0)
    def _():
        for m in range(2):
            wait_for(x_v.at[pl.ds(m * tok, tok)], sems.at[m])

            @pl.loop(m * (tok // ROWS), (m + 1) * (tok // ROWS), unroll=2)
            def _(i):
                rows = pl.ds(pl.multiple_of(i * ROWS, ROWS), ROWS)

                def block(b):
                    return x_v[rows, b * LANES : (b + 1) * LANES].astype(F32)

                def square(b):
                    d = block(b) - mean
                    return d * d

                mean = jnp.sum(sum_blocks(block, blocks), axis=1, keepdims=True) * (1.0 / width)
                mean = jnp.broadcast_to(mean, (ROWS, LANES))
                inv = lax.rsqrt(jnp.sum(sum_blocks(square, blocks), axis=1, keepdims=True) * (1.0 / width) + EPS)
                inv = jnp.broadcast_to(inv, (ROWS, LANES))
                for b in range(blocks):
                    n_v[rows, b * LANES : (b + 1) * LANES] = ((block(b) - mean) * inv).astype(BF)
                st[rows, :] = jnp.where(lane_iota(ROWS) == 0, mean, inv)

        wait_for(w_v, sems.at[2])
        latent = dot_nn(n_v[...], w_v[...])
        msg[:tokens] = latent.astype(BF)
        t0, t1 = st[:LANES].T, st[LANES:].T
        msg[tokens:] = pack_rows((t0[0:1], t0[1:2]), (t1[0:1], t1[1:2]), None)

    @pl.when(q == 3)
    def _():
        for m in range(2):
            wait_for(x_v.at[pl.ds(m * tok, tok)], sems.at[m])
        wait_for(wo_v, sems.at[2])
        msg[:tokens] = dot_nt(x_v[...], wo_v[...]).astype(BF)
        msg[tokens:] = jnp.zeros((msg.shape[0] - tokens, msg.shape[1]), BF)


def forward_body(section, sc, *refs):
    first = section == 1
    refs = list(refs)
    take = refs.pop
    msgs = [take(0) for _ in range(4)]
    h_in = take(0)
    exps = take(0)
    stash, held = take(0), take(0)
    wi_own, wo_own, wi_near, wo_near = [take(0) for _ in range(4)]
    same, cross = [take(0) for _ in range(2)], [take(0) for _ in range(2)]
    h_out, normed, msg, latf, invb, colsum_out = [take(0) for _ in range(6)]
    x_v, pick, up, cen, wo_v, wi_v, st, mc = [take(0) for _ in range(8)]
    lat_v, e_v, factor, sems = [take(0) for _ in range(4)]
    q = sc[0]
    c = q % 2
    tokens, quarter = pick.shape
    tok = tokens // 2
    cols = pl.ds(pl.multiple_of(q * quarter, quarter), quarter)
    start_weight(section - 1, sc, wo_own.at[0, 0, :, cols], wo_near, same, cross, False, wo_v, sems.at[0])
    for m in range(2):
        pltpu.make_async_copy(exps.at[section - 1, m], e_v.at[pl.ds(m * exps.shape[2], exps.shape[2])], sems.at[4]).start()
    if first:
        for m in range(2):
            pltpu.make_async_copy(h_in.at[m, :, cols], x_v.at[pl.ds(m * tok, tok)], sems.at[2]).start()
    if section == 2:
        local, slot = (q == 1) | (q == 2), jnp.where(q == 1, 1, 0)
    else:
        local, slot = (q // 2 == 0) if section == 1 else (q // 2 == 1), 1 - c
    for m in range(2):
        rows = pl.ds(m * tok, tok)
        start_first(
            [
                (local, stash.at[0, slot, sc[1 + m], :, cols], pick.at[rows]),
                (jnp.logical_not(local), held.at[rows], pick.at[rows]),
            ],
            sems.at[3],
        )
    start_weight(section, sc, wi_own.at[0, 0, cols, :], wi_near, same, cross, True, wi_v, sems.at[1])

    if first:
        for k in range(4):
            @pl.when(q == k)
            def _(k=k):
                lat_v[...] = msgs[k][...]

        (m0, m1), (v0, v1), _ = unpack_rows(lat_v[tokens:])
        both = jnp.concatenate([columns([m0, v0]), columns([m1, v1])], axis=0)
        latent = lat_v[:tokens].astype(F32)
        mean, inv = both[:, 0:1], both[:, 1:2]
        colsum_out[...] = jnp.zeros(colsum_out.shape, F32)
    else:
        latent, mean, inv, colsum = join_latent([m[...] for m in msgs], tokens, quarter)
        colsum_out[...] = jnp.broadcast_to(colsum, colsum_out.shape)
    latf[...] = latent
    invb[...] = jnp.broadcast_to(inv, invb.shape)
    mc[...] = jnp.broadcast_to(mean, mc.shape)
    wait_for(wo_v, sems.at[0])
    up[...] = dot_nn(latent.astype(BF), wo_v[...])
    wait_for(e_v, sems.at[4])
    factors(e_v, q, factor)
    if first:
        wait_for(x_v, sems.at[2])
        src = x_v
    else:
        src = h_in
    wait_for(pick, sems.at[3])

    @pl.loop(0, tokens // ROWS, unroll=4)
    def _(i):
        rows = pl.ds(pl.multiple_of(i * ROWS, ROWS), ROWS)
        mean_t, inv_t = mc[rows, :], invb[rows, :]
        fac = factor[rows, :]
        kept = []
        for b in range(quarter // LANES):
            lanes = slice(b * LANES, (b + 1) * LANES)
            h = src[rows, lanes].astype(F32)
            normed[rows, lanes] = ((h - mean_t) * inv_t).astype(BF)
            stored = pick[rows, lanes].astype(F32)
            f = fac[:, b : b + 1]
            d = jnp.clip(h + up[rows, lanes] - stored, f * -8.0, f * 7.0).astype(BF)
            h = stored + d.astype(F32)
            h_out[rows, lanes] = h
            kept.append(h)
        st[rows, :] = sum_blocks(lambda b: kept[b], quarter // LANES)

    mean_d = jnp.sum(st[...], axis=1, keepdims=True) * (1.0 / quarter)
    mc[...] = jnp.broadcast_to(mean_d, mc.shape)

    @pl.loop(0, tokens // ROWS, unroll=4)
    def _(i):
        rows = pl.ds(pl.multiple_of(i * ROWS, ROWS), ROWS)
        mean_t = mc[rows, :]
        kept = [h_out[rows, b * LANES : (b + 1) * LANES] - mean_t for b in range(quarter // LANES)]
        for b in range(quarter // LANES):
            cen[rows, b * LANES : (b + 1) * LANES] = kept[b].astype(BF)
        st[rows, :] = sum_blocks(lambda b: kept[b] * kept[b], quarter // LANES)

    var_d = jnp.sum(st[...], axis=1, keepdims=True) * (1.0 / quarter)
    st[...] = jnp.where(lane_iota(tokens) == 0, mc[...], var_d)

    wait_for(wi_v, sems.at[1])
    w = wi_v[...]
    msg[:tokens] = dot_nn(cen[...], w).astype(BF)
    colsum = dot_nn(jnp.ones((16, quarter), BF), w)[0:1]
    t0, t1 = st[:LANES].T, st[LANES:].T
    msg[tokens:] = pack_rows((t0[0:1], t0[1:2]), (t1[0:1], t1[1:2]), colsum)


def backward_body(section, sc, *refs):
    top = section == 3
    refs = list(refs)
    take = refs.pop
    msgs = [take(0) for _ in range(4)]
    if top:
        lat_msgs = [take(0) for _ in range(4)]
        h_in = take(0)
    else:
        normed_in, latf, invb, colsum_in = [take(0) for _ in range(4)]
    g_in = take(0)
    exps = take(0)
    wi_own, wo_own, wi_near, wo_near = [take(0) for _ in range(4)]
    same, cross = [take(0) for _ in range(2)], [take(0) for _ in range(2)]
    g_out, msg, glat_out = [take(0) for _ in range(3)]
    if top:
        normed, latf, g_v = [take(0) for _ in range(3)]
    gn, wo_v, wi_v, mc, inv_v, a_v, b_v, e_v, factor, sems = [take(0) for _ in range(10)]
    q = sc[0]
    tokens, quarter = gn.shape
    tok = tokens // 2
    width = 4 * quarter
    cols = pl.ds(pl.multiple_of(q * quarter, quarter), quarter)
    start_weight(section, sc, wi_own.at[0, 0, cols, :], wi_near, same, cross, True, wi_v, sems.at[0])
    for m in range(2):
        pltpu.make_async_copy(exps.at[section, m], e_v.at[pl.ds(m * exps.shape[2], exps.shape[2])], sems.at[3]).start()
    start_weight(section - 1, sc, wo_own.at[0, 0, :, cols], wo_near, same, cross, False, wo_v, sems.at[1])
    if top:
        for m in range(2):
            pltpu.make_async_copy(g_in.at[m, :, cols], g_v.at[pl.ds(m * tok, tok)], sems.at[2]).start()
        latent, mean, inv, colsum = join_latent([m[...] for m in lat_msgs], tokens, quarter)
        latf[...] = latent
        mc[...] = jnp.broadcast_to(mean, mc.shape)
        inv_v[...] = jnp.broadcast_to(inv, inv_v.shape)
        for k in range(4):
            @pl.when(q ^ 3 == k)
            def _(k=k):
                glat_out[...] = msgs[k][:tokens]

        glat = glat_out[...]
        src, norm, inv_ref = g_v, normed, inv_v
    else:
        latent, colsum = latf[...], colsum_in[0:1]
        glat = msgs[0][:tokens].astype(F32)
        for m in msgs[1:]:
            glat = glat + m[:tokens].astype(F32)
        glat = glat.astype(BF)
        glat_out[...] = glat
        src, norm, inv_ref = g_in, normed_in, invb
    wide = glat.astype(F32)
    a_v[...] = jnp.broadcast_to(jnp.sum(wide * colsum, axis=1, keepdims=True) * (1.0 / width), a_v.shape)
    b_v[...] = jnp.broadcast_to(jnp.sum(wide * latent, axis=1, keepdims=True) * (1.0 / width), b_v.shape)
    wait_for(wi_v, sems.at[0])
    gn[...] = dot_nt(glat, wi_v[...])
    wait_for(e_v, sems.at[3])
    factors(e_v, q, factor)
    if top:
        wait_for(g_v, sems.at[2])

    @pl.loop(0, tokens // ROWS, unroll=4)
    def _(i):
        rows = pl.ds(pl.multiple_of(i * ROWS, ROWS), ROWS)
        fac = factor[rows, :]
        inv_t, a_t, b_t = inv_ref[rows, :], a_v[rows, :], b_v[rows, :]
        for b in range(quarter // LANES):
            lanes = slice(b * LANES, (b + 1) * LANES)
            if top:
                n = (h_in[rows, lanes] - mc[rows, :]) * inv_t
                normed[rows, lanes] = n.astype(BF)
            else:
                n = norm[rows, lanes].astype(F32)
            f = fac[:, b : b + 1]
            g = src[rows, lanes].astype(F32) + inv_t * (gn[rows, lanes] - a_t - n * b_t)
            g_out[rows, lanes] = jnp.clip(g, f * -128.0, f * 127.0).astype(BF)

    wait_for(wo_v, sems.at[1])
    msg[...] = dot_nt(g_out[...], wo_v[...]).astype(BF)


def grads_body(normed, latf, g_ref, glat, gin, gout):
    gin[...] = dot_tn(normed[...], glat[...]).astype(BF)
    gout[...] = dot_tn(latf[...].astype(BF), g_ref[...]).astype(BF)


def grads_top_body(sc, normed, latf, g_ref, glat, gin, gout, g_v, sems):
    quarter = g_v.shape[1]
    tok = g_v.shape[0] // 2
    cols = pl.ds(pl.multiple_of(sc[0] * quarter, quarter), quarter)
    for m in range(2):
        pltpu.make_async_copy(g_ref.at[m, :, cols], g_v.at[pl.ds(m * tok, tok)], sems.at[0]).start()
    gin[...] = dot_tn(normed[...], glat[...]).astype(BF)
    wait_for(g_v, sems.at[0])
    gout[...] = dot_tn(latf[...].astype(BF), g_v[...]).astype(BF)


def grads_first_body(sc, *refs):
    refs = list(refs)
    take = refs.pop
    msgs = [take(0) for _ in range(4)]
    normed, latf, g_ref = [take(0) for _ in range(3)]
    gins = [None] + [take(0) for _ in range(3)]
    gouts = [None] + [take(0) for _ in range(3)]
    a, b = [take(0) for _ in range(5)], [take(0) for _ in range(5)]
    gin0, gout0 = take(0), take(0)
    gins[0], gouts[0] = gin0, gout0
    x, y = sc[3], sc[5]
    glat = msgs[0][...].astype(F32)
    for m in msgs[1:]:
        glat = glat + m[...].astype(F32)
    gin0[...] = dot_tn(normed[...], glat.astype(BF)).astype(BF)
    gout0[...] = dot_tn(latf[...].astype(BF), g_ref[...]).astype(BF)
    rows, low = a[0].shape[1], b[0].shape[1]
    for k in range(4):
        at = pl.ds(pl.multiple_of(((x + k) % 4) * rows, rows), rows)
        to = pl.ds(pl.multiple_of(((y + k) % 4) * low, low), low)
        for s in range(4):
            d, i = (2 + s // 2, s % 2) if k == 2 else ((0, 1, 2, 4)[k], s)
            a[d][i] = gins[s][at, :]
            b[d][i] = gouts[s][to, :]


def relay_body(a1, a3, a_lo, a_hi, b1, b3, b_lo, b_hi, a1_out, a3_out, b1_out, b3_out):
    for src, extra, at, dst in (
        (a1, a_lo, 0, a1_out),
        (a3, a_hi, 2, a3_out),
        (b1, b_lo, 0, b1_out),
        (b3, b_hi, 2, b3_out),
    ):
        for s in range(4):
            if at <= s < at + 2:
                dst[s] = total_of([src[s], extra[s - at]])
            else:
                dst[s] = src[s]


def total_of(parts):
    total = parts[0].astype(F32)
    for part in parts[1:]:
        total = total + part.astype(F32)
    return total.astype(BF)


def second_body(sc, a0, a1, a2, b0, b1, b2, c0, c1, c2, c3, d0, d1, d2, d3, a_v, b_v):
    x, y = sc[3], sc[5]
    for s in range(4):
        a_v[s] = total_of([r[s] for r in (a0, a1, a2)])
        b_v[s] = total_of([r[s] for r in (b0, b1, b2)])
    rows, cols = c0.shape[1], d0.shape[2]
    for k, (c, d) in enumerate(((c0, d0), (c1, d1), (c2, d2), (c3, d3))):
        at = pl.ds(pl.multiple_of(((y + k) % 4) * rows, rows), rows)
        to = pl.ds(pl.multiple_of(((x + k) % 4) * cols, cols), cols)
        for s in range(4):
            c[s] = a_v[s, at, :]
            d[s] = b_v[s, :, to]


def third_body(a0, a1, a2, a3, b0, b1, b2, b3, out):
    rows, low = a0.shape[1], b0.shape[1]
    for s in range(4):
        out[s, :rows] = total_of([r[s] for r in (a0, a1, a2, a3)])
        total = total_of([r[s] for r in (b0, b1, b2, b3)])
        for t in range(total.shape[1] // LANES):
            out[s, rows + t * low : rows + (t + 1) * low] = total[:, t * LANES : (t + 1) * LANES]


def rep_of(x, z, y):
    return x * 8 + z * 4 + y


EVERY = [(x, z, y) for x in range(4) for z in range(2) for y in range(4)]


def along_x(value, k):
    return lax.ppermute(value, "rep", [(rep_of(x, z, y), rep_of((x + k) % 4, z, y)) for x, z, y in EVERY])


def along_y(value, k):
    return lax.ppermute(value, "rep", [(rep_of(x, z, y), rep_of(x, z, (y + k) % 4)) for x, z, y in EVERY])


def along_z(value, k):
    return lax.ppermute(value, "rep", [(rep_of(x, z, y), rep_of(x, (z + k) % 2, y)) for x, z, y in EVERY])


def gather(value, count, move):
    return [value] + [move(value, k) for k in range(1, count)]


def gather_relayed(value, move):
    before, after = move(value, 1), move(value, 3)
    half = value.shape[0] // 2
    return [value, before, move(before[:half], 1), move(after[half:], 3), after]


def place_body(sc, a0, a1, a2, a3, a4, b0, b1, b2, b3, b4, gin, gout):
    q, x, y = sc[0], sc[3], sc[5]
    quarter = gin.shape[2] // 4
    rows, low = quarter // 16, gout.shape[2] // 4
    for back, first, a_ref, b_ref in ((0, 0, a0, b0), (1, 0, a1, b1), (2, 0, a2, b2), (2, 2, a3, b3), (3, 0, a4, b4)):
        for i in range(a_ref.shape[0]):
            j = first + i
            for d in range(4):
                base = (q ^ d) * quarter
                row = base + ((x - back + 4) % 4) * (quarter // 4) + ((y - j + 4) % 4) * rows
                gin[0, 0, pl.ds(pl.multiple_of(row, rows), rows), :] = a_ref[i, d]
                at = pl.ds(pl.multiple_of(((y - back + 4) % 4) * low, low), low)
                for t in range(quarter // 4 // LANES):
                    col = base + ((x - j + 4) % 4) * (quarter // 4) + t * LANES
                    gout[0, 0, at, pl.ds(pl.multiple_of(col, LANES), LANES)] = b_ref[i, d, t * low : (t + 1) * low, :]


def on_device(micro, grads, stash, sample_ids, fwd_exps, bwd_exps, w_in, w_out):
    q = lax.axis_index("section")
    tok, width = micro.shape[1], micro.shape[2]
    tokens, quarter, rank = 2 * tok, width // 4, w_in.shape[3]
    fwd_exps, bwd_exps = jnp.swapaxes(fwd_exps, 2, 3), jnp.swapaxes(bwd_exps, 2, 3)
    sc = sample_ids

    def swap(value, k, sources=range(4)):
        return lax.ppermute(value, "section", [(s, s ^ k) for s in sources])

    def exchange(value):
        return [value] + [swap(value, k) for k in (1, 2, 3)]

    def beside(value):
        pairs = [(s * 32 + rep_of(xx, zz, yy), (s ^ 2) * 32 + rep_of(xx, 1 - zz, yy)) for s in range(4) for xx, zz, yy in EVERY]
        return lax.ppermute(value, ("section", "rep"), pairs)

    def beside_along(value, dx, dy, core):
        pairs = [(s * 32 + rep_of(xx, zz, yy), (s ^ core) * 32 + rep_of(xx ^ dx, zz, yy ^ dy)) for s in range(4) for xx, zz, yy in EVERY]
        return lax.ppermute(value, ("section", "rep"), pairs)

    dma = pltpu.SemaphoreType.DMA
    big = (tokens, quarter)
    qi, qo = (quarter, rank), (rank, quarter)
    far, mid, sib_in, sib_out, over = call(
        send_body,
        [(big, BF, VMEM)] * 2 + [(qi, BF, VMEM), (qo, BF, VMEM), (qi, BF, VMEM)],
        [dma((14,))],
        [(sc, SMEM), (stash, HBM), (w_in, HBM), (w_out, HBM)],
    )
    over = beside(over)
    (msg0,) = call(
        first_body,
        [((tokens + 16, rank), BF, VMEM)],
        [
            pltpu.VMEM((tokens, width), BF),
            pltpu.VMEM((width, rank), BF),
            pltpu.VMEM((rank, width), BF),
            pltpu.VMEM((tokens, width), BF),
            pltpu.VMEM((tokens, LANES), F32),
            dma((3,)),
        ],
        [(sc, SMEM), (micro, HBM), (grads, HBM), (w_in, HBM), (w_out, HBM)],
        vmem=16,
        nbytes=3 * 10**7,
    )
    msg0, far = lax.optimization_barrier((msg0, far))
    far = swap(far, 2)
    over, msg0, sib_in, sib_out, mid = lax.optimization_barrier((over, msg0, sib_in, sib_out, mid))
    half = quarter // 2
    same, cross = over[:half], over[half:]
    same = jnp.concatenate([same, beside_along(same, 1, 0, 0)], 0)
    cross = jnp.concatenate([swap(cross, 1), beside_along(cross, 0, 1, 1)], 0)
    same, cross, sib_in, sib_out = lax.optimization_barrier((same, cross, sib_in, sib_out))
    pieces = [same, beside_along(same, 0, 1, 0), cross, beside_along(cross, 1, 0, 0)]
    near = [swap(sib_in, 1), swap(sib_out, 1)]
    near, msg0 = lax.optimization_barrier((near, msg0))
    msgs0 = [swap(msg0, k, (0, 3)) for k in (1, 2, 3)]
    pieces, far, near, mid, msgs0 = lax.optimization_barrier((pieces, far, near, mid, msgs0))
    msgs0 = [msg0] + msgs0
    mid = swap(mid, 1, (1, 2))
    weights = [w_in, w_out] + near + pieces
    weights = list(zip(weights, [HBM, HBM] + [ANY] * 6))

    msgs = msgs0
    h = micro
    kept = []
    for section in (1, 2, 3):
        h, normed, msg, latf, invb, colsum = call(
            functools.partial(forward_body, section),
            [
                (big, F32, VMEM),
                (big, BF, VMEM),
                ((tokens + 16, rank), BF, VMEM),
                ((tokens, rank), F32, VMEM),
                ((tokens, LANES), F32, VMEM),
                ((8, LANES), F32, VMEM),
            ],
            [
                pltpu.VMEM(big, BF),
                pltpu.VMEM(big, BF),
                pltpu.VMEM(big, F32),
                pltpu.VMEM(big, BF),
                pltpu.VMEM(qo, BF),
                pltpu.VMEM(qi, BF),
                pltpu.VMEM((tokens, LANES), F32),
                pltpu.VMEM((tokens, LANES), F32),
                pltpu.VMEM((tokens + 16, rank), BF),
                pltpu.VMEM((2 * fwd_exps.shape[2], tok), jnp.int32),
                pltpu.VMEM((tokens, LANES), F32),
                dma((5,)),
            ],
            [(sc, SMEM)]
            + [(m, VMEM) for m in msgs]
            + [(h, HBM if section == 1 else VMEM), (fwd_exps, HBM), (stash, HBM)]
            + [(mid if section == 2 else far, ANY)]
            + weights,
        )
        kept.append((normed, latf, invb, colsum))
        msgs = exchange(msg)

    gins, gouts = [None] * 4, [None] * 4
    g = grads
    for section in (3, 2, 1):
        top = section == 3
        outs = [(big, BF, VMEM), ((tokens, rank), BF, VMEM), ((tokens, rank), BF, VMEM)]
        scratch = [
            pltpu.VMEM(big, F32),
            pltpu.VMEM(qo, BF),
            pltpu.VMEM(qi, BF),
            pltpu.VMEM((tokens, LANES), F32),
            pltpu.VMEM((tokens, LANES), F32),
            pltpu.VMEM((tokens, LANES), F32),
            pltpu.VMEM((tokens, LANES), F32),
            pltpu.VMEM((2 * bwd_exps.shape[2], tok), jnp.int32),
            pltpu.VMEM((tokens, LANES), F32),
            dma((4,)),
        ]
        if top:
            outs += [(big, BF, VMEM), ((tokens, rank), F32, VMEM)]
            scratch = [pltpu.VMEM(big, BF)] + scratch
            ins = [(m, VMEM) for m in msgs0] + [(m, VMEM) for m in msgs] + [(h, VMEM), (g, HBM)]
        else:
            ins = [(m, VMEM) for m in msgs] + [(v, VMEM) for v in kept[section]] + [(g, VMEM)]
        result = call(
            functools.partial(backward_body, section),
            outs,
            scratch,
            [(sc, SMEM)] + ins + [(bwd_exps, HBM)] + weights,
        )
        next_g, msg, glat = result[:3]
        if top:
            normed, latf = result[3:]
            gin, gout = call(
                grads_top_body,
                [(qi, BF, VMEM), (qo, BF, VMEM)],
                [pltpu.VMEM(big, BF), dma((1,))],
                [(sc, SMEM), (normed, VMEM), (latf, VMEM), (g, HBM), (glat, VMEM)],
            )
        else:
            normed, latf = kept[section][:2]
            gin, gout = call(
                grads_body,
                [(qi, BF, VMEM), (qo, BF, VMEM)],
                [],
                [(normed, VMEM), (latf, VMEM), (g, VMEM), (glat, VMEM)],
            )
        msgs = exchange(msg)
        gins[section], gouts[section] = gin, gout
        g = next_g
    rows, low = quarter // 4, rank // 4
    cut = call(
        grads_first_body,
        [((n, rows, rank), BF, VMEM) for n in (4, 4, 2, 2, 4)] + [((n, low, quarter), BF, VMEM) for n in (4, 4, 2, 2, 4)],
        [pltpu.VMEM(qi, BF), pltpu.VMEM(qo, BF)],
        [(sc, SMEM)]
        + [(m, VMEM) for m in msgs]
        + [(kept[0][0], VMEM), (kept[0][1], VMEM), (g, VMEM)]
        + [(v, VMEM) for v in gins[1:] + gouts[1:]],
    )
    a, b = cut[:5], cut[5:]
    far_a, far_b = (along_x(a[2], 1), along_x(a[3], 3)), (along_y(b[2], 1), along_y(b[3], 3))
    to_a, back_a, to_b, back_b = call(
        relay_body,
        [((4, rows, rank), BF, VMEM)] * 2 + [((4, low, quarter), BF, VMEM)] * 2,
        [],
        [(v, VMEM) for v in (a[1], a[4], *far_a, b[1], b[4], *far_b)],
    )
    a = [a[0], along_x(to_a, 1), along_x(back_a, 3)]
    b = [b[0], along_y(to_b, 1), along_y(back_b, 3)]
    cut = call(
        second_body,
        [((4, rows // 4, rank), BF, VMEM)] * 4 + [((4, low, rows), BF, VMEM)] * 4,
        [pltpu.VMEM((4, rows, rank), BF), pltpu.VMEM((4, low, quarter), BF)],
        [(sc, SMEM)] + [(v, VMEM) for v in a + b],
    )
    a = [cut[0]] + [along_y(cut[k], k) for k in (1, 2, 3)]
    b = [cut[4]] + [along_x(cut[4 + k], k) for k in (1, 2, 3)]
    (both,) = call(
        third_body,
        [((4, rows // 2, rank), BF, VMEM)],
        [],
        [(v, VMEM) for v in a + b],
    )
    shares = (both.astype(F32) + along_z(both, 1).astype(F32)).astype(BF)
    own = [lax.dynamic_index_in_dim(shares, q ^ k, 0, keepdims=False) for k in range(4)]
    mine = jnp.stack([own[0]] + [swap(own[k], k) for k in (1, 2, 3)])
    a, b = mine[:, : rows // 4], mine[:, rows // 4 :]
    a, b = gather(a, 4, along_y), gather(b, 4, along_x)
    a, b = lax.optimization_barrier((jnp.stack(a), jnp.stack(b)))
    a, b = gather_relayed(a, along_x), gather_relayed(b, along_y)
    total_in, total_out = call(
        place_body,
        [((1, 1, width, rank), BF, VMEM), ((1, 1, rank, width), BF, VMEM)],
        [],
        [(sc, SMEM)] + [(v, VMEM) for v in a + b],
    )
    return total_in, total_out


def solution(mesh):
    placed = (
        P(None, "rep", None),
        P(None, "rep", None),
        P("section", None, None, "rep", None),
        P(None, "rep"),
        P(None, None, "rep", None),
        P(None, None, "rep", None),
        P("section", None, None, None),
        P("section", None, None, None),
    )
    return jax.shard_map(
        on_device,
        mesh=mesh,
        in_specs=placed,
        out_specs=(P("section", None, None, None), P("section", None, None, None)),
        check_vma=False,
    )
```

```python
import functools

import jax
import jax.numpy as jnp
from jax import lax
from jax.experimental import pallas as pl
from jax.experimental.pallas import tpu as pltpu
from jax.sharding import PartitionSpec as P

EPS = 1e-05
BF = jnp.bfloat16
F32 = jnp.float32
ROWS = 16
LANES = 128
MIB = 1024 * 1024
ANY = pl.BlockSpec(memory_space=pl.ANY)
HBM = pl.BlockSpec(memory_space=pltpu.HBM)
VMEM = pl.BlockSpec(memory_space=pltpu.VMEM)
SMEM = pl.BlockSpec(memory_space=pltpu.SMEM)


def dot_nn(a, b):
    return lax.dot_general(a, b, (((1,), (0,)), ((), ())), preferred_element_type=F32)


def dot_nt(a, b):
    return lax.dot_general(a, b, (((1,), (1,)), ((), ())), preferred_element_type=F32)


def dot_tn(a, b):
    return lax.dot_general(a, b, (((0,), (0,)), ((), ())), preferred_element_type=F32)


class Place:
    def __init__(self, ids):
        rep = lax.axis_index("rep")
        self.ids = ids
        self.at = {0: lax.axis_index("section"), 3: rep // 8, 4: rep // 4 % 2, 5: rep % 4}

    def __getitem__(self, k):
        return self.ids[k - 1, 0] if k in (1, 2) else self.at[k]


def placed(body, ids, *refs):
    body(Place(ids), *refs)


def call(body, outs, scratch, ins, flops=10**8, nbytes=4 * 10**6, vmem=12):
    return pl.pallas_call(
        functools.partial(placed, body) if ins[0][1] is SMEM else body,
        out_shape=[jax.ShapeDtypeStruct(s, d) for s, d, _ in outs],
        in_specs=[spec for _, spec in ins],
        out_specs=[spec for _, _, spec in outs],
        scratch_shapes=scratch,
        compiler_params=pltpu.CompilerParams(vmem_limit_bytes=vmem * MIB),
        cost_estimate=pl.CostEstimate(flops=flops, bytes_accessed=nbytes, transcendentals=0),
    )(*[pltpu.with_memory_space_constraint(a, pltpu.HBM) if spec is HBM else a for a, spec in ins])


def lane_iota(rows):
    return lax.broadcasted_iota(jnp.int32, (rows, LANES), 1)


def row_iota(rows):
    return lax.broadcasted_iota(jnp.int32, (rows, LANES), 0)


def three(x):
    hi = x.astype(BF).astype(F32)
    rest = x - hi
    mid = rest.astype(BF).astype(F32)
    return hi, mid, (rest - mid).astype(BF).astype(F32)


def pack_rows(first_half, second_half, extra):
    at = row_iota(16)
    out = jnp.zeros((16, LANES), F32)
    for base, (a, b) in ((0, first_half), (8, second_half)):
        for j, row in enumerate(three(a) + three(b)):
            out = jnp.where(at == base + j, row, out)
    if extra is not None:
        hi, mid, _ = three(extra)
        out = jnp.where(at == 6, hi, out)
        out = jnp.where(at == 7, mid, out)
    return out.astype(BF)


def unpack_rows(block):
    block = block.astype(F32)

    def joined(base):
        return block[base : base + 1] + block[base + 1 : base + 2] + block[base + 2 : base + 3]

    return (joined(0), joined(8)), (joined(3), joined(11)), block[6:7] + block[7:8]


def columns(rows):
    at = row_iota(LANES)
    out = jnp.zeros((LANES, LANES), F32)
    for j, row in enumerate(rows):
        out = jnp.where(at == j, row, out)
    return out.T


def join_latent(msgs, tokens, width):
    parsed = [unpack_rows(m[tokens : tokens + 16]) for m in msgs]
    total = msgs[0][:tokens].astype(F32)
    for m in msgs[1:]:
        total = total + m[:tokens].astype(F32)
    halves = []
    for half in range(2):
        means = [p[0][half] for p in parsed]
        mean = (means[0] + means[1] + means[2] + means[3]) * 0.25
        offs = [m - mean for m in means]
        var = (parsed[0][1][half] + parsed[1][1][half] + parsed[2][1][half] + parsed[3][1][half]) * 0.25
        var = var + (offs[0] * offs[0] + offs[1] * offs[1] + offs[2] * offs[2] + offs[3] * offs[3]) * 0.25
        halves.append(columns([mean, lax.rsqrt(var + EPS)] + offs))
    cols = jnp.concatenate(halves, axis=0)
    colsum = parsed[0][2]
    for d in range(4):
        total = total + cols[:, 2 + d : 3 + d] * parsed[d][2]
        if d:
            colsum = colsum + parsed[d][2]
    return total * cols[:, 1:2], cols[:, 0:1], cols[:, 1:2], colsum


def start_first(pairs, sem):
    for cond, src, dst in pairs:
        @pl.when(cond)
        def _(src=src, dst=dst):
            pltpu.make_async_copy(src, dst, sem).start()


def start_weight(section, sc, own, near, same, cross, inner, dst, sem):
    q, x, y = sc[0], sc[3], sc[5]
    zh, c = q // 2, q % 2
    here = zh == section // 2
    mine = c == section % 2
    piece = 384

    def start(src, to):
        pltpu.make_async_copy(src, to, sem).start()

    @pl.when(here & mine)
    def _():
        start(own, dst)

    @pl.when(here & jnp.logical_not(mine))
    def _():
        start(near, dst)

    def pieces(refs, first):
        for j in range(2):
            for i in range(2):
                px, py = (i, j) if first == 0 else (j, i)
                at = piece_of(x ^ px, y ^ py) * piece
                base = i * 2 * piece
                if inner:
                    start(refs[j].at[pl.ds(base, piece)], dst.at[pl.ds(pl.multiple_of(at, piece), piece)])
                else:
                    for t in range(piece // LANES):
                        cols = pl.ds(pl.multiple_of(at + t * LANES, LANES), LANES)
                        start(refs[j].at[pl.ds(base + piece + t * LANES, LANES)], dst.at[:, cols])

    @pl.when(jnp.logical_not(here) & mine)
    def _():
        pieces(same, 0)

    @pl.when(jnp.logical_not(here) & jnp.logical_not(mine))
    def _():
        pieces(cross, 1)


def piece_of(x, y):
    return (x & 1) * 2 + (y & 1)


def factors(exps, q, out):
    every = exps.shape[0] // 2
    blocks = every // 4
    for k in range(4):
        @pl.when(q == k)
        def _(k=k):
            for m in range(2):
                e = exps[m * every + k * blocks : m * every + (k + 1) * blocks, :]
                f = lax.shift_left(jnp.ones(e.shape, jnp.int32), e + 14).astype(F32) * (2.0**-14)
                full = jnp.concatenate([f, jnp.zeros((LANES - blocks, LANES), F32)], axis=0)
                out[m * LANES : (m + 1) * LANES, :] = full.T


def wait_for(dst, sem):
    pltpu.make_async_copy(dst, dst, sem).wait()


def send_body(sc, stash, w_in, w_out, far, mid, sib_in, sib_out, over, sems):
    q, x, y = sc[0], sc[3], sc[5]
    c = q % 2
    tok, quarter = far.shape[0] // 2, far.shape[1]
    piece = quarter // 4
    mid_slot = jnp.where(q == 1, 1, 0)
    copies = []

    def go(src, dst):
        copy = pltpu.make_async_copy(src, dst, sems.at[len(copies)])
        copy.start()
        copies.append(copy)

    def cols(k):
        return pl.ds(pl.multiple_of((q ^ k) * quarter, quarter), quarter)

    for k in (2, 3):
        base = (q ^ k) * quarter + piece_of(x, y) * piece
        first = (k - 2) * 2 * piece
        go(w_in.at[0, 0, pl.ds(pl.multiple_of(base, piece), piece), :], over.at[pl.ds(first, piece)])
        for t in range(piece // LANES):
            from_cols = pl.ds(pl.multiple_of(base + t * LANES, LANES), LANES)
            go(w_out.at[0, 0, :, from_cols], over.at[pl.ds(first + piece + t * LANES, LANES)])
    for m in range(2):
        go(stash.at[0, 1 - c, sc[1 + m], :, cols(2)], far.at[pl.ds(m * tok, tok)])
    go(w_out.at[0, 0, :, cols(1)], sib_out)
    go(w_in.at[0, 0, cols(1), :], sib_in)
    for m in range(2):
        go(stash.at[0, mid_slot, sc[1 + m], :, cols(1)], mid.at[pl.ds(m * tok, tok)])
    for copy in copies:
        copy.wait()


def sum_blocks(block, count):
    parts = []
    for b in range(count):
        v = block(b)
        if b < 4:
            parts.append(v)
        else:
            parts[b % 4] = parts[b % 4] + v
    return (parts[0] + parts[1]) + (parts[2] + parts[3])


def first_body(sc, micro, grads, w_in, w_out, msg, x_v, w_v, wo_v, n_v, st, sems):
    q = sc[0]
    tokens, width = x_v.shape
    tok = tokens // 2
    blocks = width // LANES

    def load(src, wsrc, wdst):
        copies = [pltpu.make_async_copy(src.at[m], x_v.at[pl.ds(m * tok, tok)], sems.at[m]) for m in range(2)]
        copies.append(pltpu.make_async_copy(wsrc.at[0, 0], wdst, sems.at[2]))
        for copy in copies:
            copy.start()
        return copies

    @pl.when(q == 0)
    def _():
        load(micro, w_in, w_v)

    @pl.when(q == 3)
    def _():
        load(grads, w_out, wo_v)

    @pl.when((q == 1) | (q == 2))
    def _():
        msg[...] = jnp.zeros(msg.shape, BF)

    @pl.when(q == 0)
    def _():
        for m in range(2):
            wait_for(x_v.at[pl.ds(m * tok, tok)], sems.at[m])

            @pl.loop(m * (tok // ROWS), (m + 1) * (tok // ROWS), unroll=2)
            def _(i):
                rows = pl.ds(pl.multiple_of(i * ROWS, ROWS), ROWS)

                def block(b):
                    return x_v[rows, b * LANES : (b + 1) * LANES].astype(F32)

                def square(b):
                    d = block(b) - mean
                    return d * d

                mean = jnp.sum(sum_blocks(block, blocks), axis=1, keepdims=True) * (1.0 / width)
                mean = jnp.broadcast_to(mean, (ROWS, LANES))
                inv = lax.rsqrt(jnp.sum(sum_blocks(square, blocks), axis=1, keepdims=True) * (1.0 / width) + EPS)
                inv = jnp.broadcast_to(inv, (ROWS, LANES))
                for b in range(blocks):
                    n_v[rows, b * LANES : (b + 1) * LANES] = ((block(b) - mean) * inv).astype(BF)
                st[rows, :] = jnp.where(lane_iota(ROWS) == 0, mean, inv)

        wait_for(w_v, sems.at[2])
        latent = dot_nn(n_v[...], w_v[...])
        msg[:tokens] = latent.astype(BF)
        t0, t1 = st[:LANES].T, st[LANES:].T
        msg[tokens:] = pack_rows((t0[0:1], t0[1:2]), (t1[0:1], t1[1:2]), None)

    @pl.when(q == 3)
    def _():
        for m in range(2):
            wait_for(x_v.at[pl.ds(m * tok, tok)], sems.at[m])
        wait_for(wo_v, sems.at[2])
        msg[:tokens] = dot_nt(x_v[...], wo_v[...]).astype(BF)
        msg[tokens:] = jnp.zeros((msg.shape[0] - tokens, msg.shape[1]), BF)


def forward_body(section, sc, *refs):
    first = section == 1
    refs = list(refs)
    take = refs.pop
    msgs = [take(0) for _ in range(4)]
    h_in = take(0)
    exps = take(0)
    stash, held = take(0), take(0)
    wi_own, wo_own, wi_near, wo_near = [take(0) for _ in range(4)]
    same, cross = [take(0) for _ in range(2)], [take(0) for _ in range(2)]
    h_out, normed, msg, latf, invb, colsum_out, wo_v, wi_v = [take(0) for _ in range(8)]
    x_v, pick, up, cen, st, mc = [take(0) for _ in range(6)]
    lat_v, e_v, factor, sems = [take(0) for _ in range(4)]
    q = sc[0]
    c = q % 2
    tokens, quarter = pick.shape
    tok = tokens // 2
    cols = pl.ds(pl.multiple_of(q * quarter, quarter), quarter)
    start_weight(section - 1, sc, wo_own.at[0, 0, :, cols], wo_near, same, cross, False, wo_v, sems.at[0])
    for m in range(2):
        pltpu.make_async_copy(exps.at[section - 1, m], e_v.at[pl.ds(m * exps.shape[2], exps.shape[2])], sems.at[4]).start()
    if first:
        for m in range(2):
            pltpu.make_async_copy(h_in.at[m, :, cols], x_v.at[pl.ds(m * tok, tok)], sems.at[2]).start()
    if section == 2:
        local, slot = (q == 1) | (q == 2), jnp.where(q == 1, 1, 0)
    else:
        local, slot = (q // 2 == 0) if section == 1 else (q // 2 == 1), 1 - c
    for m in range(2):
        rows = pl.ds(m * tok, tok)
        start_first(
            [
                (local, stash.at[0, slot, sc[1 + m], :, cols], pick.at[rows]),
                (jnp.logical_not(local), held.at[rows], pick.at[rows]),
            ],
            sems.at[3],
        )
    start_weight(section, sc, wi_own.at[0, 0, cols, :], wi_near, same, cross, True, wi_v, sems.at[1])

    if first:
        for k in range(4):
            @pl.when(q == k)
            def _(k=k):
                lat_v[...] = msgs[k][...]

        (m0, m1), (v0, v1), _ = unpack_rows(lat_v[tokens:])
        both = jnp.concatenate([columns([m0, v0]), columns([m1, v1])], axis=0)
        latent = lat_v[:tokens].astype(F32)
        mean, inv = both[:, 0:1], both[:, 1:2]
        colsum_out[...] = jnp.zeros(colsum_out.shape, F32)
    else:
        latent, mean, inv, colsum = join_latent([m[...] for m in msgs], tokens, quarter)
        colsum_out[...] = jnp.broadcast_to(colsum, colsum_out.shape)
    latf[...] = latent
    invb[...] = jnp.broadcast_to(inv, invb.shape)
    mc[...] = jnp.broadcast_to(mean, mc.shape)
    wait_for(wo_v, sems.at[0])
    up[...] = dot_nn(latent.astype(BF), wo_v[...])
    wait_for(e_v, sems.at[4])
    factors(e_v, q, factor)
    if first:
        wait_for(x_v, sems.at[2])
        src = x_v
    else:
        src = h_in
    wait_for(pick, sems.at[3])

    @pl.loop(0, tokens // ROWS, unroll=4)
    def _(i):
        rows = pl.ds(pl.multiple_of(i * ROWS, ROWS), ROWS)
        mean_t, inv_t = mc[rows, :], invb[rows, :]
        fac = factor[rows, :]
        kept = []
        for b in range(quarter // LANES):
            lanes = slice(b * LANES, (b + 1) * LANES)
            h = src[rows, lanes].astype(F32)
            normed[rows, lanes] = ((h - mean_t) * inv_t).astype(BF)
            stored = pick[rows, lanes].astype(F32)
            f = fac[:, b : b + 1]
            d = jnp.clip(h + up[rows, lanes] - stored, f * -8.0, f * 7.0).astype(BF)
            h = stored + d.astype(F32)
            h_out[rows, lanes] = h
            kept.append(h)
        st[rows, :] = sum_blocks(lambda b: kept[b], quarter // LANES)

    mean_d = jnp.sum(st[...], axis=1, keepdims=True) * (1.0 / quarter)
    mc[...] = jnp.broadcast_to(mean_d, mc.shape)

    @pl.loop(0, tokens // ROWS, unroll=4)
    def _(i):
        rows = pl.ds(pl.multiple_of(i * ROWS, ROWS), ROWS)
        mean_t = mc[rows, :]
        kept = [h_out[rows, b * LANES : (b + 1) * LANES] - mean_t for b in range(quarter // LANES)]
        for b in range(quarter // LANES):
            cen[rows, b * LANES : (b + 1) * LANES] = kept[b].astype(BF)
        st[rows, :] = sum_blocks(lambda b: kept[b] * kept[b], quarter // LANES)

    var_d = jnp.sum(st[...], axis=1, keepdims=True) * (1.0 / quarter)
    st[...] = jnp.where(lane_iota(tokens) == 0, mc[...], var_d)

    wait_for(wi_v, sems.at[1])
    w = wi_v[...]
    msg[:tokens] = dot_nn(cen[...], w).astype(BF)
    colsum = dot_nn(jnp.ones((16, quarter), BF), w)[0:1]
    t0, t1 = st[:LANES].T, st[LANES:].T
    msg[tokens:] = pack_rows((t0[0:1], t0[1:2]), (t1[0:1], t1[1:2]), colsum)


def backward_body(section, sc, *refs):
    top = section == 3
    refs = list(refs)
    take = refs.pop
    msgs = [take(0) for _ in range(4)]
    if top:
        lat_msgs = [take(0) for _ in range(4)]
        h_in = take(0)
    else:
        normed_in, latf, invb, colsum_in = [take(0) for _ in range(4)]
    g_in = take(0)
    exps, wo_v, wi_v = [take(0) for _ in range(3)]
    g_out, msg, glat_out = [take(0) for _ in range(3)]
    if top:
        normed, latf, g_v = [take(0) for _ in range(3)]
    gn, mc, inv_v, a_v, b_v, e_v, factor, sems = [take(0) for _ in range(8)]
    q = sc[0]
    tokens, quarter = gn.shape
    tok = tokens // 2
    width = 4 * quarter
    cols = pl.ds(pl.multiple_of(q * quarter, quarter), quarter)
    for m in range(2):
        pltpu.make_async_copy(exps.at[section, m], e_v.at[pl.ds(m * exps.shape[2], exps.shape[2])], sems.at[1]).start()
    if top:
        for m in range(2):
            pltpu.make_async_copy(g_in.at[m, :, cols], g_v.at[pl.ds(m * tok, tok)], sems.at[0]).start()
        latent, mean, inv, colsum = join_latent([m[...] for m in lat_msgs], tokens, quarter)
        latf[...] = latent
        mc[...] = jnp.broadcast_to(mean, mc.shape)
        inv_v[...] = jnp.broadcast_to(inv, inv_v.shape)
        for k in range(4):
            @pl.when(q ^ 3 == k)
            def _(k=k):
                glat_out[...] = msgs[k][:tokens]

        glat = glat_out[...]
        src, norm, inv_ref = g_v, normed, inv_v
    else:
        latent, colsum = latf[...], colsum_in[0:1]
        glat = msgs[0][:tokens].astype(F32)
        for m in msgs[1:]:
            glat = glat + m[:tokens].astype(F32)
        glat = glat.astype(BF)
        glat_out[...] = glat
        src, norm, inv_ref = g_in, normed_in, invb
    wide = glat.astype(F32)
    a_v[...] = jnp.broadcast_to(jnp.sum(wide * colsum, axis=1, keepdims=True) * (1.0 / width), a_v.shape)
    b_v[...] = jnp.broadcast_to(jnp.sum(wide * latent, axis=1, keepdims=True) * (1.0 / width), b_v.shape)
    gn[...] = dot_nt(glat, wi_v[...])
    wait_for(e_v, sems.at[1])
    factors(e_v, q, factor)
    if top:
        wait_for(g_v, sems.at[0])

    @pl.loop(0, tokens // ROWS, unroll=4)
    def _(i):
        rows = pl.ds(pl.multiple_of(i * ROWS, ROWS), ROWS)
        fac = factor[rows, :]
        inv_t, a_t, b_t = inv_ref[rows, :], a_v[rows, :], b_v[rows, :]
        for b in range(quarter // LANES):
            lanes = slice(b * LANES, (b + 1) * LANES)
            if top:
                n = (h_in[rows, lanes] - mc[rows, :]) * inv_t
                normed[rows, lanes] = n.astype(BF)
            else:
                n = norm[rows, lanes].astype(F32)
            f = fac[:, b : b + 1]
            g = src[rows, lanes].astype(F32) + inv_t * (gn[rows, lanes] - a_t - n * b_t)
            g_out[rows, lanes] = jnp.clip(g, f * -128.0, f * 127.0).astype(BF)

    msg[...] = dot_nt(g_out[...], wo_v[...]).astype(BF)


def grads_body(normed, latf, g_ref, glat, gin, gout):
    gin[...] = dot_tn(normed[...], glat[...]).astype(BF)
    gout[...] = dot_tn(latf[...].astype(BF), g_ref[...]).astype(BF)


def grads_top_body(sc, normed, latf, g_ref, glat, gin, gout, g_v, sems):
    quarter = g_v.shape[1]
    tok = g_v.shape[0] // 2
    cols = pl.ds(pl.multiple_of(sc[0] * quarter, quarter), quarter)
    for m in range(2):
        pltpu.make_async_copy(g_ref.at[m, :, cols], g_v.at[pl.ds(m * tok, tok)], sems.at[0]).start()
    gin[...] = dot_tn(normed[...], glat[...]).astype(BF)
    wait_for(g_v, sems.at[0])
    gout[...] = dot_tn(latf[...].astype(BF), g_v[...]).astype(BF)


def grads_first_body(sc, *refs):
    refs = list(refs)
    take = refs.pop
    msgs = [take(0) for _ in range(4)]
    normed, latf, g_ref = [take(0) for _ in range(3)]
    gins = [None] + [take(0) for _ in range(3)]
    gouts = [None] + [take(0) for _ in range(3)]
    a, b = [take(0) for _ in range(5)], [take(0) for _ in range(5)]
    gin0, gout0 = take(0), take(0)
    gins[0], gouts[0] = gin0, gout0
    x, y = sc[3], sc[5]
    glat = msgs[0][...].astype(F32)
    for m in msgs[1:]:
        glat = glat + m[...].astype(F32)
    gin0[...] = dot_tn(normed[...], glat.astype(BF)).astype(BF)
    gout0[...] = dot_tn(latf[...].astype(BF), g_ref[...]).astype(BF)
    rows, low = a[0].shape[1], b[0].shape[1]
    for k in range(4):
        at = pl.ds(pl.multiple_of(((x + k) % 4) * rows, rows), rows)
        to = pl.ds(pl.multiple_of(((y + k) % 4) * low, low), low)
        for s in range(4):
            d, i = (2 + s // 2, s % 2) if k == 2 else ((0, 1, 2, 4)[k], s)
            a[d][i] = gins[s][at, :]
            b[d][i] = gouts[s][to, :]


def relay_body(a1, a3, a_lo, a_hi, b1, b3, b_lo, b_hi, a1_out, a3_out, b1_out, b3_out):
    for src, extra, at, dst in (
        (a1, a_lo, 0, a1_out),
        (a3, a_hi, 2, a3_out),
        (b1, b_lo, 0, b1_out),
        (b3, b_hi, 2, b3_out),
    ):
        for s in range(4):
            if at <= s < at + 2:
                dst[s] = total_of([src[s], extra[s - at]])
            else:
                dst[s] = src[s]


def total_of(parts):
    total = parts[0].astype(F32)
    for part in parts[1:]:
        total = total + part.astype(F32)
    return total.astype(BF)


def second_body(sc, a0, a1, a2, b0, b1, b2, c0, c1, c2, c3, d0, d1, d2, d3, a_v, b_v):
    x, y = sc[3], sc[5]
    for s in range(4):
        a_v[s] = total_of([r[s] for r in (a0, a1, a2)])
        b_v[s] = total_of([r[s] for r in (b0, b1, b2)])
    rows, cols = c0.shape[1], d0.shape[2]
    for k, (c, d) in enumerate(((c0, d0), (c1, d1), (c2, d2), (c3, d3))):
        at = pl.ds(pl.multiple_of(((y + k) % 4) * rows, rows), rows)
        to = pl.ds(pl.multiple_of(((x + k) % 4) * cols, cols), cols)
        for s in range(4):
            c[s] = a_v[s, at, :]
            d[s] = b_v[s, :, to]


def third_body(a0, a1, a2, a3, b0, b1, b2, b3, out):
    rows, low = a0.shape[1], b0.shape[1]
    for s in range(4):
        out[s, :rows] = total_of([r[s] for r in (a0, a1, a2, a3)])
        total = total_of([r[s] for r in (b0, b1, b2, b3)])
        for t in range(total.shape[1] // LANES):
            out[s, rows + t * low : rows + (t + 1) * low] = total[:, t * LANES : (t + 1) * LANES]


def rep_of(x, z, y):
    return x * 8 + z * 4 + y


EVERY = [(x, z, y) for x in range(4) for z in range(2) for y in range(4)]


def along_x(value, k):
    return lax.ppermute(value, "rep", [(rep_of(x, z, y), rep_of((x + k) % 4, z, y)) for x, z, y in EVERY])


def along_y(value, k):
    return lax.ppermute(value, "rep", [(rep_of(x, z, y), rep_of(x, z, (y + k) % 4)) for x, z, y in EVERY])


def along_z(value, k):
    return lax.ppermute(value, "rep", [(rep_of(x, z, y), rep_of(x, (z + k) % 2, y)) for x, z, y in EVERY])


def gather(value, count, move):
    return [value] + [move(value, k) for k in range(1, count)]


def gather_relayed(value, move):
    before, after = move(value, 1), move(value, 3)
    half = value.shape[0] // 2
    return [value, before, move(before[:half], 1), move(after[half:], 3), after]


def place_body(sc, a0, a1, a2, a3, a4, b0, b1, b2, b3, b4, gin, gout):
    q, x, y = sc[0], sc[3], sc[5]
    quarter = gin.shape[2] // 4
    rows, low = quarter // 16, gout.shape[2] // 4
    for back, first, a_ref, b_ref in ((0, 0, a0, b0), (1, 0, a1, b1), (2, 0, a2, b2), (2, 2, a3, b3), (3, 0, a4, b4)):
        for i in range(a_ref.shape[0]):
            j = first + i
            for d in range(4):
                base = (q ^ d) * quarter
                row = base + ((x - back + 4) % 4) * (quarter // 4) + ((y - j + 4) % 4) * rows
                gin[0, 0, pl.ds(pl.multiple_of(row, rows), rows), :] = a_ref[i, d]
                at = pl.ds(pl.multiple_of(((y - back + 4) % 4) * low, low), low)
                for t in range(quarter // 4 // LANES):
                    col = base + ((x - j + 4) % 4) * (quarter // 4) + t * LANES
                    gout[0, 0, at, pl.ds(pl.multiple_of(col, LANES), LANES)] = b_ref[i, d, t * low : (t + 1) * low, :]


def on_device(micro, grads, stash, sample_ids, fwd_exps, bwd_exps, w_in, w_out):
    q = lax.axis_index("section")
    tok, width = micro.shape[1], micro.shape[2]
    tokens, quarter, rank = 2 * tok, width // 4, w_in.shape[3]
    fwd_exps, bwd_exps = jnp.swapaxes(fwd_exps, 2, 3), jnp.swapaxes(bwd_exps, 2, 3)
    sc = sample_ids

    def swap(value, k, sources=range(4)):
        return lax.ppermute(value, "section", [(s, s ^ k) for s in sources])

    def exchange(value):
        return [value] + [swap(value, k) for k in (1, 2, 3)]

    def beside(value):
        pairs = [(s * 32 + rep_of(xx, zz, yy), (s ^ 2) * 32 + rep_of(xx, 1 - zz, yy)) for s in range(4) for xx, zz, yy in EVERY]
        return lax.ppermute(value, ("section", "rep"), pairs)

    def beside_along(value, dx, dy, core):
        pairs = [(s * 32 + rep_of(xx, zz, yy), (s ^ core) * 32 + rep_of(xx ^ dx, zz, yy ^ dy)) for s in range(4) for xx, zz, yy in EVERY]
        return lax.ppermute(value, ("section", "rep"), pairs)

    dma = pltpu.SemaphoreType.DMA
    big = (tokens, quarter)
    qi, qo = (quarter, rank), (rank, quarter)
    far, mid, sib_in, sib_out, over = call(
        send_body,
        [(big, BF, VMEM)] * 2 + [(qi, BF, VMEM), (qo, BF, VMEM), (qi, BF, VMEM)],
        [dma((14,))],
        [(sc, SMEM), (stash, HBM), (w_in, HBM), (w_out, HBM)],
    )
    over = beside(over)
    (msg0,) = call(
        first_body,
        [((tokens + 16, rank), BF, VMEM)],
        [
            pltpu.VMEM((tokens, width), BF),
            pltpu.VMEM((width, rank), BF),
            pltpu.VMEM((rank, width), BF),
            pltpu.VMEM((tokens, width), BF),
            pltpu.VMEM((tokens, LANES), F32),
            dma((3,)),
        ],
        [(sc, SMEM), (micro, HBM), (grads, HBM), (w_in, HBM), (w_out, HBM)],
        vmem=16,
        nbytes=3 * 10**7,
    )
    msg0, far = lax.optimization_barrier((msg0, far))
    far = swap(far, 2)
    near_msg = swap(msg0, 1, (0, 3))
    over, msg0, sib_in, sib_out = lax.optimization_barrier((over, msg0, sib_in, sib_out))
    half = quarter // 2
    same, cross = over[:half], over[half:]
    same = jnp.concatenate([same, beside_along(same, 1, 0, 0)], 0)
    cross = jnp.concatenate([swap(cross, 1), beside_along(cross, 0, 1, 1)], 0)
    same, cross, sib_in, sib_out = lax.optimization_barrier((same, cross, sib_in, sib_out))
    pieces = [same, beside_along(same, 0, 1, 0), cross, beside_along(cross, 1, 0, 0)]
    near = [swap(sib_in, 1), swap(sib_out, 1)]
    near, msg0 = lax.optimization_barrier((near, msg0))
    msgs0 = [near_msg] + [swap(msg0, k, (0, 3)) for k in (2, 3)]
    pieces, far, near, msgs0 = lax.optimization_barrier((pieces, far, near, msgs0))
    msgs0 = [msg0] + msgs0
    weights = [w_in, w_out] + near + pieces
    weights = list(zip(weights, [HBM, HBM] + [ANY] * 6))

    msgs = msgs0
    h = micro
    kept = []
    held = {}
    for section in (1, 2, 3):
        h, normed, msg, latf, invb, colsum, low_out, high_in = call(
            functools.partial(forward_body, section),
            [
                (big, F32, VMEM),
                (big, BF, VMEM),
                ((tokens + 16, rank), BF, VMEM),
                ((tokens, rank), F32, VMEM),
                ((tokens, LANES), F32, VMEM),
                ((8, LANES), F32, VMEM),
                (qo, BF, VMEM),
                (qi, BF, VMEM),
            ],
            [
                pltpu.VMEM(big, BF),
                pltpu.VMEM(big, BF),
                pltpu.VMEM(big, F32),
                pltpu.VMEM(big, BF),
                pltpu.VMEM((tokens, LANES), F32),
                pltpu.VMEM((tokens, LANES), F32),
                pltpu.VMEM((tokens + 16, rank), BF),
                pltpu.VMEM((2 * fwd_exps.shape[2], tok), jnp.int32),
                pltpu.VMEM((tokens, LANES), F32),
                dma((5,)),
            ],
            [(sc, SMEM)]
            + [(m, VMEM) for m in msgs]
            + [(h, HBM if section == 1 else VMEM), (fwd_exps, HBM), (stash, HBM)]
            + [(mid if section == 2 else far, ANY)]
            + weights,
        )
        kept.append((normed, latf, invb, colsum))
        held[section] = [low_out, high_in]
        if section == 1:
            msg, mid = lax.optimization_barrier((msg, mid))
            mid = swap(mid, 1, (1, 2))
        msgs = exchange(msg)

    gins, gouts = {}, {}
    g = grads
    for section in (3, 2, 1):
        top = section == 3
        outs = [(big, BF, VMEM), ((tokens, rank), BF, VMEM), ((tokens, rank), BF, VMEM)]
        scratch = [
            pltpu.VMEM(big, F32),
            pltpu.VMEM((tokens, LANES), F32),
            pltpu.VMEM((tokens, LANES), F32),
            pltpu.VMEM((tokens, LANES), F32),
            pltpu.VMEM((tokens, LANES), F32),
            pltpu.VMEM((2 * bwd_exps.shape[2], tok), jnp.int32),
            pltpu.VMEM((tokens, LANES), F32),
            dma((2,)),
        ]
        if top:
            outs += [(big, BF, VMEM), ((tokens, rank), F32, VMEM)]
            scratch = [pltpu.VMEM(big, BF)] + scratch
            ins = [(m, VMEM) for m in msgs0] + [(m, VMEM) for m in msgs] + [(h, VMEM), (g, HBM)]
        else:
            ins = [(m, VMEM) for m in msgs] + [(v, VMEM) for v in kept[section]] + [(g, VMEM)]
        result = call(
            functools.partial(backward_body, section),
            outs,
            scratch,
            [(sc, SMEM)] + ins + [(bwd_exps, HBM)] + [(w, VMEM) for w in held[section]],
        )
        next_g, msg, glat = result[:3]
        if top:
            normed, latf = result[3:]
            gin, gout = call(
                grads_top_body,
                [(qi, BF, VMEM), (qo, BF, VMEM)],
                [pltpu.VMEM(big, BF), dma((1,))],
                [(sc, SMEM), (normed, VMEM), (latf, VMEM), (g, HBM), (glat, VMEM)],
            )
        else:
            normed, latf = kept[section][:2]
            gin, gout = call(
                grads_body,
                [(qi, BF, VMEM), (qo, BF, VMEM)],
                [],
                [(normed, VMEM), (latf, VMEM), (g, VMEM), (glat, VMEM)],
            )
        msgs = exchange(msg)
        gins[section], gouts[section] = gin, gout
        if section == 2:
            msgs, gins, gouts = lax.optimization_barrier((msgs, gins, gouts))
        g = next_g
    rows, low = quarter // 4, rank // 4
    cut = call(
        grads_first_body,
        [((n, rows, rank), BF, VMEM) for n in (4, 4, 2, 2, 4)] + [((n, low, quarter), BF, VMEM) for n in (4, 4, 2, 2, 4)],
        [pltpu.VMEM(qi, BF), pltpu.VMEM(qo, BF)],
        [(sc, SMEM)]
        + [(m, VMEM) for m in msgs]
        + [(kept[0][0], VMEM), (kept[0][1], VMEM), (g, VMEM)]
        + [(terms[s], VMEM) for terms in (gins, gouts) for s in (1, 2, 3)],
    )
    a, b = cut[:5], cut[5:]
    far_a, far_b = (along_x(a[2], 1), along_x(a[3], 3)), (along_y(b[2], 1), along_y(b[3], 3))
    to_a, back_a, to_b, back_b = call(
        relay_body,
        [((4, rows, rank), BF, VMEM)] * 2 + [((4, low, quarter), BF, VMEM)] * 2,
        [],
        [(v, VMEM) for v in (a[1], a[4], *far_a, b[1], b[4], *far_b)],
    )
    a = [a[0], along_x(to_a, 1), along_x(back_a, 3)]
    b = [b[0], along_y(to_b, 1), along_y(back_b, 3)]
    cut = call(
        second_body,
        [((4, rows // 4, rank), BF, VMEM)] * 4 + [((4, low, rows), BF, VMEM)] * 4,
        [pltpu.VMEM((4, rows, rank), BF), pltpu.VMEM((4, low, quarter), BF)],
        [(sc, SMEM)] + [(v, VMEM) for v in a + b],
    )
    a = [cut[0]] + [along_y(cut[k], k) for k in (1, 2, 3)]
    b = [cut[4]] + [along_x(cut[4 + k], k) for k in (1, 2, 3)]
    (both,) = call(
        third_body,
        [((4, rows // 2, rank), BF, VMEM)],
        [],
        [(v, VMEM) for v in a + b],
    )
    shares = (both.astype(F32) + along_z(both, 1).astype(F32)).astype(BF)
    own = [lax.dynamic_index_in_dim(shares, q ^ k, 0, keepdims=False) for k in range(4)]
    mine = jnp.stack([own[0]] + [swap(own[k], k) for k in (1, 2, 3)])
    a, b = mine[:, : rows // 4], mine[:, rows // 4 :]
    a, b = gather(a, 4, along_y), gather(b, 4, along_x)
    a, b = lax.optimization_barrier((jnp.stack(a), jnp.stack(b)))
    a, b = gather_relayed(a, along_x), gather_relayed(b, along_y)
    total_in, total_out = call(
        place_body,
        [((1, 1, width, rank), BF, VMEM), ((1, 1, rank, width), BF, VMEM)],
        [],
        [(sc, SMEM)] + [(v, VMEM) for v in a + b],
    )
    return total_in, total_out


def solution(mesh):
    placed = (
        P(None, "rep", None),
        P(None, "rep", None),
        P("section", None, None, "rep", None),
        P(None, "rep"),
        P(None, None, "rep", None),
        P(None, None, "rep", None),
        P("section", None, None, None),
        P("section", None, None, None),
    )
    return jax.shard_map(
        on_device,
        mesh=mesh,
        in_specs=placed,
        out_specs=(P("section", None, None, None), P("section", None, None, None)),
        check_vma=False,
    )
```

```python
import functools

import jax
import jax.numpy as jnp
from jax import lax
from jax.experimental import pallas as pl
from jax.experimental.pallas import tpu as pltpu
from jax.sharding import PartitionSpec as P

EPS = 1e-05
BF = jnp.bfloat16
F32 = jnp.float32
ROWS = 16
LANES = 128
MIB = 1024 * 1024
ANY = pl.BlockSpec(memory_space=pl.ANY)
HBM = pl.BlockSpec(memory_space=pltpu.HBM)
VMEM = pl.BlockSpec(memory_space=pltpu.VMEM)
SMEM = pl.BlockSpec(memory_space=pltpu.SMEM)


def dot_nn(a, b):
    return lax.dot_general(a, b, (((1,), (0,)), ((), ())), preferred_element_type=F32)


def dot_nt(a, b):
    return lax.dot_general(a, b, (((1,), (1,)), ((), ())), preferred_element_type=F32)


def dot_tn(a, b):
    return lax.dot_general(a, b, (((0,), (0,)), ((), ())), preferred_element_type=F32)


class Place:
    def __init__(self, ids):
        rep = lax.axis_index("rep")
        self.ids = ids
        self.at = {0: lax.axis_index("section"), 3: rep // 8, 4: rep // 4 % 2, 5: rep % 4}

    def __getitem__(self, k):
        return self.ids[k - 1, 0] if k in (1, 2) else self.at[k]


def placed(body, ids, *refs):
    body(Place(ids), *refs)


def call(body, outs, scratch, ins, flops=10**8, nbytes=4 * 10**6, vmem=12, aliases=None):
    return pl.pallas_call(
        functools.partial(placed, body) if ins[0][1] is SMEM else body,
        out_shape=[jax.ShapeDtypeStruct(s, d) for s, d, _ in outs],
        in_specs=[spec for _, spec in ins],
        out_specs=[spec for _, _, spec in outs],
        scratch_shapes=scratch,
        input_output_aliases=aliases or {},
        compiler_params=pltpu.CompilerParams(vmem_limit_bytes=vmem * MIB),
        cost_estimate=pl.CostEstimate(flops=flops, bytes_accessed=nbytes, transcendentals=0),
    )(*[pltpu.with_memory_space_constraint(a, pltpu.HBM) if spec is HBM else a for a, spec in ins])


def lane_iota(rows):
    return lax.broadcasted_iota(jnp.int32, (rows, LANES), 1)


def row_iota(rows):
    return lax.broadcasted_iota(jnp.int32, (rows, LANES), 0)


def three(x):
    hi = x.astype(BF).astype(F32)
    rest = x - hi
    mid = rest.astype(BF).astype(F32)
    return hi, mid, (rest - mid).astype(BF).astype(F32)


def pack_rows(first_half, second_half, extra):
    at = row_iota(16)
    out = jnp.zeros((16, LANES), F32)
    for base, (a, b) in ((0, first_half), (8, second_half)):
        for j, row in enumerate(three(a) + three(b)):
            out = jnp.where(at == base + j, row, out)
    if extra is not None:
        hi, mid, _ = three(extra)
        out = jnp.where(at == 6, hi, out)
        out = jnp.where(at == 7, mid, out)
    return out.astype(BF)


def unpack_rows(block):
    block = block.astype(F32)

    def joined(base):
        return block[base : base + 1] + block[base + 1 : base + 2] + block[base + 2 : base + 3]

    return (joined(0), joined(8)), (joined(3), joined(11)), block[6:7] + block[7:8]


def columns(rows):
    at = row_iota(LANES)
    out = jnp.zeros((LANES, LANES), F32)
    for j, row in enumerate(rows):
        out = jnp.where(at == j, row, out)
    return out.T


def join_latent(msgs, tokens, width):
    parsed = [unpack_rows(m[tokens : tokens + 16]) for m in msgs]
    total = msgs[0][:tokens].astype(F32)
    for m in msgs[1:]:
        total = total + m[:tokens].astype(F32)
    halves = []
    for half in range(2):
        means = [p[0][half] for p in parsed]
        mean = (means[0] + means[1] + means[2] + means[3]) * 0.25
        offs = [m - mean for m in means]
        var = (parsed[0][1][half] + parsed[1][1][half] + parsed[2][1][half] + parsed[3][1][half]) * 0.25
        var = var + (offs[0] * offs[0] + offs[1] * offs[1] + offs[2] * offs[2] + offs[3] * offs[3]) * 0.25
        halves.append(columns([mean, lax.rsqrt(var + EPS)] + offs))
    cols = jnp.concatenate(halves, axis=0)
    colsum = parsed[0][2]
    for d in range(4):
        total = total + cols[:, 2 + d : 3 + d] * parsed[d][2]
        if d:
            colsum = colsum + parsed[d][2]
    return total * cols[:, 1:2], cols[:, 0:1], cols[:, 1:2], colsum


def start_first(pairs, sem):
    for cond, src, dst in pairs:
        @pl.when(cond)
        def _(src=src, dst=dst):
            pltpu.make_async_copy(src, dst, sem).start()


def start_weight(section, sc, own, near, same, cross, inner, dst, sem):
    q, x, y = sc[0], sc[3], sc[5]
    zh, c = q // 2, q % 2
    here = zh == section // 2
    mine = c == section % 2
    piece = 384

    def start(src, to):
        pltpu.make_async_copy(src, to, sem).start()

    @pl.when(here & mine)
    def _():
        start(own, dst)

    @pl.when(here & jnp.logical_not(mine))
    def _():
        start(near, dst)

    def pieces(refs, first):
        for j in range(2):
            for i in range(2):
                px, py = (i, j) if first == 0 else (j, i)
                at = piece_of(x ^ px, y ^ py) * piece
                base = i * 2 * piece
                if inner:
                    start(refs[j].at[pl.ds(base, piece)], dst.at[pl.ds(pl.multiple_of(at, piece), piece)])
                else:
                    for t in range(piece // LANES):
                        cols = pl.ds(pl.multiple_of(at + t * LANES, LANES), LANES)
                        start(refs[j].at[pl.ds(base + piece + t * LANES, LANES)], dst.at[:, cols])

    @pl.when(jnp.logical_not(here) & mine)
    def _():
        pieces(same, 0)

    @pl.when(jnp.logical_not(here) & jnp.logical_not(mine))
    def _():
        pieces(cross, 1)


def piece_of(x, y):
    return (x & 1) * 2 + (y & 1)


def factors(exps, q, out):
    every = exps.shape[0] // 2
    blocks = every // 4
    for k in range(4):
        @pl.when(q == k)
        def _(k=k):
            for m in range(2):
                e = exps[m * every + k * blocks : m * every + (k + 1) * blocks, :]
                f = lax.shift_left(jnp.ones(e.shape, jnp.int32), e + 14).astype(F32) * (2.0**-14)
                full = jnp.concatenate([f, jnp.zeros((LANES - blocks, LANES), F32)], axis=0)
                out[m * LANES : (m + 1) * LANES, :] = full.T


def wait_for(dst, sem):
    pltpu.make_async_copy(dst, dst, sem).wait()


def send_body(sc, stash, w_in, w_out, far, mid, sib_in, sib_out, over, sems):
    q, x, y = sc[0], sc[3], sc[5]
    c = q % 2
    tok, quarter = far.shape[0] // 2, far.shape[1]
    piece = quarter // 4
    mid_slot = jnp.where(q == 1, 1, 0)
    copies = []

    def go(src, dst):
        copy = pltpu.make_async_copy(src, dst, sems.at[len(copies)])
        copy.start()
        copies.append(copy)

    def cols(k):
        return pl.ds(pl.multiple_of((q ^ k) * quarter, quarter), quarter)

    for k in (2, 3):
        base = (q ^ k) * quarter + piece_of(x, y) * piece
        first = (k - 2) * 2 * piece
        go(w_in.at[0, 0, pl.ds(pl.multiple_of(base, piece), piece), :], over.at[pl.ds(first, piece)])
        for t in range(piece // LANES):
            from_cols = pl.ds(pl.multiple_of(base + t * LANES, LANES), LANES)
            go(w_out.at[0, 0, :, from_cols], over.at[pl.ds(first + piece + t * LANES, LANES)])
    for m in range(2):
        go(stash.at[0, 1 - c, sc[1 + m], :, cols(2)], far.at[pl.ds(m * tok, tok)])
    go(w_out.at[0, 0, :, cols(1)], sib_out)
    go(w_in.at[0, 0, cols(1), :], sib_in)
    for m in range(2):
        go(stash.at[0, mid_slot, sc[1 + m], :, cols(1)], mid.at[pl.ds(m * tok, tok)])
    for copy in copies:
        copy.wait()


def sum_blocks(block, count):
    parts = []
    for b in range(count):
        v = block(b)
        if b < 4:
            parts.append(v)
        else:
            parts[b % 4] = parts[b % 4] + v
    return (parts[0] + parts[1]) + (parts[2] + parts[3])


def first_body(sc, micro, grads, w_in, w_out, msg, x_v, w_v, wo_v, n_v, st, sems):
    q = sc[0]
    tokens, width = x_v.shape
    tok = tokens // 2
    blocks = width // LANES

    def load(src, wsrc, wdst):
        copies = [pltpu.make_async_copy(src.at[m], x_v.at[pl.ds(m * tok, tok)], sems.at[m]) for m in range(2)]
        copies.append(pltpu.make_async_copy(wsrc.at[0, 0], wdst, sems.at[2]))
        for copy in copies:
            copy.start()
        return copies

    @pl.when(q == 0)
    def _():
        load(micro, w_in, w_v)

    @pl.when(q == 3)
    def _():
        load(grads, w_out, wo_v)

    @pl.when((q == 1) | (q == 2))
    def _():
        msg[...] = jnp.zeros(msg.shape, BF)

    @pl.when(q == 0)
    def _():
        for m in range(2):
            wait_for(x_v.at[pl.ds(m * tok, tok)], sems.at[m])

            @pl.loop(m * (tok // ROWS), (m + 1) * (tok // ROWS), unroll=2)
            def _(i):
                rows = pl.ds(pl.multiple_of(i * ROWS, ROWS), ROWS)

                def block(b):
                    return x_v[rows, b * LANES : (b + 1) * LANES].astype(F32)

                def square(b):
                    d = block(b) - mean
                    return d * d

                mean = jnp.sum(sum_blocks(block, blocks), axis=1, keepdims=True) * (1.0 / width)
                mean = jnp.broadcast_to(mean, (ROWS, LANES))
                inv = lax.rsqrt(jnp.sum(sum_blocks(square, blocks), axis=1, keepdims=True) * (1.0 / width) + EPS)
                inv = jnp.broadcast_to(inv, (ROWS, LANES))
                for b in range(blocks):
                    n_v[rows, b * LANES : (b + 1) * LANES] = ((block(b) - mean) * inv).astype(BF)
                st[rows, :] = jnp.where(lane_iota(ROWS) == 0, mean, inv)

        wait_for(w_v, sems.at[2])
        latent = dot_nn(n_v[...], w_v[...])
        msg[:tokens] = latent.astype(BF)
        t0, t1 = st[:LANES].T, st[LANES:].T
        msg[tokens:] = pack_rows((t0[0:1], t0[1:2]), (t1[0:1], t1[1:2]), None)

    @pl.when(q == 3)
    def _():
        for m in range(2):
            wait_for(x_v.at[pl.ds(m * tok, tok)], sems.at[m])
        wait_for(wo_v, sems.at[2])
        msg[:tokens] = dot_nt(x_v[...], wo_v[...]).astype(BF)
        msg[tokens:] = jnp.zeros((msg.shape[0] - tokens, msg.shape[1]), BF)


def forward_body(section, sc, *refs):
    first = section == 1
    refs = list(refs)
    take = refs.pop
    msgs = [take(0) for _ in range(4)]
    h_in = take(0)
    exps = take(0)
    stash, held = take(0), take(0)
    wi_own, wo_own, wi_near, wo_near = [take(0) for _ in range(4)]
    same, cross = [take(0) for _ in range(2)], [take(0) for _ in range(2)]
    h_out, normed, msg, latf, invb, colsum_out, wo_v, wi_v = [take(0) for _ in range(8)]
    x_v, pick, up, cen, st, mc = [take(0) for _ in range(6)]
    lat_v, e_v, factor, sems = [take(0) for _ in range(4)]
    q = sc[0]
    c = q % 2
    tokens, quarter = pick.shape
    tok = tokens // 2
    cols = pl.ds(pl.multiple_of(q * quarter, quarter), quarter)
    start_weight(section - 1, sc, wo_own.at[0, 0, :, cols], wo_near, same, cross, False, wo_v, sems.at[0])
    for m in range(2):
        pltpu.make_async_copy(exps.at[section - 1, m], e_v.at[pl.ds(m * exps.shape[2], exps.shape[2])], sems.at[4]).start()
    if first:
        for m in range(2):
            pltpu.make_async_copy(h_in.at[m, :, cols], x_v.at[pl.ds(m * tok, tok)], sems.at[2]).start()
    if section == 2:
        local, slot = (q == 1) | (q == 2), jnp.where(q == 1, 1, 0)
    else:
        local, slot = (q // 2 == 0) if section == 1 else (q // 2 == 1), 1 - c
    for m in range(2):
        rows = pl.ds(m * tok, tok)
        start_first(
            [
                (local, stash.at[0, slot, sc[1 + m], :, cols], pick.at[rows]),
                (jnp.logical_not(local), held.at[rows], pick.at[rows]),
            ],
            sems.at[3],
        )
    start_weight(section, sc, wi_own.at[0, 0, cols, :], wi_near, same, cross, True, wi_v, sems.at[1])

    if first:
        for k in range(4):
            @pl.when(q == k)
            def _(k=k):
                lat_v[...] = msgs[k][...]

        (m0, m1), (v0, v1), _ = unpack_rows(lat_v[tokens:])
        both = jnp.concatenate([columns([m0, v0]), columns([m1, v1])], axis=0)
        latent = lat_v[:tokens].astype(F32)
        mean, inv = both[:, 0:1], both[:, 1:2]
        colsum_out[...] = jnp.zeros(colsum_out.shape, F32)
    else:
        latent, mean, inv, colsum = join_latent([m[...] for m in msgs], tokens, quarter)
        colsum_out[...] = jnp.broadcast_to(colsum, colsum_out.shape)
    latf[...] = latent
    invb[...] = jnp.broadcast_to(inv, invb.shape)
    mc[...] = jnp.broadcast_to(mean, mc.shape)
    wait_for(wo_v, sems.at[0])
    up[...] = dot_nn(latent.astype(BF), wo_v[...])
    wait_for(e_v, sems.at[4])
    factors(e_v, q, factor)
    if first:
        wait_for(x_v, sems.at[2])
        src = x_v
    else:
        src = h_in
    wait_for(pick, sems.at[3])

    @pl.loop(0, tokens // ROWS, unroll=4)
    def _(i):
        rows = pl.ds(pl.multiple_of(i * ROWS, ROWS), ROWS)
        mean_t, inv_t = mc[rows, :], invb[rows, :]
        fac = factor[rows, :]
        kept = []
        for b in range(quarter // LANES):
            lanes = slice(b * LANES, (b + 1) * LANES)
            h = src[rows, lanes].astype(F32)
            normed[rows, lanes] = ((h - mean_t) * inv_t).astype(BF)
            stored = pick[rows, lanes].astype(F32)
            f = fac[:, b : b + 1]
            d = jnp.clip(h + up[rows, lanes] - stored, f * -8.0, f * 7.0).astype(BF)
            h = stored + d.astype(F32)
            h_out[rows, lanes] = h
            kept.append(h)
        st[rows, :] = sum_blocks(lambda b: kept[b], quarter // LANES)

    mean_d = jnp.sum(st[...], axis=1, keepdims=True) * (1.0 / quarter)
    mc[...] = jnp.broadcast_to(mean_d, mc.shape)

    @pl.loop(0, tokens // ROWS, unroll=4)
    def _(i):
        rows = pl.ds(pl.multiple_of(i * ROWS, ROWS), ROWS)
        mean_t = mc[rows, :]
        kept = [h_out[rows, b * LANES : (b + 1) * LANES] - mean_t for b in range(quarter // LANES)]
        for b in range(quarter // LANES):
            cen[rows, b * LANES : (b + 1) * LANES] = kept[b].astype(BF)
        st[rows, :] = sum_blocks(lambda b: kept[b] * kept[b], quarter // LANES)

    var_d = jnp.sum(st[...], axis=1, keepdims=True) * (1.0 / quarter)
    st[...] = jnp.where(lane_iota(tokens) == 0, mc[...], var_d)

    wait_for(wi_v, sems.at[1])
    w = wi_v[...]
    msg[:tokens] = dot_nn(cen[...], w).astype(BF)
    colsum = dot_nn(jnp.ones((16, quarter), BF), w)[0:1]
    t0, t1 = st[:LANES].T, st[LANES:].T
    msg[tokens:] = pack_rows((t0[0:1], t0[1:2]), (t1[0:1], t1[1:2]), colsum)


def backward_body(section, sc, *refs):
    top = section == 3
    refs = list(refs)
    take = refs.pop
    msgs = [take(0) for _ in range(4)]
    if top:
        lat_msgs = [take(0) for _ in range(4)]
        h_in = take(0)
    else:
        normed_in, latf, invb, colsum_in = [take(0) for _ in range(4)]
    g_in = take(0)
    exps, wo_v, wi_v = [take(0) for _ in range(3)]
    g_out, msg, glat_out = [take(0) for _ in range(3)]
    if top:
        normed, latf, g_v = [take(0) for _ in range(3)]
    gn, mc, inv_v, a_v, b_v, e_v, factor, sems = [take(0) for _ in range(8)]
    q = sc[0]
    tokens, quarter = gn.shape
    tok = tokens // 2
    width = 4 * quarter
    cols = pl.ds(pl.multiple_of(q * quarter, quarter), quarter)
    for m in range(2):
        pltpu.make_async_copy(exps.at[section, m], e_v.at[pl.ds(m * exps.shape[2], exps.shape[2])], sems.at[1]).start()
    if top:
        for m in range(2):
            pltpu.make_async_copy(g_in.at[m, :, cols], g_v.at[pl.ds(m * tok, tok)], sems.at[0]).start()
        latent, mean, inv, colsum = join_latent([m[...] for m in lat_msgs], tokens, quarter)
        latf[...] = latent
        mc[...] = jnp.broadcast_to(mean, mc.shape)
        inv_v[...] = jnp.broadcast_to(inv, inv_v.shape)
        for k in range(4):
            @pl.when(q ^ 3 == k)
            def _(k=k):
                glat_out[...] = msgs[k][:tokens]

        glat = glat_out[...]
        src, norm, inv_ref = g_v, normed, inv_v
    else:
        latent, colsum = latf[...], colsum_in[0:1]
        glat = msgs[0][:tokens].astype(F32)
        for m in msgs[1:]:
            glat = glat + m[:tokens].astype(F32)
        glat = glat.astype(BF)
        glat_out[...] = glat
        src, norm, inv_ref = g_in, normed_in, invb
    wide = glat.astype(F32)
    a_v[...] = jnp.broadcast_to(jnp.sum(wide * colsum, axis=1, keepdims=True) * (1.0 / width), a_v.shape)
    b_v[...] = jnp.broadcast_to(jnp.sum(wide * latent, axis=1, keepdims=True) * (1.0 / width), b_v.shape)
    gn[...] = dot_nt(glat, wi_v[...])
    wait_for(e_v, sems.at[1])
    factors(e_v, q, factor)
    if top:
        wait_for(g_v, sems.at[0])

    @pl.loop(0, tokens // ROWS, unroll=4)
    def _(i):
        rows = pl.ds(pl.multiple_of(i * ROWS, ROWS), ROWS)
        fac = factor[rows, :]
        inv_t, a_t, b_t = inv_ref[rows, :], a_v[rows, :], b_v[rows, :]
        for b in range(quarter // LANES):
            lanes = slice(b * LANES, (b + 1) * LANES)
            if top:
                n = (h_in[rows, lanes] - mc[rows, :]) * inv_t
                normed[rows, lanes] = n.astype(BF)
            else:
                n = norm[rows, lanes].astype(F32)
            f = fac[:, b : b + 1]
            g = src[rows, lanes].astype(F32) + inv_t * (gn[rows, lanes] - a_t - n * b_t)
            g_out[rows, lanes] = jnp.clip(g, f * -128.0, f * 127.0).astype(BF)

    msg[...] = dot_nt(g_out[...], wo_v[...]).astype(BF)


def grads_body(normed, latf, g_ref, glat, gin, gout):
    gin[...] = dot_tn(normed[...], glat[...]).astype(BF)
    gout[...] = dot_tn(latf[...].astype(BF), g_ref[...]).astype(BF)


def grads_top_body(sc, normed, latf, g_ref, glat, gin, gout, g_v, sems):
    quarter = g_v.shape[1]
    tok = g_v.shape[0] // 2
    cols = pl.ds(pl.multiple_of(sc[0] * quarter, quarter), quarter)
    for m in range(2):
        pltpu.make_async_copy(g_ref.at[m, :, cols], g_v.at[pl.ds(m * tok, tok)], sems.at[0]).start()
    gin[...] = dot_tn(normed[...], glat[...]).astype(BF)
    wait_for(g_v, sems.at[0])
    gout[...] = dot_tn(latf[...].astype(BF), g_v[...]).astype(BF)


def grads_first_body(sc, *refs):
    refs = list(refs)
    take = refs.pop
    msgs = [take(0) for _ in range(4)]
    normed, latf, g_ref = [take(0) for _ in range(3)]
    gins = [None] + [take(0) for _ in range(3)]
    gouts = [None] + [take(0) for _ in range(3)]
    a, b = [take(0) for _ in range(5)], [take(0) for _ in range(5)]
    gin0, gout0 = take(0), take(0)
    gins[0], gouts[0] = gin0, gout0
    x, y = sc[3], sc[5]
    glat = msgs[0][...].astype(F32)
    for m in msgs[1:]:
        glat = glat + m[...].astype(F32)
    gin0[...] = dot_tn(normed[...], glat.astype(BF)).astype(BF)
    gout0[...] = dot_tn(latf[...].astype(BF), g_ref[...]).astype(BF)
    rows, low = a[0].shape[1], b[0].shape[1]
    for k in range(4):
        at = pl.ds(pl.multiple_of(((x + k) % 4) * rows, rows), rows)
        to = pl.ds(pl.multiple_of(((y + k) % 4) * low, low), low)
        for s in range(4):
            d, i = (2 + s // 2, s % 2) if k == 2 else ((0, 1, 2, 4)[k], s)
            a[d][i] = gins[s][at, :]
            b[d][i] = gouts[s][to, :]


def relay_body(a1, a3, a_lo, a_hi, b1, b3, b_lo, b_hi, a1_out, a3_out, b1_out, b3_out):
    for src, extra, at, dst in (
        (a1, a_lo, 0, a1_out),
        (a3, a_hi, 2, a3_out),
        (b1, b_lo, 0, b1_out),
        (b3, b_hi, 2, b3_out),
    ):
        for s in range(4):
            if at <= s < at + 2:
                dst[s] = total_of([src[s], extra[s - at]])
            else:
                dst[s] = src[s]


def total_of(parts):
    total = parts[0].astype(F32)
    for part in parts[1:]:
        total = total + part.astype(F32)
    return total.astype(BF)


def second_body(sc, a0, a1, a2, b0, b1, b2, c0, c1, c2, c3, d0, d1, d2, d3, a_v, b_v):
    x, y = sc[3], sc[5]
    for s in range(4):
        a_v[s] = total_of([r[s] for r in (a0, a1, a2)])
        b_v[s] = total_of([r[s] for r in (b0, b1, b2)])
    rows, cols = c0.shape[1], d0.shape[2]
    for k, (c, d) in enumerate(((c0, d0), (c1, d1), (c2, d2), (c3, d3))):
        at = pl.ds(pl.multiple_of(((y + k) % 4) * rows, rows), rows)
        to = pl.ds(pl.multiple_of(((x + k) % 4) * cols, cols), cols)
        for s in range(4):
            c[s] = a_v[s, at, :]
            d[s] = b_v[s, :, to]


def third_body(a0, a1, a2, a3, b0, b1, b2, b3, out):
    rows, low = a0.shape[1], b0.shape[1]
    for s in range(4):
        out[s, :rows] = total_of([r[s] for r in (a0, a1, a2, a3)])
        total = total_of([r[s] for r in (b0, b1, b2, b3)])
        for t in range(total.shape[1] // LANES):
            out[s, rows + t * low : rows + (t + 1) * low] = total[:, t * LANES : (t + 1) * LANES]


def rep_of(x, z, y):
    return x * 8 + z * 4 + y


EVERY = [(x, z, y) for x in range(4) for z in range(2) for y in range(4)]


def along_x(value, k):
    return lax.ppermute(value, "rep", [(rep_of(x, z, y), rep_of((x + k) % 4, z, y)) for x, z, y in EVERY])


def along_y(value, k):
    return lax.ppermute(value, "rep", [(rep_of(x, z, y), rep_of(x, z, (y + k) % 4)) for x, z, y in EVERY])


def along_z(value, k):
    return lax.ppermute(value, "rep", [(rep_of(x, z, y), rep_of(x, (z + k) % 2, y)) for x, z, y in EVERY])


def gather(value, count, move):
    return [value] + [move(value, k) for k in range(1, count)]


def gather_relayed(value, move):
    before, after = move(value, 1), move(value, 3)
    half = value.shape[0] // 2
    return [value, before, move(before[:half], 1), move(after[half:], 3), after]


def place_pieces(sc, parts, gin, gout, gin_v, gout_v, sem):
    q, x, y = sc[0], sc[3], sc[5]
    quarter = gin.shape[2] // 4
    rows, low = quarter // 16, gout.shape[2] // 4
    copies = []
    for back, first, a_ref, b_ref in parts:
        for i in range(a_ref.shape[0]):
            j = first + i
            for d in range(4):
                base = (q ^ d) * quarter
                row = base + ((x - back + 4) % 4) * (quarter // 4) + ((y - j + 4) % 4) * rows
                gin_v[pl.ds(pl.multiple_of(row, rows), rows), :] = a_ref[i, d]
                at = pl.ds(pl.multiple_of(((y - back + 4) % 4) * low, low), low)
                for t in range(quarter // 4 // LANES):
                    col = base + ((x - j + 4) % 4) * (quarter // 4) + t * LANES
                    gout_v[at, pl.ds(pl.multiple_of(col, LANES), LANES)] = b_ref[i, d, t * low : (t + 1) * low, :]
        if first + a_ref.shape[0] == 4:
            for d in range(4):
                row = d * quarter + ((x - back + 4) % 4) * (quarter // 4)
                whole = pl.ds(pl.multiple_of(row, quarter // 4), quarter // 4)
                copies.append(pltpu.make_async_copy(gin_v.at[whole], gin.at[0, 0, whole], sem.at[len(copies)]))
                copies[-1].start()
            whole = pl.ds(pl.multiple_of(((y - back + 4) % 4) * low, low), low)
            copies.append(pltpu.make_async_copy(gout_v.at[whole], gout.at[0, 0, whole], sem.at[len(copies)]))
            copies[-1].start()
    for copy in copies:
        copy.wait()


def place_body(sc, a0, a1, a4, b0, b1, b4, gin, gout, gin_v, gout_v, sem):
    place_pieces(sc, ((0, 0, a0, b0), (1, 0, a1, b1), (3, 0, a4, b4)), gin, gout, gin_v, gout_v, sem)


def place_last_body(sc, a2, a3, b2, b3, gin_in, gout_in, gin, gout, gin_v, gout_v, sem):
    place_pieces(sc, ((2, 0, a2, b2), (2, 2, a3, b3)), gin, gout, gin_v, gout_v, sem)


def on_device(micro, grads, stash, sample_ids, fwd_exps, bwd_exps, w_in, w_out):
    q = lax.axis_index("section")
    tok, width = micro.shape[1], micro.shape[2]
    tokens, quarter, rank = 2 * tok, width // 4, w_in.shape[3]
    fwd_exps, bwd_exps = jnp.swapaxes(fwd_exps, 2, 3), jnp.swapaxes(bwd_exps, 2, 3)
    sc = sample_ids

    def swap(value, k, sources=range(4)):
        return lax.ppermute(value, "section", [(s, s ^ k) for s in sources])

    def exchange(value):
        return [value] + [swap(value, k) for k in (1, 2, 3)]

    def beside(value):
        pairs = [(s * 32 + rep_of(xx, zz, yy), (s ^ 2) * 32 + rep_of(xx, 1 - zz, yy)) for s in range(4) for xx, zz, yy in EVERY]
        return lax.ppermute(value, ("section", "rep"), pairs)

    def beside_along(value, dx, dy, core):
        pairs = [(s * 32 + rep_of(xx, zz, yy), (s ^ core) * 32 + rep_of(xx ^ dx, zz, yy ^ dy)) for s in range(4) for xx, zz, yy in EVERY]
        return lax.ppermute(value, ("section", "rep"), pairs)

    dma = pltpu.SemaphoreType.DMA
    big = (tokens, quarter)
    qi, qo = (quarter, rank), (rank, quarter)
    far, mid, sib_in, sib_out, over = call(
        send_body,
        [(big, BF, VMEM)] * 2 + [(qi, BF, VMEM), (qo, BF, VMEM), (qi, BF, VMEM)],
        [dma((14,))],
        [(sc, SMEM), (stash, HBM), (w_in, HBM), (w_out, HBM)],
    )
    over = beside(over)
    (msg0,) = call(
        first_body,
        [((tokens + 16, rank), BF, VMEM)],
        [
            pltpu.VMEM((tokens, width), BF),
            pltpu.VMEM((width, rank), BF),
            pltpu.VMEM((rank, width), BF),
            pltpu.VMEM((tokens, width), BF),
            pltpu.VMEM((tokens, LANES), F32),
            dma((3,)),
        ],
        [(sc, SMEM), (micro, HBM), (grads, HBM), (w_in, HBM), (w_out, HBM)],
        vmem=16,
        nbytes=3 * 10**7,
    )
    msg0, far = lax.optimization_barrier((msg0, far))
    far = swap(far, 2)
    near_msg = swap(msg0, 1, (0, 3))
    over, msg0, sib_in, sib_out = lax.optimization_barrier((over, msg0, sib_in, sib_out))
    half = quarter // 2
    same, cross = over[:half], over[half:]
    same = jnp.concatenate([same, beside_along(same, 1, 0, 0)], 0)
    cross = jnp.concatenate([swap(cross, 1), beside_along(cross, 0, 1, 1)], 0)
    same, cross, sib_in, sib_out = lax.optimization_barrier((same, cross, sib_in, sib_out))
    pieces = [same, beside_along(same, 0, 1, 0), cross, beside_along(cross, 1, 0, 0)]
    near = [swap(sib_in, 1), swap(sib_out, 1)]
    near, msg0 = lax.optimization_barrier((near, msg0))
    msgs0 = [near_msg] + [swap(msg0, k, (0, 3)) for k in (2, 3)]
    pieces, far, near, msgs0 = lax.optimization_barrier((pieces, far, near, msgs0))
    msgs0 = [msg0] + msgs0
    weights = [w_in, w_out] + near + pieces
    weights = list(zip(weights, [HBM, HBM] + [ANY] * 6))

    msgs = msgs0
    h = micro
    kept = []
    held = {}
    for section in (1, 2, 3):
        h, normed, msg, latf, invb, colsum, low_out, high_in = call(
            functools.partial(forward_body, section),
            [
                (big, F32, VMEM),
                (big, BF, VMEM),
                ((tokens + 16, rank), BF, VMEM),
                ((tokens, rank), F32, VMEM),
                ((tokens, LANES), F32, VMEM),
                ((8, LANES), F32, VMEM),
                (qo, BF, VMEM),
                (qi, BF, VMEM),
            ],
            [
                pltpu.VMEM(big, BF),
                pltpu.VMEM(big, BF),
                pltpu.VMEM(big, F32),
                pltpu.VMEM(big, BF),
                pltpu.VMEM((tokens, LANES), F32),
                pltpu.VMEM((tokens, LANES), F32),
                pltpu.VMEM((tokens + 16, rank), BF),
                pltpu.VMEM((2 * fwd_exps.shape[2], tok), jnp.int32),
                pltpu.VMEM((tokens, LANES), F32),
                dma((5,)),
            ],
            [(sc, SMEM)]
            + [(m, VMEM) for m in msgs]
            + [(h, HBM if section == 1 else VMEM), (fwd_exps, HBM), (stash, HBM)]
            + [(mid if section == 2 else far, ANY)]
            + weights,
        )
        kept.append((normed, latf, invb, colsum))
        held[section] = [low_out, high_in]
        if section == 1:
            msg, mid = lax.optimization_barrier((msg, mid))
            mid = swap(mid, 1, (1, 2))
        msgs = exchange(msg)

    gins, gouts = {}, {}
    g = grads
    for section in (3, 2, 1):
        top = section == 3
        outs = [(big, BF, VMEM), ((tokens, rank), BF, VMEM), ((tokens, rank), BF, VMEM)]
        scratch = [
            pltpu.VMEM(big, F32),
            pltpu.VMEM((tokens, LANES), F32),
            pltpu.VMEM((tokens, LANES), F32),
            pltpu.VMEM((tokens, LANES), F32),
            pltpu.VMEM((tokens, LANES), F32),
            pltpu.VMEM((2 * bwd_exps.shape[2], tok), jnp.int32),
            pltpu.VMEM((tokens, LANES), F32),
            dma((2,)),
        ]
        if top:
            outs += [(big, BF, VMEM), ((tokens, rank), F32, VMEM)]
            scratch = [pltpu.VMEM(big, BF)] + scratch
            ins = [(m, VMEM) for m in msgs0] + [(m, VMEM) for m in msgs] + [(h, VMEM), (g, HBM)]
        else:
            ins = [(m, VMEM) for m in msgs] + [(v, VMEM) for v in kept[section]] + [(g, VMEM)]
        result = call(
            functools.partial(backward_body, section),
            outs,
            scratch,
            [(sc, SMEM)] + ins + [(bwd_exps, HBM)] + [(w, VMEM) for w in held[section]],
        )
        next_g, msg, glat = result[:3]
        if top:
            normed, latf = result[3:]
            gin, gout = call(
                grads_top_body,
                [(qi, BF, VMEM), (qo, BF, VMEM)],
                [pltpu.VMEM(big, BF), dma((1,))],
                [(sc, SMEM), (normed, VMEM), (latf, VMEM), (g, HBM), (glat, VMEM)],
            )
        else:
            normed, latf = kept[section][:2]
            gin, gout = call(
                grads_body,
                [(qi, BF, VMEM), (qo, BF, VMEM)],
                [],
                [(normed, VMEM), (latf, VMEM), (g, VMEM), (glat, VMEM)],
            )
        msgs = exchange(msg)
        gins[section], gouts[section] = gin, gout
        if section == 2:
            msgs, gins, gouts = lax.optimization_barrier((msgs, gins, gouts))
        g = next_g
    rows, low = quarter // 4, rank // 4
    cut = call(
        grads_first_body,
        [((n, rows, rank), BF, VMEM) for n in (4, 4, 2, 2, 4)] + [((n, low, quarter), BF, VMEM) for n in (4, 4, 2, 2, 4)],
        [pltpu.VMEM(qi, BF), pltpu.VMEM(qo, BF)],
        [(sc, SMEM)]
        + [(m, VMEM) for m in msgs]
        + [(kept[0][0], VMEM), (kept[0][1], VMEM), (g, VMEM)]
        + [(terms[s], VMEM) for terms in (gins, gouts) for s in (1, 2, 3)],
    )
    a, b = cut[:5], cut[5:]
    far_a, far_b = (along_x(a[2], 1), along_x(a[3], 3)), (along_y(b[2], 1), along_y(b[3], 3))
    to_a, back_a, to_b, back_b = call(
        relay_body,
        [((4, rows, rank), BF, VMEM)] * 2 + [((4, low, quarter), BF, VMEM)] * 2,
        [],
        [(v, VMEM) for v in (a[1], a[4], *far_a, b[1], b[4], *far_b)],
    )
    a = [a[0], along_x(to_a, 1), along_x(back_a, 3)]
    b = [b[0], along_y(to_b, 1), along_y(back_b, 3)]
    cut = call(
        second_body,
        [((4, rows // 4, rank), BF, VMEM)] * 4 + [((4, low, rows), BF, VMEM)] * 4,
        [pltpu.VMEM((4, rows, rank), BF), pltpu.VMEM((4, low, quarter), BF)],
        [(sc, SMEM)] + [(v, VMEM) for v in a + b],
    )
    a = [cut[0]] + [along_y(cut[k], k) for k in (1, 2, 3)]
    b = [cut[4]] + [along_x(cut[4 + k], k) for k in (1, 2, 3)]
    (both,) = call(
        third_body,
        [((4, rows // 2, rank), BF, VMEM)],
        [],
        [(v, VMEM) for v in a + b],
    )
    shares = (both.astype(F32) + along_z(both, 1).astype(F32)).astype(BF)
    own = [lax.dynamic_index_in_dim(shares, q ^ k, 0, keepdims=False) for k in range(4)]
    mine = jnp.stack([own[0]] + [swap(own[k], k) for k in (1, 2, 3)])
    a, b = mine[:, : rows // 4], mine[:, rows // 4 :]
    a, b = gather(a, 4, along_y), gather(b, 4, along_x)
    a, b = jnp.stack(a), jnp.stack(b)
    a, b = gather_relayed(a, along_x), gather_relayed(b, along_y)
    totals = [((1, 1, width, rank), BF, HBM), ((1, 1, rank, width), BF, HBM)]
    whole = [pltpu.VMEM((width, rank), BF), pltpu.VMEM((rank, width), BF)]
    total_in, total_out = call(
        place_body,
        totals,
        whole + [dma((15,))],
        [(sc, SMEM)] + [(v, VMEM) for v in (a[0], a[1], a[4], b[0], b[1], b[4])],
    )
    total_in, total_out = call(
        place_last_body,
        totals,
        whole + [dma((5,))],
        [(sc, SMEM)] + [(v, VMEM) for v in (a[2], a[3], b[2], b[3])] + [(total_in, HBM), (total_out, HBM)],
        aliases={5: 0, 6: 1},
    )
    return total_in, total_out


def solution(mesh):
    placed = (
        P(None, "rep", None),
        P(None, "rep", None),
        P("section", None, None, "rep", None),
        P(None, "rep"),
        P(None, None, "rep", None),
        P(None, None, "rep", None),
        P("section", None, None, None),
        P("section", None, None, None),
    )
    return jax.shard_map(
        on_device,
        mesh=mesh,
        in_specs=placed,
        out_specs=(P("section", None, None, None), P("section", None, None, None)),
        check_vma=False,
    )
```

```python
import functools

import jax
import jax.numpy as jnp
from jax import lax
from jax.experimental import pallas as pl
from jax.experimental.pallas import tpu as pltpu
from jax.sharding import PartitionSpec as P

EPS = 1e-05
BF = jnp.bfloat16
F32 = jnp.float32
ROWS = 16
LANES = 128
MIB = 1024 * 1024
ANY = pl.BlockSpec(memory_space=pl.ANY)
HBM = pl.BlockSpec(memory_space=pltpu.HBM)
VMEM = pl.BlockSpec(memory_space=pltpu.VMEM)
SMEM = pl.BlockSpec(memory_space=pltpu.SMEM)


def dot_nn(a, b):
    return lax.dot_general(a, b, (((1,), (0,)), ((), ())), preferred_element_type=F32)


def dot_nt(a, b):
    return lax.dot_general(a, b, (((1,), (1,)), ((), ())), preferred_element_type=F32)


def dot_tn(a, b):
    return lax.dot_general(a, b, (((0,), (0,)), ((), ())), preferred_element_type=F32)


class Place:
    def __init__(self, ids):
        rep = lax.axis_index("rep")
        self.ids = ids
        self.at = {0: lax.axis_index("section"), 3: rep // 8, 4: rep // 4 % 2, 5: rep % 4}

    def __getitem__(self, k):
        return self.ids[k - 1, 0] if k in (1, 2) else self.at[k]


def placed(body, ids, *refs):
    body(Place(ids), *refs)


def call(body, outs, scratch, ins, flops=10**8, nbytes=4 * 10**6, vmem=12, aliases=None):
    return pl.pallas_call(
        functools.partial(placed, body) if ins[0][1] is SMEM else body,
        out_shape=[jax.ShapeDtypeStruct(s, d) for s, d, _ in outs],
        in_specs=[spec for _, spec in ins],
        out_specs=[spec for _, _, spec in outs],
        scratch_shapes=scratch,
        input_output_aliases=aliases or {},
        compiler_params=pltpu.CompilerParams(vmem_limit_bytes=vmem * MIB),
        cost_estimate=pl.CostEstimate(flops=flops, bytes_accessed=nbytes, transcendentals=0),
    )(*[pltpu.with_memory_space_constraint(a, pltpu.HBM) if spec is HBM else a for a, spec in ins])


def lane_iota(rows):
    return lax.broadcasted_iota(jnp.int32, (rows, LANES), 1)


def row_iota(rows):
    return lax.broadcasted_iota(jnp.int32, (rows, LANES), 0)


def three(x):
    hi = x.astype(BF).astype(F32)
    rest = x - hi
    mid = rest.astype(BF).astype(F32)
    return hi, mid, (rest - mid).astype(BF).astype(F32)


def pack_rows(first_half, second_half, extra):
    at = row_iota(16)
    out = jnp.zeros((16, LANES), F32)
    for base, (a, b) in ((0, first_half), (8, second_half)):
        for j, row in enumerate(three(a) + three(b)):
            out = jnp.where(at == base + j, row, out)
    if extra is not None:
        hi, mid, _ = three(extra)
        out = jnp.where(at == 6, hi, out)
        out = jnp.where(at == 7, mid, out)
    return out.astype(BF)


def unpack_rows(block):
    block = block.astype(F32)

    def joined(base):
        return block[base : base + 1] + block[base + 1 : base + 2] + block[base + 2 : base + 3]

    return (joined(0), joined(8)), (joined(3), joined(11)), block[6:7] + block[7:8]


def columns(rows):
    at = row_iota(LANES)
    out = jnp.zeros((LANES, LANES), F32)
    for j, row in enumerate(rows):
        out = jnp.where(at == j, row, out)
    return out.T


def join_latent(msgs, tokens, width):
    parsed = [unpack_rows(m[tokens : tokens + 16]) for m in msgs]
    total = msgs[0][:tokens].astype(F32)
    for m in msgs[1:]:
        total = total + m[:tokens].astype(F32)
    halves = []
    for half in range(2):
        means = [p[0][half] for p in parsed]
        mean = (means[0] + means[1] + means[2] + means[3]) * 0.25
        offs = [m - mean for m in means]
        var = (parsed[0][1][half] + parsed[1][1][half] + parsed[2][1][half] + parsed[3][1][half]) * 0.25
        var = var + (offs[0] * offs[0] + offs[1] * offs[1] + offs[2] * offs[2] + offs[3] * offs[3]) * 0.25
        halves.append(columns([mean, lax.rsqrt(var + EPS)] + offs))
    cols = jnp.concatenate(halves, axis=0)
    colsum = parsed[0][2]
    for d in range(4):
        total = total + cols[:, 2 + d : 3 + d] * parsed[d][2]
        if d:
            colsum = colsum + parsed[d][2]
    return total * cols[:, 1:2], cols[:, 0:1], cols[:, 1:2], colsum


def start_first(pairs, sem):
    for cond, src, dst in pairs:
        @pl.when(cond)
        def _(src=src, dst=dst):
            pltpu.make_async_copy(src, dst, sem).start()


def start_weight(section, sc, own, near, same, cross, inner, dst, sem):
    q, x, y = sc[0], sc[3], sc[5]
    zh, c = q // 2, q % 2
    here = zh == section // 2
    mine = c == section % 2
    piece = 384

    def start(src, to):
        pltpu.make_async_copy(src, to, sem).start()

    @pl.when(here & mine)
    def _():
        start(own, dst)

    @pl.when(here & jnp.logical_not(mine))
    def _():
        start(near, dst)

    def pieces(refs, first):
        for j in range(2):
            for i in range(2):
                px, py = (i, j) if first == 0 else (j, i)
                at = piece_of(x ^ px, y ^ py) * piece
                base = i * 2 * piece
                if inner:
                    start(refs[j].at[pl.ds(base, piece)], dst.at[pl.ds(pl.multiple_of(at, piece), piece)])
                else:
                    for t in range(piece // LANES):
                        cols = pl.ds(pl.multiple_of(at + t * LANES, LANES), LANES)
                        start(refs[j].at[pl.ds(base + piece + t * LANES, LANES)], dst.at[:, cols])

    @pl.when(jnp.logical_not(here) & mine)
    def _():
        pieces(same, 0)

    @pl.when(jnp.logical_not(here) & jnp.logical_not(mine))
    def _():
        pieces(cross, 1)


def piece_of(x, y):
    return (x & 1) * 2 + (y & 1)


def factors(exps, q, out):
    every = exps.shape[0] // 2
    blocks = every // 4
    for k in range(4):
        @pl.when(q == k)
        def _(k=k):
            for m in range(2):
                e = exps[m * every + k * blocks : m * every + (k + 1) * blocks, :]
                f = lax.shift_left(jnp.ones(e.shape, jnp.int32), e + 14).astype(F32) * (2.0**-14)
                full = jnp.concatenate([f, jnp.zeros((LANES - blocks, LANES), F32)], axis=0)
                out[m * LANES : (m + 1) * LANES, :] = full.T


def wait_for(dst, sem):
    pltpu.make_async_copy(dst, dst, sem).wait()


def send_body(sc, stash, w_in, w_out, far, mid, sib_in, sib_out, over, sems):
    q, x, y = sc[0], sc[3], sc[5]
    c = q % 2
    tok, quarter = far.shape[0] // 2, far.shape[1]
    piece = quarter // 4
    mid_slot = jnp.where(q == 1, 1, 0)
    copies = []

    def go(src, dst):
        copy = pltpu.make_async_copy(src, dst, sems.at[len(copies)])
        copy.start()
        copies.append(copy)

    def cols(k):
        return pl.ds(pl.multiple_of((q ^ k) * quarter, quarter), quarter)

    for k in (2, 3):
        base = (q ^ k) * quarter + piece_of(x, y) * piece
        first = (k - 2) * 2 * piece
        go(w_in.at[0, 0, pl.ds(pl.multiple_of(base, piece), piece), :], over.at[pl.ds(first, piece)])
        for t in range(piece // LANES):
            from_cols = pl.ds(pl.multiple_of(base + t * LANES, LANES), LANES)
            go(w_out.at[0, 0, :, from_cols], over.at[pl.ds(first + piece + t * LANES, LANES)])
    for m in range(2):
        go(stash.at[0, 1 - c, sc[1 + m], :, cols(2)], far.at[pl.ds(m * tok, tok)])
    go(w_out.at[0, 0, :, cols(1)], sib_out)
    go(w_in.at[0, 0, cols(1), :], sib_in)
    for m in range(2):
        go(stash.at[0, mid_slot, sc[1 + m], :, cols(1)], mid.at[pl.ds(m * tok, tok)])
    for copy in copies:
        copy.wait()


def sum_blocks(block, count):
    parts = []
    for b in range(count):
        v = block(b)
        if b < 4:
            parts.append(v)
        else:
            parts[b % 4] = parts[b % 4] + v
    return (parts[0] + parts[1]) + (parts[2] + parts[3])


def first_body(sc, micro, grads, w_in, w_out, msg, x_v, w_v, wo_v, n_v, st, sems):
    q = sc[0]
    tokens, width = x_v.shape
    tok = tokens // 2
    blocks = width // LANES

    def load(src, wsrc, wdst):
        copies = [pltpu.make_async_copy(src.at[m], x_v.at[pl.ds(m * tok, tok)], sems.at[m]) for m in range(2)]
        copies.append(pltpu.make_async_copy(wsrc.at[0, 0], wdst, sems.at[2]))
        for copy in copies:
            copy.start()
        return copies

    @pl.when(q == 0)
    def _():
        load(micro, w_in, w_v)

    @pl.when(q == 3)
    def _():
        load(grads, w_out, wo_v)

    @pl.when((q == 1) | (q == 2))
    def _():
        msg[...] = jnp.zeros(msg.shape, BF)

    @pl.when(q == 0)
    def _():
        for m in range(2):
            wait_for(x_v.at[pl.ds(m * tok, tok)], sems.at[m])

            @pl.loop(m * (tok // ROWS), (m + 1) * (tok // ROWS), unroll=2)
            def _(i):
                rows = pl.ds(pl.multiple_of(i * ROWS, ROWS), ROWS)

                def block(b):
                    return x_v[rows, b * LANES : (b + 1) * LANES].astype(F32)

                def square(b):
                    d = block(b) - mean
                    return d * d

                mean = jnp.sum(sum_blocks(block, blocks), axis=1, keepdims=True) * (1.0 / width)
                mean = jnp.broadcast_to(mean, (ROWS, LANES))
                inv = lax.rsqrt(jnp.sum(sum_blocks(square, blocks), axis=1, keepdims=True) * (1.0 / width) + EPS)
                inv = jnp.broadcast_to(inv, (ROWS, LANES))
                for b in range(blocks):
                    n_v[rows, b * LANES : (b + 1) * LANES] = ((block(b) - mean) * inv).astype(BF)
                st[rows, :] = jnp.where(lane_iota(ROWS) == 0, mean, inv)

        wait_for(w_v, sems.at[2])
        latent = dot_nn(n_v[...], w_v[...])
        msg[:tokens] = latent.astype(BF)
        t0, t1 = st[:LANES].T, st[LANES:].T
        msg[tokens:] = pack_rows((t0[0:1], t0[1:2]), (t1[0:1], t1[1:2]), None)

    @pl.when(q == 3)
    def _():
        for m in range(2):
            wait_for(x_v.at[pl.ds(m * tok, tok)], sems.at[m])
        wait_for(wo_v, sems.at[2])
        msg[:tokens] = dot_nt(x_v[...], wo_v[...]).astype(BF)
        msg[tokens:] = jnp.zeros((msg.shape[0] - tokens, msg.shape[1]), BF)


def forward_body(section, sc, *refs):
    first = section == 1
    refs = list(refs)
    take = refs.pop
    msgs = [take(0) for _ in range(4)]
    h_in = take(0)
    exps = take(0)
    stash, held = take(0), take(0)
    wi_own, wo_own, wi_near, wo_near = [take(0) for _ in range(4)]
    same, cross = [take(0) for _ in range(2)], [take(0) for _ in range(2)]
    h_out, normed, msg, latf, invb, colsum_out, wo_v, wi_v = [take(0) for _ in range(8)]
    x_v, pick, up, cen, st, mc = [take(0) for _ in range(6)]
    lat_v, e_v, factor, sems = [take(0) for _ in range(4)]
    q = sc[0]
    c = q % 2
    tokens, quarter = pick.shape
    tok = tokens // 2
    cols = pl.ds(pl.multiple_of(q * quarter, quarter), quarter)
    start_weight(section - 1, sc, wo_own.at[0, 0, :, cols], wo_near, same, cross, False, wo_v, sems.at[0])
    for m in range(2):
        pltpu.make_async_copy(exps.at[section - 1, m], e_v.at[pl.ds(m * exps.shape[2], exps.shape[2])], sems.at[4]).start()
    if first:
        for m in range(2):
            pltpu.make_async_copy(h_in.at[m, :, cols], x_v.at[pl.ds(m * tok, tok)], sems.at[2]).start()
    if section == 2:
        local, slot = (q == 1) | (q == 2), jnp.where(q == 1, 1, 0)
    else:
        local, slot = (q // 2 == 0) if section == 1 else (q // 2 == 1), 1 - c
    for m in range(2):
        rows = pl.ds(m * tok, tok)
        start_first(
            [
                (local, stash.at[0, slot, sc[1 + m], :, cols], pick.at[rows]),
                (jnp.logical_not(local), held.at[rows], pick.at[rows]),
            ],
            sems.at[3],
        )
    start_weight(section, sc, wi_own.at[0, 0, cols, :], wi_near, same, cross, True, wi_v, sems.at[1])

    if first:
        for k in range(4):
            @pl.when(q == k)
            def _(k=k):
                lat_v[...] = msgs[k][...]

        (m0, m1), (v0, v1), _ = unpack_rows(lat_v[tokens:])
        both = jnp.concatenate([columns([m0, v0]), columns([m1, v1])], axis=0)
        latent = lat_v[:tokens].astype(F32)
        mean, inv = both[:, 0:1], both[:, 1:2]
        colsum_out[...] = jnp.zeros(colsum_out.shape, F32)
    else:
        latent, mean, inv, colsum = join_latent([m[...] for m in msgs], tokens, quarter)
        colsum_out[...] = jnp.broadcast_to(colsum, colsum_out.shape)
    latf[...] = latent
    invb[...] = jnp.broadcast_to(inv, invb.shape)
    mc[...] = jnp.broadcast_to(mean, mc.shape)
    wait_for(wo_v, sems.at[0])
    up[...] = dot_nn(latent.astype(BF), wo_v[...])
    wait_for(e_v, sems.at[4])
    factors(e_v, q, factor)
    if first:
        wait_for(x_v, sems.at[2])
        src = x_v
    else:
        src = h_in
    wait_for(pick, sems.at[3])

    @pl.loop(0, tokens // ROWS, unroll=4)
    def _(i):
        rows = pl.ds(pl.multiple_of(i * ROWS, ROWS), ROWS)
        mean_t, inv_t = mc[rows, :], invb[rows, :]
        fac = factor[rows, :]
        kept = []
        for b in range(quarter // LANES):
            lanes = slice(b * LANES, (b + 1) * LANES)
            h = src[rows, lanes].astype(F32)
            normed[rows, lanes] = ((h - mean_t) * inv_t).astype(BF)
            stored = pick[rows, lanes].astype(F32)
            f = fac[:, b : b + 1]
            d = jnp.clip(h + up[rows, lanes] - stored, f * -8.0, f * 7.0).astype(BF)
            h = stored + d.astype(F32)
            h_out[rows, lanes] = h
            kept.append(h)
        st[rows, :] = sum_blocks(lambda b: kept[b], quarter // LANES)

    mean_d = jnp.sum(st[...], axis=1, keepdims=True) * (1.0 / quarter)
    mc[...] = jnp.broadcast_to(mean_d, mc.shape)

    @pl.loop(0, tokens // ROWS, unroll=4)
    def _(i):
        rows = pl.ds(pl.multiple_of(i * ROWS, ROWS), ROWS)
        mean_t = mc[rows, :]
        kept = [h_out[rows, b * LANES : (b + 1) * LANES] - mean_t for b in range(quarter // LANES)]
        for b in range(quarter // LANES):
            cen[rows, b * LANES : (b + 1) * LANES] = kept[b].astype(BF)
        st[rows, :] = sum_blocks(lambda b: kept[b] * kept[b], quarter // LANES)

    var_d = jnp.sum(st[...], axis=1, keepdims=True) * (1.0 / quarter)
    st[...] = jnp.where(lane_iota(tokens) == 0, mc[...], var_d)

    wait_for(wi_v, sems.at[1])
    w = wi_v[...]
    msg[:tokens] = dot_nn(cen[...], w).astype(BF)
    colsum = dot_nn(jnp.ones((16, quarter), BF), w)[0:1]
    t0, t1 = st[:LANES].T, st[LANES:].T
    msg[tokens:] = pack_rows((t0[0:1], t0[1:2]), (t1[0:1], t1[1:2]), colsum)


def backward_body(section, sc, *refs):
    top = section == 3
    refs = list(refs)
    take = refs.pop
    msgs = [take(0) for _ in range(4)]
    if top:
        lat_msgs = [take(0) for _ in range(4)]
        h_in = take(0)
    else:
        normed_in, latf, invb, colsum_in = [take(0) for _ in range(4)]
    g_in = take(0)
    exps, wo_v, wi_v = [take(0) for _ in range(3)]
    g_out, msg, glat_out = [take(0) for _ in range(3)]
    if top:
        normed, latf, g_v = [take(0) for _ in range(3)]
    gn, mc, inv_v, a_v, b_v, e_v, factor, sems = [take(0) for _ in range(8)]
    q = sc[0]
    tokens, quarter = gn.shape
    tok = tokens // 2
    width = 4 * quarter
    cols = pl.ds(pl.multiple_of(q * quarter, quarter), quarter)
    for m in range(2):
        pltpu.make_async_copy(exps.at[section, m], e_v.at[pl.ds(m * exps.shape[2], exps.shape[2])], sems.at[1]).start()
    if top:
        for m in range(2):
            pltpu.make_async_copy(g_in.at[m, :, cols], g_v.at[pl.ds(m * tok, tok)], sems.at[0]).start()
        latent, mean, inv, colsum = join_latent([m[...] for m in lat_msgs], tokens, quarter)
        latf[...] = latent
        mc[...] = jnp.broadcast_to(mean, mc.shape)
        inv_v[...] = jnp.broadcast_to(inv, inv_v.shape)
        for k in range(4):
            @pl.when(q ^ 3 == k)
            def _(k=k):
                glat_out[...] = msgs[k][:tokens]

        glat = glat_out[...]
        src, norm, inv_ref = g_v, normed, inv_v
    else:
        latent, colsum = latf[...], colsum_in[0:1]
        glat = msgs[0][:tokens].astype(F32)
        for m in msgs[1:]:
            glat = glat + m[:tokens].astype(F32)
        glat = glat.astype(BF)
        glat_out[...] = glat
        src, norm, inv_ref = g_in, normed_in, invb
    wide = glat.astype(F32)
    a_v[...] = jnp.broadcast_to(jnp.sum(wide * colsum, axis=1, keepdims=True) * (1.0 / width), a_v.shape)
    b_v[...] = jnp.broadcast_to(jnp.sum(wide * latent, axis=1, keepdims=True) * (1.0 / width), b_v.shape)
    gn[...] = dot_nt(glat, wi_v[...])
    wait_for(e_v, sems.at[1])
    factors(e_v, q, factor)
    if top:
        wait_for(g_v, sems.at[0])

    @pl.loop(0, tokens // ROWS, unroll=4)
    def _(i):
        rows = pl.ds(pl.multiple_of(i * ROWS, ROWS), ROWS)
        fac = factor[rows, :]
        inv_t, a_t, b_t = inv_ref[rows, :], a_v[rows, :], b_v[rows, :]
        for b in range(quarter // LANES):
            lanes = slice(b * LANES, (b + 1) * LANES)
            if top:
                n = (h_in[rows, lanes] - mc[rows, :]) * inv_t
                normed[rows, lanes] = n.astype(BF)
            else:
                n = norm[rows, lanes].astype(F32)
            f = fac[:, b : b + 1]
            g = src[rows, lanes].astype(F32) + inv_t * (gn[rows, lanes] - a_t - n * b_t)
            g_out[rows, lanes] = jnp.clip(g, f * -128.0, f * 127.0).astype(BF)

    msg[...] = dot_nt(g_out[...], wo_v[...]).astype(BF)


def grads_body(normed, latf, g_ref, glat, gin, gout):
    gin[...] = dot_tn(normed[...], glat[...]).astype(BF)
    gout[...] = dot_tn(latf[...].astype(BF), g_ref[...]).astype(BF)


def grads_top_body(sc, normed, latf, g_ref, glat, gin, gout, g_v, sems):
    quarter = g_v.shape[1]
    tok = g_v.shape[0] // 2
    cols = pl.ds(pl.multiple_of(sc[0] * quarter, quarter), quarter)
    for m in range(2):
        pltpu.make_async_copy(g_ref.at[m, :, cols], g_v.at[pl.ds(m * tok, tok)], sems.at[0]).start()
    gin[...] = dot_tn(normed[...], glat[...]).astype(BF)
    wait_for(g_v, sems.at[0])
    gout[...] = dot_tn(latf[...].astype(BF), g_v[...]).astype(BF)


def grads_first_body(sc, *refs):
    refs = list(refs)
    take = refs.pop
    msgs = [take(0) for _ in range(4)]
    normed, latf, g_ref = [take(0) for _ in range(3)]
    gins = [None] + [take(0) for _ in range(3)]
    gouts = [None] + [take(0) for _ in range(3)]
    a, b = [take(0) for _ in range(5)], [take(0) for _ in range(5)]
    gin0, gout0 = take(0), take(0)
    gins[0], gouts[0] = gin0, gout0
    x, y = sc[3], sc[5]
    glat = msgs[0][...].astype(F32)
    for m in msgs[1:]:
        glat = glat + m[...].astype(F32)
    gin0[...] = dot_tn(normed[...], glat.astype(BF)).astype(BF)
    gout0[...] = dot_tn(latf[...].astype(BF), g_ref[...]).astype(BF)
    rows, low = a[0].shape[1], b[0].shape[1]
    for k in range(4):
        at = pl.ds(pl.multiple_of(((x + k) % 4) * rows, rows), rows)
        to = pl.ds(pl.multiple_of(((y + k) % 4) * low, low), low)
        for s in range(4):
            d, i = (2 + s // 2, s % 2) if k == 2 else ((0, 1, 2, 4)[k], s)
            a[d][i] = gins[s][at, :]
            b[d][i] = gouts[s][to, :]


def relay_body(a1, a3, a_lo, a_hi, a1_out, a3_out):
    for src, extra, at, dst in (
        (a1, a_lo, 0, a1_out),
        (a3, a_hi, 2, a3_out),
    ):
        for s in range(4):
            if at <= s < at + 2:
                dst[s] = total_of([src[s], extra[s - at]])
            else:
                dst[s] = src[s]


def total_of(parts):
    total = parts[0].astype(F32)
    for part in parts[1:]:
        total = total + part.astype(F32)
    return total.astype(BF)


def second_in_body(sc, a0, a1, a2, c0, c1, c2, c3, a_v):
    for s in range(4):
        a_v[s] = total_of([r[s] for r in (a0, a1, a2)])
    rows = c0.shape[1]
    for k, c in enumerate((c0, c1, c2, c3)):
        at = pl.ds(pl.multiple_of(((sc[5] + k) % 4) * rows, rows), rows)
        for s in range(4):
            c[s] = a_v[s, at, :]


def second_out_body(sc, b0, b1, b2, d0, d1, d2, d3, b_v):
    for s in range(4):
        b_v[s] = total_of([r[s] for r in (b0, b1, b2)])
    cols = d0.shape[2]
    for k, d in enumerate((d0, d1, d2, d3)):
        to = pl.ds(pl.multiple_of(((sc[3] + k) % 4) * cols, cols), cols)
        for s in range(4):
            d[s] = b_v[s, :, to]


def third_body(a0, a1, a2, a3, b0, b1, b2, b3, out):
    rows, low = a0.shape[1], b0.shape[1]
    for s in range(4):
        out[s, :rows] = total_of([r[s] for r in (a0, a1, a2, a3)])
        total = total_of([r[s] for r in (b0, b1, b2, b3)])
        for t in range(total.shape[1] // LANES):
            out[s, rows + t * low : rows + (t + 1) * low] = total[:, t * LANES : (t + 1) * LANES]


def rep_of(x, z, y):
    return x * 8 + z * 4 + y


EVERY = [(x, z, y) for x in range(4) for z in range(2) for y in range(4)]


def along_x(value, k):
    return lax.ppermute(value, "rep", [(rep_of(x, z, y), rep_of((x + k) % 4, z, y)) for x, z, y in EVERY])


def along_y(value, k):
    return lax.ppermute(value, "rep", [(rep_of(x, z, y), rep_of(x, z, (y + k) % 4)) for x, z, y in EVERY])


def along_z(value, k):
    return lax.ppermute(value, "rep", [(rep_of(x, z, y), rep_of(x, (z + k) % 2, y)) for x, z, y in EVERY])


def gather(value, count, move):
    return [value] + [move(value, k) for k in range(1, count)]


def gather_relayed(value, move):
    before, after = move(value, 1), move(value, 3)
    half = value.shape[0] // 2
    return [value, before, move(before[:half], 1), move(after[half:], 3), after]


def place_pieces(sc, parts, gin, gout, gin_v, gout_v, sem):
    q, x, y = sc[0], sc[3], sc[5]
    quarter = gin.shape[2] // 4
    rows, low = quarter // 16, gout.shape[2] // 4
    copies = []
    for back, first, a_ref, b_ref in parts:
        for i in range(a_ref.shape[0]):
            j = first + i
            for d in range(4):
                base = (q ^ d) * quarter
                row = base + ((x - back + 4) % 4) * (quarter // 4) + ((y - j + 4) % 4) * rows
                gin_v[pl.ds(pl.multiple_of(row, rows), rows), :] = a_ref[i, d]
                at = pl.ds(pl.multiple_of(((y - back + 4) % 4) * low, low), low)
                for t in range(quarter // 4 // LANES):
                    col = base + ((x - j + 4) % 4) * (quarter // 4) + t * LANES
                    gout_v[at, pl.ds(pl.multiple_of(col, LANES), LANES)] = b_ref[i, d, t * low : (t + 1) * low, :]
        if first + a_ref.shape[0] == 4:
            for d in range(4):
                row = d * quarter + ((x - back + 4) % 4) * (quarter // 4)
                whole = pl.ds(pl.multiple_of(row, quarter // 4), quarter // 4)
                copies.append(pltpu.make_async_copy(gin_v.at[whole], gin.at[0, 0, whole], sem.at[len(copies)]))
                copies[-1].start()
            whole = pl.ds(pl.multiple_of(((y - back + 4) % 4) * low, low), low)
            copies.append(pltpu.make_async_copy(gout_v.at[whole], gout.at[0, 0, whole], sem.at[len(copies)]))
            copies[-1].start()
    for copy in copies:
        copy.wait()


def place_body(sc, a0, a1, a4, b0, b1, b4, gin, gout, gin_v, gout_v, sem):
    place_pieces(sc, ((0, 0, a0, b0), (1, 0, a1, b1), (3, 0, a4, b4)), gin, gout, gin_v, gout_v, sem)


def place_last_body(sc, a2, a3, b2, b3, gin_in, gout_in, gin, gout, gin_v, gout_v, sem):
    place_pieces(sc, ((2, 0, a2, b2), (2, 2, a3, b3)), gin, gout, gin_v, gout_v, sem)


def on_device(micro, grads, stash, sample_ids, fwd_exps, bwd_exps, w_in, w_out):
    q = lax.axis_index("section")
    tok, width = micro.shape[1], micro.shape[2]
    tokens, quarter, rank = 2 * tok, width // 4, w_in.shape[3]
    fwd_exps, bwd_exps = jnp.swapaxes(fwd_exps, 2, 3), jnp.swapaxes(bwd_exps, 2, 3)
    sc = sample_ids

    def swap(value, k, sources=range(4)):
        return lax.ppermute(value, "section", [(s, s ^ k) for s in sources])

    def exchange(value):
        return [value] + [swap(value, k) for k in (1, 2, 3)]

    def beside(value):
        pairs = [(s * 32 + rep_of(xx, zz, yy), (s ^ 2) * 32 + rep_of(xx, 1 - zz, yy)) for s in range(4) for xx, zz, yy in EVERY]
        return lax.ppermute(value, ("section", "rep"), pairs)

    def beside_along(value, dx, dy, core):
        pairs = [(s * 32 + rep_of(xx, zz, yy), (s ^ core) * 32 + rep_of(xx ^ dx, zz, yy ^ dy)) for s in range(4) for xx, zz, yy in EVERY]
        return lax.ppermute(value, ("section", "rep"), pairs)

    dma = pltpu.SemaphoreType.DMA
    big = (tokens, quarter)
    qi, qo = (quarter, rank), (rank, quarter)
    far, mid, sib_in, sib_out, over = call(
        send_body,
        [(big, BF, VMEM)] * 2 + [(qi, BF, VMEM), (qo, BF, VMEM), (qi, BF, VMEM)],
        [dma((14,))],
        [(sc, SMEM), (stash, HBM), (w_in, HBM), (w_out, HBM)],
    )
    over = beside(over)
    (msg0,) = call(
        first_body,
        [((tokens + 16, rank), BF, VMEM)],
        [
            pltpu.VMEM((tokens, width), BF),
            pltpu.VMEM((width, rank), BF),
            pltpu.VMEM((rank, width), BF),
            pltpu.VMEM((tokens, width), BF),
            pltpu.VMEM((tokens, LANES), F32),
            dma((3,)),
        ],
        [(sc, SMEM), (micro, HBM), (grads, HBM), (w_in, HBM), (w_out, HBM)],
        vmem=16,
        nbytes=3 * 10**7,
    )
    msg0, far = lax.optimization_barrier((msg0, far))
    far = swap(far, 2)
    near_msg = swap(msg0, 1, (0, 3))
    over, msg0, sib_in, sib_out = lax.optimization_barrier((over, msg0, sib_in, sib_out))
    half = quarter // 2
    same, cross = over[:half], over[half:]
    same = jnp.concatenate([same, beside_along(same, 1, 0, 0)], 0)
    cross = jnp.concatenate([swap(cross, 1), beside_along(cross, 0, 1, 1)], 0)
    same, cross, sib_in, sib_out = lax.optimization_barrier((same, cross, sib_in, sib_out))
    pieces = [same, beside_along(same, 0, 1, 0), cross, beside_along(cross, 1, 0, 0)]
    near = [swap(sib_in, 1), swap(sib_out, 1)]
    near, msg0 = lax.optimization_barrier((near, msg0))
    msgs0 = [near_msg] + [swap(msg0, k, (0, 3)) for k in (2, 3)]
    pieces, far, near, msgs0 = lax.optimization_barrier((pieces, far, near, msgs0))
    msgs0 = [msg0] + msgs0
    weights = [w_in, w_out] + near + pieces
    weights = list(zip(weights, [HBM, HBM] + [ANY] * 6))

    msgs = msgs0
    h = micro
    kept = []
    held = {}
    for section in (1, 2, 3):
        h, normed, msg, latf, invb, colsum, low_out, high_in = call(
            functools.partial(forward_body, section),
            [
                (big, F32, VMEM),
                (big, BF, VMEM),
                ((tokens + 16, rank), BF, VMEM),
                ((tokens, rank), F32, VMEM),
                ((tokens, LANES), F32, VMEM),
                ((8, LANES), F32, VMEM),
                (qo, BF, VMEM),
                (qi, BF, VMEM),
            ],
            [
                pltpu.VMEM(big, BF),
                pltpu.VMEM(big, BF),
                pltpu.VMEM(big, F32),
                pltpu.VMEM(big, BF),
                pltpu.VMEM((tokens, LANES), F32),
                pltpu.VMEM((tokens, LANES), F32),
                pltpu.VMEM((tokens + 16, rank), BF),
                pltpu.VMEM((2 * fwd_exps.shape[2], tok), jnp.int32),
                pltpu.VMEM((tokens, LANES), F32),
                dma((5,)),
            ],
            [(sc, SMEM)]
            + [(m, VMEM) for m in msgs]
            + [(h, HBM if section == 1 else VMEM), (fwd_exps, HBM), (stash, HBM)]
            + [(mid if section == 2 else far, ANY)]
            + weights,
        )
        kept.append((normed, latf, invb, colsum))
        held[section] = [low_out, high_in]
        if section == 1:
            msg, mid = lax.optimization_barrier((msg, mid))
            mid = swap(mid, 1, (1, 2))
        msgs = exchange(msg)

    gins, gouts = {}, {}
    g = grads
    for section in (3, 2, 1):
        top = section == 3
        outs = [(big, BF, VMEM), ((tokens, rank), BF, VMEM), ((tokens, rank), BF, VMEM)]
        scratch = [
            pltpu.VMEM(big, F32),
            pltpu.VMEM((tokens, LANES), F32),
            pltpu.VMEM((tokens, LANES), F32),
            pltpu.VMEM((tokens, LANES), F32),
            pltpu.VMEM((tokens, LANES), F32),
            pltpu.VMEM((2 * bwd_exps.shape[2], tok), jnp.int32),
            pltpu.VMEM((tokens, LANES), F32),
            dma((2,)),
        ]
        if top:
            outs += [(big, BF, VMEM), ((tokens, rank), F32, VMEM)]
            scratch = [pltpu.VMEM(big, BF)] + scratch
            ins = [(m, VMEM) for m in msgs0] + [(m, VMEM) for m in msgs] + [(h, VMEM), (g, HBM)]
        else:
            ins = [(m, VMEM) for m in msgs] + [(v, VMEM) for v in kept[section]] + [(g, VMEM)]
        result = call(
            functools.partial(backward_body, section),
            outs,
            scratch,
            [(sc, SMEM)] + ins + [(bwd_exps, HBM)] + [(w, VMEM) for w in held[section]],
        )
        next_g, msg, glat = result[:3]
        if top:
            normed, latf = result[3:]
            gin, gout = call(
                grads_top_body,
                [(qi, BF, VMEM), (qo, BF, VMEM)],
                [pltpu.VMEM(big, BF), dma((1,))],
                [(sc, SMEM), (normed, VMEM), (latf, VMEM), (g, HBM), (glat, VMEM)],
            )
        else:
            normed, latf = kept[section][:2]
            gin, gout = call(
                grads_body,
                [(qi, BF, VMEM), (qo, BF, VMEM)],
                [],
                [(normed, VMEM), (latf, VMEM), (g, VMEM), (glat, VMEM)],
            )
        msgs = exchange(msg)
        gins[section], gouts[section] = gin, gout
        if section == 2:
            msgs, gins, gouts = lax.optimization_barrier((msgs, gins, gouts))
        g = next_g
    rows, low = quarter // 4, rank // 4
    cut = call(
        grads_first_body,
        [((n, rows, rank), BF, VMEM) for n in (4, 4, 2, 2, 4)] + [((n, low, quarter), BF, VMEM) for n in (4, 4, 2, 2, 4)],
        [pltpu.VMEM(qi, BF), pltpu.VMEM(qo, BF)],
        [(sc, SMEM)]
        + [(m, VMEM) for m in msgs]
        + [(kept[0][0], VMEM), (kept[0][1], VMEM), (g, VMEM)]
        + [(terms[s], VMEM) for terms in (gins, gouts) for s in (1, 2, 3)],
    )
    a, b = cut[:5], cut[5:]
    far_a, far_b = (along_x(a[2], 1), along_x(a[3], 3)), (along_y(b[2], 1), along_y(b[3], 3))
    whole_a, whole_b = (4, rows, rank), (4, low, quarter)
    to_a, back_a = call(relay_body, [(whole_a, BF, VMEM)] * 2, [], [(v, VMEM) for v in (a[1], a[4], *far_a)])
    to_b, back_b = call(relay_body, [(whole_b, BF, VMEM)] * 2, [], [(v, VMEM) for v in (b[1], b[4], *far_b)])
    a = [a[0], along_x(to_a, 1), along_x(back_a, 3)]
    b = [b[0], along_y(to_b, 1), along_y(back_b, 3)]
    cut_a = call(
        second_in_body,
        [((4, rows // 4, rank), BF, VMEM)] * 4,
        [pltpu.VMEM(whole_a, BF)],
        [(sc, SMEM)] + [(v, VMEM) for v in a],
    )
    cut_b = call(
        second_out_body,
        [((4, low, rows), BF, VMEM)] * 4,
        [pltpu.VMEM(whole_b, BF)],
        [(sc, SMEM)] + [(v, VMEM) for v in b],
    )
    a = [cut_a[0]] + [along_y(cut_a[k], k) for k in (1, 2, 3)]
    b = [cut_b[0]] + [along_x(cut_b[k], k) for k in (1, 2, 3)]
    (both,) = call(
        third_body,
        [((4, rows // 2, rank), BF, VMEM)],
        [],
        [(v, VMEM) for v in a + b],
    )
    shares = (both.astype(F32) + along_z(both, 1).astype(F32)).astype(BF)
    own = [lax.dynamic_index_in_dim(shares, q ^ k, 0, keepdims=False) for k in range(4)]
    mine = jnp.stack([own[0]] + [swap(own[k], k) for k in (1, 2, 3)])
    a, b = mine[:, : rows // 4], mine[:, rows // 4 :]
    a, b = gather(a, 4, along_y), gather(b, 4, along_x)
    a, b = jnp.stack(a), jnp.stack(b)
    a, b = gather_relayed(a, along_x), gather_relayed(b, along_y)
    totals = [((1, 1, width, rank), BF, HBM), ((1, 1, rank, width), BF, HBM)]
    whole = [pltpu.VMEM((width, rank), BF), pltpu.VMEM((rank, width), BF)]
    total_in, total_out = call(
        place_body,
        totals,
        whole + [dma((15,))],
        [(sc, SMEM)] + [(v, VMEM) for v in (a[0], a[1], a[4], b[0], b[1], b[4])],
    )
    total_in, total_out = call(
        place_last_body,
        totals,
        whole + [dma((5,))],
        [(sc, SMEM)] + [(v, VMEM) for v in (a[2], a[3], b[2], b[3])] + [(total_in, HBM), (total_out, HBM)],
        aliases={5: 0, 6: 1},
    )
    return total_in, total_out


def solution(mesh):
    placed = (
        P(None, "rep", None),
        P(None, "rep", None),
        P("section", None, None, "rep", None),
        P(None, "rep"),
        P(None, None, "rep", None),
        P(None, None, "rep", None),
        P("section", None, None, None),
        P("section", None, None, None),
    )
    return jax.shard_map(
        on_device,
        mesh=mesh,
        in_specs=placed,
        out_specs=(P("section", None, None, None), P("section", None, None, None)),
        check_vma=False,
    )
```
